32 devices in a mesh: row: 8 (over z, y), col: 4 (over x, core).
Axes of the slice: x: 2, y: 2, z: 4, core: 2. Of those that a mesh axis runs over, the one named last changes fastest.
Arguments:
- volume: bfloat16 [48, 32, 128, 32], P(None, ('row', 'col')), may hold values from -6 to 6
- norm_gain: float32 [2, 48], replicated, may hold values from 0.1 to 1.9
- in_proj: bfloat16 [2, 320, 48], replicated, may hold values from -0.875 to 0.875
- dt_proj: bfloat16 [2, 3, 48], replicated, may hold values from -0.875 to 0.875
- dt_bias: float32 [2, 3], replicated, may hold values from -2 to 1
- decay_rate: float32 [2, 3], replicated, may hold values from 2e-07 to 0.05
- conv_weight: float32 [2, 224, 4], replicated, may hold values from -3 to 3
- conv_bias: float32 [2, 224], replicated, may hold values from -3 to 3
- skip_gain: float32 [2, 3], replicated, may hold values from 0.5 to 1.5
- out_gain: float32 [2, 96], replicated, may hold values from 0.1 to 1.9
- out_proj: bfloat16 [2, 48, 96], replicated, may hold values from -0.625 to 0.625
- head_weight: bfloat16 [14, 48], replicated, may hold values from -2.6875 to 2.6875
- head_bias: float32 [14], replicated, may hold values from -6 to 6
- labels: int32 [32, 32, 128], P(('row', 'col')), may hold values from 0 to 13
- distance: int32 [14, 32, 32, 128], P(None, ('row', 'col')), may hold values from -16384 to 16384
Outputs:
- features: bfloat16 [48, 32, 32, 128], P(None, ('row', 'col'))
- logit_grad: float32 [14, 32, 32, 128], P(None, ('row', 'col'))
- total_loss: float32 [], replicated
The draws below stay inside these ranges and needn't reach their ends.
All inputs are finite; a program needn't handle non-finite values.
Results may differ from the reference program's by a relative error of at most 0.006.
The reference program's roundings to bfloat16 on the way count: a program that leaves them out, or rounds other values in their place, can miss the bound.
Values may be sent and summed in bfloat16 or wider, within the bound.
No kernel may reach another device: no remote copies, remote signals or barrier semaphores. Data moves between devices by JAX's collectives and lax.ppermute only.
A program may use at most 192 MiB of HBM per device.

```python
import math
import jax
import jax.numpy as jnp
from jax import lax

D = 48
HEADS = 3
STATE = 64
CLASSES = 14
KERNEL = 4
SCAN_BLOCK = 128
BLOCKS = 2
YS = 128
INNER = 96
CONV_CH = 224
SIDE = 32
NTOT = 131072


def place_ends(drawn, key, low, high):
    longest = drawn.shape.index(max(drawn.shape))
    spots = []
    for shift in (0, 1):
        where = [jax.random.randint(jax.random.fold_in(key, axis), (), 0, length) for axis, length in enumerate(drawn.shape)]
        where[longest] = (where[longest] + shift) % drawn.shape[longest]
        spots.append(tuple(where))
    return drawn.at[spots[0]].set(low).at[spots[1]].set(high)


def steps_of(stream_key, shape, split, least, high):
    def one(axis_at, blocks):
        heights = jax.random.uniform(jax.random.fold_in(jax.random.fold_in(stream_key, 6), axis_at), (blocks,), jnp.float32, least / len(split), high / len(split))
        return jnp.repeat(jnp.exp(heights), shape[axis_at] // blocks).reshape((-1,) + (1,) * (len(shape) - axis_at - 1))

    level = one(*split[0])
    for cut in split[1:]:
        level = level * one(*cut)
    return level


def scatter_about(rng, extent, width, bound, cuts=(), kind=jnp.bfloat16):
    array = width * jax.random.normal(rng, extent, jnp.float32)
    if cuts:
        array = array * steps_of(rng, extent, cuts, -0.22, 0.18)
    return jnp.clip(array, -bound, bound).astype(kind)


def setup_inputs(seed: int = 0) -> dict:
    keys = jax.random.split(jax.random.key(seed), 16)
    volume = scatter_about(keys[0], (D, SIDE, YS, SIDE), 1.0, 6.0, ((1, 32),))
    norm_gain = jnp.clip(1.0 + 0.18 * jax.random.normal(keys[1], (BLOCKS, D), jnp.float32), 0.1, 1.9)
    in_proj = scatter_about(keys[2], (BLOCKS, 2 * INNER + 2 * STATE, D), D ** -0.5, 0.875)
    dt_proj = scatter_about(keys[3], (BLOCKS, HEADS, D), D ** -0.5, 0.875)
    dt_bias = jnp.clip(jax.random.uniform(keys[4], (BLOCKS, HEADS), jnp.float32, -2.0, 1.0), -2.0, 1.0)
    decay_rate = jnp.clip(jnp.exp(jax.random.uniform(keys[5], (BLOCKS, HEADS), jnp.float32, math.log(2.0000000233721948e-07), math.log(0.05))), 2.0000000233721948e-07, 0.05)
    conv_weight = scatter_about(keys[6], (BLOCKS, CONV_CH, KERNEL), 0.5, 3.0, (), jnp.float32)
    conv_bias = scatter_about(keys[7], (BLOCKS, CONV_CH), 0.5, 3.0, (), jnp.float32)
    skip_gain = jnp.clip(jax.random.uniform(keys[8], (BLOCKS, HEADS), jnp.float32, 0.5, 1.5), 0.5, 1.5)
    out_gain = jnp.clip(1.0 + 0.18 * jax.random.normal(keys[9], (BLOCKS, INNER), jnp.float32), 0.1, 1.9)
    out_proj = scatter_about(keys[10], (BLOCKS, D, INNER), INNER ** -0.5, 0.625)
    head_weight = scatter_about(keys[11], (CLASSES, D), 0.45, 2.6875)
    head_bias = scatter_about(keys[12], (CLASSES,), 1.0, 6.0, (), jnp.float32)
    labels = place_ends(jax.random.randint(keys[13], (SIDE, SIDE, YS), 0, CLASSES), jax.random.fold_in(keys[13], 1), 0, CLASSES - 1).astype(jnp.int32)
    distance = place_ends(jax.random.randint(keys[14], (CLASSES, SIDE, SIDE, YS), -16384, 16385), jax.random.fold_in(keys[14], 1), -16384, 16384).astype(jnp.int32)
    return {"volume": volume, "norm_gain": norm_gain, "in_proj": in_proj, "dt_proj": dt_proj, "dt_bias": dt_bias, "decay_rate": decay_rate, "conv_weight": conv_weight, "conv_bias": conv_bias, "skip_gain": skip_gain, "out_gain": out_gain, "out_proj": out_proj, "head_weight": head_weight, "head_bias": head_bias, "labels": labels, "distance": distance}


eps = 1e-05
dist_unit = 4096.0
group_limit = 2048

def rms_scale(values, scale_gain):
    mean_sq = lax.optimization_barrier(jnp.mean(values * values, axis=0, keepdims=True))
    return values * lax.rsqrt(mean_sq + eps) * scale_gain[:, None]

def causal_conv(conv_in, tail_block, conv_weight, conv_bias):
    channels = conv_in.shape[0]
    tokens_here = conv_in.shape[1]
    span_count = tokens_here // SCAN_BLOCK
    tap_count = conv_weight.shape[1]
    blocks = conv_in.reshape(channels, span_count, SCAN_BLOCK)
    before = jnp.concatenate([tail_block[:, None, :], blocks[:, :-1]], axis=1)
    paired = jnp.concatenate([before, blocks], axis=2)
    source = lax.broadcasted_iota(jnp.int32, (2 * SCAN_BLOCK, SCAN_BLOCK), 0)
    target = lax.broadcasted_iota(jnp.int32, (2 * SCAN_BLOCK, SCAN_BLOCK), 1)
    conv_sum = jnp.zeros((channels, span_count, SCAN_BLOCK), jnp.float32) + conv_bias[:, None, None]
    for offset in range(tap_count):
        lag = tap_count - 1 - offset
        table = (source == target + SCAN_BLOCK - lag).astype(jnp.bfloat16)
        moved = jnp.einsum('cks,st->ckt', paired.astype(jnp.float32), table.astype(jnp.float32))
        conv_sum = conv_sum + conv_weight[:, offset:offset + 1, None] * moved
    return conv_sum.reshape(channels, tokens_here)

def local_pass(hidden_part, conv_tail, layer_params):
    norm_gain, in_proj, dt_proj, dt_bias, decay_rate, conv_weight, conv_bias, skip_gain, out_gain, out_proj = layer_params
    inner_width = out_proj.shape[1]
    head_count = decay_rate.shape[0]
    head_width = inner_width // head_count
    state_width = (in_proj.shape[0] - 2 * inner_width) // 2
    tokens_here = hidden_part.shape[1]
    span_count = tokens_here // SCAN_BLOCK
    normed = rms_scale(hidden_part.astype(jnp.float32), norm_gain).astype(jnp.bfloat16)
    projected = jnp.dot(in_proj, normed, preferred_element_type=jnp.float32).astype(jnp.bfloat16)
    dt_raw = jnp.dot(dt_proj, normed, preferred_element_type=jnp.float32)
    gate_part = projected[:inner_width]
    conv_in = projected[inner_width:]
    conv_sum = causal_conv(conv_in, conv_tail, conv_weight, conv_bias)
    conv_out = jax.nn.silu(conv_sum).astype(jnp.bfloat16)
    next_tail = conv_in[:, tokens_here - SCAN_BLOCK:]
    inner_values = conv_out[:inner_width]
    write_coef = conv_out[inner_width:inner_width + state_width]
    read_coef = conv_out[inner_width + state_width:]
    step_size = jax.nn.softplus(dt_raw + dt_bias[:, None])
    log_decay = -decay_rate[:, None] * step_size
    cum_decay = jnp.cumsum(log_decay.reshape(head_count, span_count, SCAN_BLOCK), axis=2)
    step_blocks = step_size.reshape(head_count, span_count, SCAN_BLOCK)
    write_blocks = write_coef.reshape(state_width, span_count, SCAN_BLOCK).astype(jnp.float32)
    read_blocks = read_coef.reshape(state_width, span_count, SCAN_BLOCK).astype(jnp.float32)
    scores = jnp.einsum('nkt,nks->kts', read_blocks, write_blocks)
    causal_mask = lax.broadcasted_iota(jnp.int32, (SCAN_BLOCK, SCAN_BLOCK), 0) >= lax.broadcasted_iota(jnp.int32, (SCAN_BLOCK, SCAN_BLOCK), 1)
    decay_gap = cum_decay[:, :, :, None] - cum_decay[:, :, None, :]
    decay_weight = jnp.exp(jnp.where(causal_mask, decay_gap, -jnp.inf))
    weights = (scores[None] * decay_weight * step_blocks[:, :, None, :]).astype(jnp.bfloat16)
    inner_heads = inner_values.reshape(head_count, head_width, span_count, SCAN_BLOCK)
    intra_out = jnp.einsum('hkts,hpks->hpkt', weights.astype(jnp.float32), inner_heads.astype(jnp.float32))
    local_out = intra_out + skip_gain[:, None, None, None] * inner_heads.astype(jnp.float32)
    block_decay = cum_decay[:, :, -1]
    carry_weight = jnp.exp(block_decay[:, :, None] - cum_decay) * step_blocks
    scaled_inner = (inner_heads.astype(jnp.float32) * carry_weight[:, None]).astype(jnp.bfloat16)
    block_state = jnp.einsum('hpkl,nkl->khpn', scaled_inner.astype(jnp.float32), write_blocks)
    return (next_tail, (local_out.reshape(inner_width, tokens_here), gate_part, read_coef, cum_decay, block_state, block_decay.T))

def finish_pass(hidden_part, local_out, gate_part, read_coef, cum_decay, entering, layer_params):
    norm_gain, in_proj, dt_proj, dt_bias, decay_rate, conv_weight, conv_bias, skip_gain, out_gain, out_proj = layer_params
    inner_width = out_proj.shape[1]
    head_count = decay_rate.shape[0]
    head_width = inner_width // head_count
    state_width = read_coef.shape[0]
    tokens_here = hidden_part.shape[1]
    span_count = tokens_here // SCAN_BLOCK
    read_blocks = read_coef.reshape(state_width, span_count, SCAN_BLOCK).astype(jnp.float32)
    inter_out = jnp.einsum('khpn,nkl->hpkl', entering.astype(jnp.float32), read_blocks)
    scan_out = local_out.reshape(head_count, head_width, span_count, SCAN_BLOCK) + jnp.exp(cum_decay)[:, None] * inter_out
    gated = scan_out.reshape(inner_width, tokens_here) * jax.nn.silu(gate_part.astype(jnp.float32))
    gated = rms_scale(gated, out_gain).astype(jnp.bfloat16)
    result = hidden_part.astype(jnp.float32) + jnp.dot(out_proj, gated, preferred_element_type=jnp.float32)
    return result.astype(jnp.bfloat16)

def mamba_layer(hidden, layer_params):
    model_width = hidden.shape[0]
    total_tokens = hidden.shape[1]
    group_size = min(group_limit, total_tokens)
    group_count = total_tokens // group_size
    conv_weight = layer_params[5]
    decay_rate = layer_params[4]
    out_proj = layer_params[9]
    head_count = decay_rate.shape[0]
    head_width = out_proj.shape[1] // head_count
    state_width = (layer_params[1].shape[0] - 2 * out_proj.shape[1]) // 2
    pieces = hidden.reshape(model_width, group_count, group_size).transpose(1, 0, 2)
    tail_start = jnp.zeros((conv_weight.shape[0], SCAN_BLOCK), jnp.bfloat16)
    state_start = jnp.zeros((head_count, head_width, state_width), jnp.float32)

    def group_step(carry, hidden_part):
        conv_tail, state_now = carry
        next_tail, parts = local_pass(hidden_part, conv_tail, layer_params)
        local_out, gate_part, read_coef, cum_decay, block_state, block_decay = parts

        def span_step(state_run, item):
            decay_now, contrib = item
            return (jnp.exp(decay_now)[:, None, None] * state_run + contrib, state_run)
        state_next, entering = lax.scan(span_step, state_now, (block_decay, block_state))
        result = finish_pass(hidden_part, local_out, gate_part, read_coef, cum_decay, entering.astype(jnp.bfloat16), layer_params)
        return ((next_tail, state_next), result)
    _, outputs = lax.scan(group_step, (tail_start, state_start), pieces)
    return outputs.transpose(1, 0, 2).reshape(model_width, total_tokens)

def reference(volume, norm_gain, in_proj, dt_proj, dt_bias, decay_rate, conv_weight, conv_bias, skip_gain, out_gain, out_proj, head_weight, head_bias, labels, distance):
    arrays = (norm_gain, in_proj, dt_proj, dt_bias, decay_rate, conv_weight, conv_bias, skip_gain, out_gain, out_proj)
    model_width = volume.shape[0]
    start_seq = volume.reshape(model_width, -1)
    after_first = mamba_layer(start_seq, tuple((entry[0] for entry in arrays)))
    relaid = after_first.reshape(model_width, SIDE, YS, SIDE).transpose(0, 3, 1, 2).reshape(model_width, -1)
    second = mamba_layer(relaid, tuple((entry[1] for entry in arrays)))
    features = second.reshape(model_width, SIDE, SIDE, YS)
    logits = jnp.dot(head_weight, second, preferred_element_type=jnp.float32) + head_bias[:, None]
    row_peak = lax.optimization_barrier(jnp.max(logits, axis=0, keepdims=True))
    shifted = jnp.exp(logits - row_peak)
    partition = lax.optimization_barrier(jnp.sum(shifted, axis=0, keepdims=True))
    probability = shifted / partition
    log_norm = row_peak[0] + jnp.log(partition[0])
    classes = logits.shape[0]
    one_hot = (labels.reshape(1, -1) == lax.broadcasted_iota(jnp.int32, (classes, 1), 0)).astype(jnp.float32)
    distance_map = distance.reshape(classes, -1).astype(jnp.float32) / dist_unit
    expect = lax.optimization_barrier(jnp.sum(probability * distance_map, axis=0))
    voxel_loss = log_norm - lax.optimization_barrier(jnp.sum(one_hot * logits, axis=0)) + expect
    logit_grad = probability - one_hot + probability * (distance_map - expect[None])
    x_index = lax.broadcasted_iota(jnp.int32, (SIDE, SIDE * YS), 0).astype(jnp.float32)
    voxel_weight = 1.0 + 3.0 * x_index / (SIDE - 1.0)
    total_loss = jnp.sum(voxel_weight * voxel_loss.reshape(SIDE, SIDE * YS)) / (2.5 * NTOT)
    return (features, logit_grad.reshape(classes, SIDE, SIDE, YS), total_loss)
```

```python
import functools

import jax
import jax.numpy as jnp
from jax import lax
from jax.experimental import pallas as pl
from jax.experimental.pallas import tpu as pltpu
from jax.sharding import PartitionSpec as P

SCAN_BLOCK = 128
LANES = 128

eps = 1e-05
dist_unit = 4096.0
axes = ("row", "col")
f32, bf16 = jnp.float32, jnp.bfloat16
vmem_bytes = 48 * 1024 * 1024


def silu(v):
    return 0.5 * v * (1.0 + jnp.tanh(0.5 * v))


def rounded(v):
    return v.astype(bf16).astype(f32)


def normalise(hidden, gain_col):
    values = hidden.astype(f32)
    mean_sq = jnp.mean(values * values, axis=0, keepdims=True)
    return (values * lax.rsqrt(mean_sq + eps) * gain_col).astype(bf16)


def project(weight, normed):
    return jnp.dot(weight, normed, preferred_element_type=f32)


def contract(a, b, dim):
    return lax.dot_general(a, b, (((dim,), (dim,)), ((), ())), preferred_element_type=f32)


def spread(rows, first, count, height):
    return jnp.concatenate(
        [jnp.broadcast_to(rows[first + h : first + h + 1], (height, rows.shape[1])) for h in range(count)], axis=0
    )


def taps(conv_in, moved_ref, cols, first):
    rows = conv_in.shape[0]
    lane = lax.broadcasted_iota(jnp.int32, (rows, SCAN_BLOCK), 1)
    tap_count = moved_ref.shape[0] + 1
    total = cols[first : first + rows, tap_count : tap_count + 1] + jnp.zeros((rows, SCAN_BLOCK), f32)
    for offset in range(tap_count):
        lag = tap_count - 1 - offset
        if lag:
            now = pltpu.roll(conv_in, lag, 1)
            shifted = jnp.where(lane < lag, moved_ref[lag - 1], now)
            moved_ref[lag - 1] = now
        else:
            shifted = conv_in
        total = total + cols[first : first + rows, offset : offset + 1] * shifted
    return total


def keep_tail(tail_in, moved_ref):
    for lag in range(1, moved_ref.shape[0] + 1):
        moved_ref[lag - 1] = pltpu.roll(tail_in, lag, 1)


def state_kernel(
    heads, hid_ref, tail_ref, weight_ref, dt_ref, cols_ref, gain_ref, head_ref, tri_ref,
    inner_ref, write_ref, dec_ref, state_ref, total_ref, moved_ref, carry_ref,
):
    group = hid_ref.shape[0]
    inner = inner_ref.shape[1]
    width = inner // heads
    state = write_ref.shape[1]
    weight = weight_ref[...]
    gain_col = gain_ref[...]
    cols = cols_ref[...]
    head_cols = head_ref[...]

    @pl.when(pl.program_id(0) == 0)
    def _():
        carry_ref[...] = jnp.zeros_like(carry_ref)
        tail_in = rounded(project(weight, normalise(tail_ref[...], gain_col)))
        keep_tail(tail_in, moved_ref)

    lane = lax.broadcasted_iota(jnp.int32, (1, LANES), 1)
    normed = [normalise(hid_ref[u], gain_col) for u in range(group)]
    dt_raw = [project(dt_ref[...], n) for n in normed]
    step = [v + head_cols[:, 0:1] for v in dt_raw]
    step = [jnp.maximum(v, 0.0) + jnp.log1p(jnp.exp(-jnp.abs(v))) for v in step]
    log_decay = jnp.concatenate([head_cols[:, 1:2] * v for v in step], axis=0)
    high = log_decay.astype(bf16)
    rest = log_decay - high.astype(f32)
    middle = rest.astype(bf16)
    low = (rest - middle.astype(f32)).astype(bf16)
    tri = tri_ref[...]
    cum_all = project(low, tri) + project(middle, tri) + project(high, tri)
    for u in range(group):
        cum = cum_all[8 * u : 8 * u + 8]
        last = jnp.broadcast_to(cum[:, SCAN_BLOCK - 1 :], cum.shape)
        carry_weight = jnp.exp(last - cum) * step[u]
        dec_ref[u, 0:8, :] = cum
        dec_ref[u, 8:16, :] = step[u]
        conv_in = rounded(project(weight, normed[u]))
        conv_out = silu(taps(conv_in, moved_ref, cols, 0)).astype(bf16)
        inner_values = conv_out[:inner]
        write = conv_out[inner:]
        inner_ref[u] = inner_values
        write_ref[u] = write
        scaled = inner_values.astype(f32) * spread(carry_weight, 0, heads, width)
        scaled = jnp.concatenate([scaled, jnp.zeros((LANES - inner, SCAN_BLOCK), f32)], axis=0)
        block_state = contract(write, scaled.astype(bf16), 1)
        decay_row = last[heads - 1 : heads]
        for h in range(heads - 2, -1, -1):
            decay_row = jnp.where(lane < (h + 1) * width, last[h : h + 1], decay_row)
        state_ref[u] = carry_ref[...]
        carry_ref[0:state, :] = jnp.exp(decay_row) * carry_ref[0:state, :] + block_state
        carry_ref[state:, :] = carry_ref[state:, :] + decay_row
    total_ref[...] = carry_ref[...]


def local_kernel(
    heads, hid_ref, tail_ref, weight_ref, cols_ref, gain_ref, head_ref, inner_ref, write_ref, dec_ref,
    local_ref, gate_ref, read_ref, moved_ref,
):
    group = hid_ref.shape[0]
    inner = inner_ref.shape[1]
    width = inner // heads
    weight = weight_ref[...]
    gain_col = gain_ref[...]
    cols = cols_ref[...]
    head_cols = head_ref[...]
    conv_first = cols.shape[0] - read_ref.shape[1]

    @pl.when(pl.program_id(0) == 0)
    def _():
        tail_in = rounded(project(weight[inner:], normalise(tail_ref[...], gain_col)))
        keep_tail(tail_in, moved_ref)

    source = lax.broadcasted_iota(jnp.int32, (SCAN_BLOCK, SCAN_BLOCK), 0)
    target = lax.broadcasted_iota(jnp.int32, (SCAN_BLOCK, SCAN_BLOCK), 1)
    causal = source <= target
    for u in range(group):
        normed = normalise(hid_ref[u], gain_col)
        projected = rounded(project(weight, normed))
        gate_ref[u] = silu(projected[:inner])
        read = silu(taps(projected[inner:], moved_ref, cols, conv_first)).astype(bf16)
        read_ref[u] = read
        scores = contract(write_ref[u], read, 0)
        cum = dec_ref[u, 0:8, :]
        step = dec_ref[u, 8:16, :]
        source_cols = jnp.transpose(cum - jnp.log(step), (1, 0))
        for h in range(heads):
            gap = jnp.where(causal, cum[h : h + 1] - source_cols[:, h : h + 1], -jnp.inf)
            weights = (scores * jnp.exp(gap)).astype(bf16)
            values = inner_ref[u, h * width : (h + 1) * width, :]
            local_ref[u, h * width : (h + 1) * width, :] = (
                project(values, weights) + head_cols[h : h + 1, 2:3] * values.astype(f32)
            )


def finished(u, heads, enter, hid_ref, local_ref, gate_ref, read_ref, dec_ref, state_ref, out_gain, out_proj):
    inner = local_ref.shape[1]
    width = inner // heads
    state = read_ref.shape[1]
    entering = jnp.exp(state_ref[u, state : state + 1, :]) * enter + state_ref[u, 0:state, :]
    inter = contract(entering.astype(bf16), read_ref[u], 0)[:inner]
    scan_out = local_ref[u] + spread(jnp.exp(dec_ref[u, 0:8, :]), 0, heads, width) * inter
    gated = scan_out * gate_ref[u]
    mean_sq = jnp.mean(gated * gated, axis=0, keepdims=True)
    gated = (gated * lax.rsqrt(mean_sq + eps) * out_gain).astype(bf16)
    return (hid_ref[u].astype(f32) + project(out_proj, gated)).astype(bf16)


def finish_kernel(
    heads, enter_ref, hid_ref, local_ref, gate_ref, read_ref, dec_ref, state_ref, gain_ref, proj_ref, out_ref
):
    enter = enter_ref[0 : read_ref.shape[1], :]
    for u in range(hid_ref.shape[0]):
        out_ref[u] = finished(
            u, heads, enter, hid_ref, local_ref, gate_ref, read_ref, dec_ref, state_ref, gain_ref[...], proj_ref[...]
        )


def head_kernel(
    heads, enter_ref, hid_ref, local_ref, gate_ref, read_ref, dec_ref, state_ref, gain_ref, proj_ref,
    head_ref, bias_ref, labels_ref, distance_ref, features_ref, grad_ref, loss_ref, feature_scr, logit_scr,
):
    group = hid_ref.shape[0]
    classes = distance_ref.shape[0]
    enter = enter_ref[0 : read_ref.shape[1], :]

    @pl.when(pl.program_id(0) == 0)
    def _():
        loss_ref[...] = jnp.zeros_like(loss_ref)

    for u in range(group):
        result = finished(
            u, heads, enter, hid_ref, local_ref, gate_ref, read_ref, dec_ref, state_ref, gain_ref[...], proj_ref[...]
        )
        logits = project(head_ref[...], result) + bias_ref[...]
        feature_scr[pl.ds(u, result.shape[0], stride=group), :] = result.astype(f32)
        logit_scr[pl.ds(u, logits.shape[0], stride=group), :] = logits
    features = feature_scr[...].reshape(-1, group, SCAN_BLOCK)
    features_ref[...] = features.astype(bf16)
    logits = logit_scr[...].reshape(-1, group, SCAN_BLOCK)[:classes]
    labels = labels_ref[...]
    peak = jnp.max(logits, axis=0)
    shifted = jnp.exp(logits - peak[None])
    partition = jnp.sum(shifted, axis=0)
    probability = shifted / partition[None]
    distance_map = distance_ref[...].astype(f32) * (1.0 / dist_unit)
    weighted = probability * distance_map
    expect = jnp.sum(weighted, axis=0)
    hot = labels[None] == lax.broadcasted_iota(jnp.int32, logits.shape, 0)
    chosen = jnp.sum(jnp.where(hot, logits, 0.0), axis=0)
    loss = peak + jnp.log(partition) - chosen + expect
    grad_ref[...] = probability - jnp.where(hot, 1.0, 0.0) + weighted - probability * expect[None]
    loss_ref[...] += jnp.sum(loss.reshape(-1, 8, SCAN_BLOCK), axis=0)


def whole(shape):
    return pl.BlockSpec(shape, lambda g: (0,) * len(shape))


def blocks(group, *rest):
    return pl.BlockSpec((group,) + rest, lambda g: (g,) + (0,) * len(rest))


def params():
    return pltpu.CompilerParams(vmem_limit_bytes=vmem_bytes)


def prefix_state(total):
    size = lax.axis_size(axes)
    me = lax.axis_index(axes)
    rows = total.shape[0] - 8

    def combine(earlier, latter):
        log = latter[rows : rows + 1]
        return jnp.concatenate(
            [jnp.exp(log) * earlier[:rows] + latter[:rows], earlier[rows:] + latter[rows:]], axis=0
        )

    before = jnp.zeros_like(total)
    reach = 1
    while reach < size:
        other = lax.ppermute(total, axes, [(i, i ^ reach) for i in range(size)])
        upper = (me & reach) != 0
        before = jnp.where(upper, combine(other, before), before)
        if 2 * reach < size:
            total = combine(jnp.where(upper, other, total), jnp.where(upper, total, other))
        reach *= 2
    return before


def layer_start(hidden, tail, prep, group):
    count, model, _ = hidden.shape
    heads, inner, state = prep["heads"], prep["inner"], prep["state"]
    steps = count // group
    conv_cols = prep["cols"]
    tile = lambda rows, kind: jax.ShapeDtypeStruct((count, rows, SCAN_BLOCK), kind)
    first_rows = inner + state
    inner_values, write, dec, states, total = pl.pallas_call(
        functools.partial(state_kernel, heads),
        grid=(steps,),
        in_specs=[
            blocks(group, model, SCAN_BLOCK),
            whole((model, SCAN_BLOCK)),
            whole((first_rows, model)),
            whole((8, model)),
            whole(conv_cols.shape),
            whole((model, 1)),
            whole((8, 8)),
            whole((SCAN_BLOCK, SCAN_BLOCK)),
        ],
        out_specs=[
            blocks(group, inner, SCAN_BLOCK),
            blocks(group, state, SCAN_BLOCK),
            blocks(group, 16, SCAN_BLOCK),
            blocks(group, state + 8, LANES),
            whole((state + 8, LANES)),
        ],
        out_shape=[
            tile(inner, bf16),
            tile(state, bf16),
            tile(16, f32),
            tile(state + 8, f32),
            jax.ShapeDtypeStruct((state + 8, LANES), f32),
        ],
        scratch_shapes=[
            pltpu.VMEM((prep["taps"] - 1, first_rows, SCAN_BLOCK), f32),
            pltpu.VMEM((state + 8, LANES), f32),
        ],
        compiler_params=params(),
        name="states",
    )(
        hidden, tail, prep["in_first"], prep["dt_proj"], conv_cols, prep["gain"], prep["head_cols"], prep["tri"]
    )
    local, gate, read = pl.pallas_call(
        functools.partial(local_kernel, heads),
        grid=(steps,),
        in_specs=[
            blocks(group, model, SCAN_BLOCK),
            whole((model, SCAN_BLOCK)),
            whole((first_rows, model)),
            whole(conv_cols.shape),
            whole((model, 1)),
            whole((8, 8)),
            blocks(group, inner, SCAN_BLOCK),
            blocks(group, state, SCAN_BLOCK),
            blocks(group, 16, SCAN_BLOCK),
        ],
        out_specs=[
            blocks(group, inner, SCAN_BLOCK),
            blocks(group, inner, SCAN_BLOCK),
            blocks(group, state, SCAN_BLOCK),
        ],
        out_shape=[tile(inner, f32), tile(inner, f32), tile(state, bf16)],
        scratch_shapes=[pltpu.VMEM((prep["taps"] - 1, state, SCAN_BLOCK), f32)],
        compiler_params=params(),
        name="local",
    )(
        hidden, tail, prep["in_second"], conv_cols, prep["gain"], prep["head_cols"], inner_values, write, dec
    )
    enter = prefix_state(total)
    return enter, local, gate, read, dec, states


def finish_specs(group, model, inner, state):
    return [
        whole((state + 8, LANES)),
        blocks(group, model, SCAN_BLOCK),
        blocks(group, inner, SCAN_BLOCK),
        blocks(group, inner, SCAN_BLOCK),
        blocks(group, state, SCAN_BLOCK),
        blocks(group, 16, SCAN_BLOCK),
        blocks(group, state + 8, LANES),
        whole((inner, 1)),
        whole((model, inner)),
    ]


def prepare(norm_gain, in_proj, dt_proj, dt_bias, decay_rate, conv_weight, conv_bias, skip_gain, out_gain, out_proj):
    inner = out_proj.shape[1]
    heads = decay_rate.shape[0]
    state = (in_proj.shape[0] - 2 * inner) // 2
    tap_count = conv_weight.shape[1]
    cols = jnp.concatenate([conv_weight, conv_bias[:, None]], axis=1)
    cols = jnp.pad(cols, ((0, 0), (0, 8 - cols.shape[1])))
    head_cols = jnp.stack([dt_bias, -decay_rate, skip_gain], axis=1)
    return dict(
        heads=heads,
        inner=inner,
        state=state,
        taps=tap_count,
        cols=cols,
        gain=norm_gain[:, None],
        in_first=in_proj[inner : 2 * inner + state],
        in_second=jnp.concatenate([in_proj[:inner], in_proj[2 * inner + state :]], axis=0),
        dt_proj=jnp.pad(dt_proj, ((0, 8 - heads), (0, 0))),
        head_cols=jnp.pad(head_cols, ((0, 8 - heads), (0, 8 - head_cols.shape[1]))),
        out_gain=out_gain[:, None],
        out_proj=out_proj,
        tri=(
            lax.broadcasted_iota(jnp.int32, (SCAN_BLOCK, SCAN_BLOCK), 0)
            <= lax.broadcasted_iota(jnp.int32, (SCAN_BLOCK, SCAN_BLOCK), 1)
        ).astype(bf16),
    )


def per_device(
    volume, norm_gain, in_proj, dt_proj, dt_bias, decay_rate, conv_weight, conv_bias, skip_gain, out_gain,
    out_proj, head_weight, head_bias, labels, distance,
):
    arrays = (
        norm_gain, in_proj, dt_proj, dt_bias, decay_rate, conv_weight, conv_bias, skip_gain, out_gain, out_proj
    )
    size = lax.axis_size(axes)
    me = lax.axis_index(axes)
    model, _, cells_y, cells_x = volume.shape
    classes = head_weight.shape[0]
    prep = [prepare(*(entry[b] for entry in arrays)) for b in range(2)]
    heads, inner, state = (prep[0][k] for k in ("heads", "inner", "state"))
    forward = [(i, i + 1) for i in range(size - 1)]
    count = cells_y * cells_x // SCAN_BLOCK
    group = min(16, count)

    hidden = volume.reshape(model, count, SCAN_BLOCK).transpose(1, 0, 2)
    tail = lax.ppermute(hidden[-1], axes, forward)
    parts = layer_start(hidden, tail, prep[0], group)
    enter, local, gate, read, dec, states = parts
    after = pl.pallas_call(
        functools.partial(finish_kernel, heads),
        grid=(count // group,),
        in_specs=finish_specs(group, model, inner, state),
        out_specs=blocks(group, model, SCAN_BLOCK),
        out_shape=jax.ShapeDtypeStruct(hidden.shape, bf16),
        compiler_params=params(),
        name="finish",
    )(enter, hidden, local, gate, read, dec, states, prep[0]["out_gain"], prep[0]["out_proj"])

    planes = after.transpose(1, 0, 2).reshape(model, cells_y, cells_x).transpose(2, 0, 1)
    hidden = lax.all_to_all(planes, axes, split_axis=0, concat_axis=0, tiled=True)
    count = hidden.shape[0]
    group = min(16, count)
    tail = lax.ppermute(hidden[-1], axes, forward)
    parts = layer_start(hidden, tail, prep[1], group)
    enter, local, gate, read, dec, states = parts
    pad_classes = 16
    head_pad = jnp.pad(head_weight, ((0, pad_classes - classes), (0, 0)))
    bias_pad = jnp.pad(head_bias, (0, pad_classes - classes))[:, None]
    plane = lambda rows: pl.BlockSpec((rows, group, SCAN_BLOCK), lambda g: (0, g, 0))
    features, grad, loss = pl.pallas_call(
        functools.partial(head_kernel, heads),
        grid=(count // group,),
        in_specs=finish_specs(group, model, inner, state)
        + [
            whole((pad_classes, model)),
            whole((pad_classes, 1)),
            pl.BlockSpec((group, SCAN_BLOCK), lambda g: (g, 0)),
            plane(classes),
        ],
        out_specs=[plane(model), plane(classes), whole((8, SCAN_BLOCK))],
        out_shape=[
            jax.ShapeDtypeStruct((model, count, SCAN_BLOCK), bf16),
            jax.ShapeDtypeStruct((classes, count, SCAN_BLOCK), f32),
            jax.ShapeDtypeStruct((8, SCAN_BLOCK), f32),
        ],
        scratch_shapes=[
            pltpu.VMEM((model * group, SCAN_BLOCK), f32),
            pltpu.VMEM((pad_classes * group, SCAN_BLOCK), f32),
        ],
        compiler_params=params(),
        name="heads",
    )(
        enter, hidden, local, gate, read, dec, states, prep[1]["out_gain"], prep[1]["out_proj"],
        head_pad, bias_pad, labels.reshape(count, SCAN_BLOCK), distance.reshape(classes, count, SCAN_BLOCK),
    )
    voxel_weight = 1.0 + 3.0 * me.astype(f32) / (size - 1.0)
    voxel_count = count * SCAN_BLOCK * size
    own = voxel_weight * jnp.sum(loss, axis=0, keepdims=True)
    shared = lax.all_to_all(jnp.broadcast_to(own, (size, SCAN_BLOCK)), axes, 0, 0, tiled=True)
    total_loss = jnp.sum(shared) / (2.5 * voxel_count)
    return (
        features.reshape(model, 1, count, SCAN_BLOCK),
        grad.reshape(classes, 1, count, SCAN_BLOCK),
        total_loss,
    )


def solution(mesh):
    plane = P(None, axes, None, None)
    return jax.shard_map(
        per_device,
        mesh=mesh,
        in_specs=(plane,) + (P(),) * 12 + (P(axes, None, None), plane),
        out_specs=(plane, plane, P()),
        check_vma=False,
    )
```

```python
import functools

import jax
import jax.numpy as jnp
from jax import lax
from jax.experimental import pallas as pl
from jax.experimental.pallas import tpu as pltpu
from jax.sharding import PartitionSpec as P

SCAN_BLOCK = 128
LANES = 128

eps = 1e-05
dist_unit = 4096.0
axes = ("row", "col")
f32, bf16 = jnp.float32, jnp.bfloat16
vmem_bytes = 24 * 1024 * 1024
wide = 4


def half_silu(v):
    return v + v * jnp.tanh(v)


def rounded(v):
    return v.astype(bf16).astype(f32)


def normalise(hidden, gain_col):
    values = hidden.astype(f32)
    mean_sq = jnp.mean(values * values, axis=0, keepdims=True)
    return (values * lax.rsqrt(mean_sq + eps) * gain_col).astype(bf16)


def project(weight, normed):
    return jnp.dot(weight, normed, preferred_element_type=f32)


def contract(a, b, dim):
    return lax.dot_general(a, b, (((dim,), (dim,)), ((), ())), preferred_element_type=f32)


def spread(rows, first, count, height):
    return jnp.concatenate(
        [jnp.broadcast_to(rows[first + h : first + h + 1], (height, rows.shape[1])) for h in range(count)], axis=0
    )


def side_by_side(ref, first, count, rows=None):
    rows = ref.shape[1] if rows is None else rows
    return jnp.concatenate([ref[u][:rows] for u in range(first, first + count)], axis=1)


def span(u, count=1):
    return slice(u * SCAN_BLOCK, (u + count) * SCAN_BLOCK)


def padded(values, rows, lanes):
    if values.shape[1] < lanes:
        values = jnp.concatenate([values, jnp.zeros((values.shape[0], lanes - values.shape[1]), f32)], axis=1)
    if values.shape[0] < rows:
        values = jnp.concatenate([values, jnp.zeros((rows - values.shape[0], lanes), f32)], axis=0)
    return values


def turned(values):
    lanes = -(-values.shape[1] // LANES) * LANES
    return jnp.transpose(padded(values, -(-values.shape[0] // 8) * 8, lanes), (1, 0))


def columns(*rows):
    return turned(jnp.concatenate(rows, axis=0))


def columns_of(layer, rows_ref):
    return jnp.transpose(rows_ref[layer], (1, 0))


def tail_tile(tail_ref, model):
    if tail_ref.ndim == 2:
        return tail_ref[...]
    block = tail_ref[0].astype(f32)
    rows = block[model:]
    kept = lax.broadcasted_iota(jnp.int32, rows.shape, 0) >= rows.shape[0] - 3
    rows = jnp.where(kept, rows, 0.0)
    tile = jnp.concatenate([jnp.zeros((SCAN_BLOCK - rows.shape[0], LANES), f32), rows], axis=0)
    return jnp.transpose(tile, (1, 0))[:model].astype(bf16)


def swap_lanes(parts):
    count = len(parts)
    if count == 1:
        return parts
    width = LANES // count
    place = lax.broadcasted_iota(jnp.int32, parts[0].shape, 1) // width
    result = []
    for b in range(count):
        total = None
        for a, part in enumerate(parts):
            shift = (a - b) * width % LANES
            moved = pltpu.roll(part, shift, 1) if shift else part
            total = moved if total is None else jnp.where(place == a, moved, total)
        result.append(total)
    return result


def to_sequence(volume_ref, hid_ref, turn_ref, tile_ref):
    model, cells_x, cells_y = volume_ref.shape
    count = hid_ref.shape[0]
    per = LANES // cells_x
    for c in range(0, model, per):
        turn_ref[c // per] = jnp.transpose(volume_ref[c : c + per].astype(f32).reshape(LANES, cells_y), (1, 0))
    for c in range(0, model, per):
        parts = [turn_ref[c // per, pl.ds(a, count, stride=per), :] for a in range(per)]
        for j, part in enumerate(swap_lanes(parts)):
            tile_ref[pl.ds(c + j, count, stride=model), :] = part
    for u in range(count):
        hid_ref[u] = tile_ref[u * model : (u + 1) * model, :].astype(bf16)


def to_planes(tile_ref, out_ref, turn_ref, plane_ref, model, cells_x):
    rows = out_ref.shape[1]
    cells_y = out_ref.shape[2]
    per = LANES // cells_x
    count = cells_y // per
    for c in range(0, model, per):
        parts = [tile_ref[pl.ds(c + j, count, stride=model), :] for j in range(per)]
        for a, part in enumerate(swap_lanes(parts)):
            turn_ref[c // per, pl.ds(a, count, stride=per), :] = part
    for c in range(0, model, per):
        turn = jnp.transpose(turn_ref[c // per], (1, 0))
        for j in range(per):
            plane_ref[pl.ds(c + j, cells_x, stride=rows), :] = turn[j * cells_x : (j + 1) * cells_x]
    for x in range(cells_x + 1):
        plane_ref[x * rows + model : (x + 1) * rows, :] = jnp.zeros((rows - model, LANES), f32)
    for y in range(cells_y - 3, cells_y):
        block, a = divmod(y, per)
        turn = jnp.transpose(padded(tile_ref[block * model : (block + 1) * model, :], LANES, LANES), (1, 0))
        at = 2 * rows - cells_y + y
        plane_ref[pl.ds(at, cells_x, stride=rows), :] = turn[a * cells_x : (a + 1) * cells_x]
    for x in range(cells_x):
        out_ref[x] = plane_ref[x * rows : (x + 1) * rows, :].astype(bf16)


def convolve(proj_ref, rows, cols, first, outs):
    group = proj_ref.shape[1] // SCAN_BLOCK - 1
    tap_count = 4
    for r in range(0, rows, 16):
        conv_in = proj_ref[r : r + 16, :]
        half = 0.5 * cols[first + r : first + r + 16, :]
        total = None
        for offset in range(tap_count):
            lag = tap_count - 1 - offset
            shifted = pltpu.roll(conv_in, lag, 1) if lag else conv_in
            term = half[:, offset : offset + 1] * shifted[:, SCAN_BLOCK:]
            total = half[:, tap_count : tap_count + 1] + term if total is None else total + term
        conv_out = half_silu(total).astype(bf16)
        ref, at = next((ref, r - low) for ref, low, high in outs if low <= r < high)
        for u in range(group):
            ref[u, at : at + 16, :] = conv_out[:, span(u)]
    proj_ref[:, span(0)] = proj_ref[:, span(group)]


def state_kernel(
    layer, heads, from_volume, hid_ref, tail_ref, matrix_ref, rows_ref, inner_ref, write_ref, dec_ref, state_ref, total_ref, *rest
):
    if from_volume:
        volume_ref, hid_ref, proj_ref, carry_ref, turn_ref, tile_ref = (hid_ref,) + rest

        @pl.when(pl.program_id(0) == 0)
        def _():
            to_sequence(volume_ref, hid_ref, turn_ref, tile_ref)

        hid_ref = hid_ref.at[pl.ds(pl.program_id(0) * inner_ref.shape[0], inner_ref.shape[0])]
    else:
        proj_ref, carry_ref = rest
    model = matrix_ref.shape[1]
    group = inner_ref.shape[0]
    inner = inner_ref.shape[1]
    width = inner // heads
    state = write_ref.shape[1]
    rows = inner + state
    weight = jnp.transpose(matrix_ref[layer].astype(f32), (1, 0))
    dt_first = 2 * (inner + state)
    weight = jnp.concatenate([weight[inner : inner + rows], weight[dt_first : dt_first + 8]], axis=0).astype(bf16)
    cols = columns_of(layer, rows_ref)
    gain_col = cols[:model, 5:6]
    head_cols = cols[:8, 6:8]

    @pl.when(pl.program_id(0) == 0)
    def _():
        carry_ref[...] = jnp.zeros_like(carry_ref)
        proj_ref[:, span(0)] = rounded(project(weight, normalise(tail_tile(tail_ref, model), gain_col))[:rows])

    lane = lax.broadcasted_iota(jnp.int32, (1, LANES), 1)
    dt_raw = []
    for q in range(0, group, wide):
        projected = project(weight, normalise(side_by_side(hid_ref, q, wide, model), gain_col))
        proj_ref[:, span(q + 1, wide)] = rounded(projected[:rows])
        dt_raw.append(projected[rows:])
    step = jnp.concatenate(dt_raw, axis=1) + head_cols[:, 0:1]
    step = jnp.maximum(step, 0.0) + jnp.log1p(jnp.exp(-jnp.abs(step)))
    log_decay = head_cols[:, 1:2] * step
    step = jnp.concatenate([step[:, span(u)] for u in range(group)], axis=0)
    log_decay = jnp.concatenate([log_decay[:, span(u)] for u in range(group)], axis=0)
    high = log_decay.astype(bf16)
    rest = log_decay - high.astype(f32)
    middle = rest.astype(bf16)
    low = (rest - middle.astype(f32)).astype(bf16)
    square = (SCAN_BLOCK, SCAN_BLOCK)
    earlier = lax.broadcasted_iota(jnp.int32, square, 0) <= lax.broadcasted_iota(jnp.int32, square, 1)
    tri = jnp.where(earlier, 1.0, 0.0).astype(bf16)
    cum = project(low, tri) + project(middle, tri) + project(high, tri)
    last = jnp.broadcast_to(cum[:, SCAN_BLOCK - 1 :], cum.shape)
    carry_weight = jnp.exp(last - cum) * step
    for u in range(group):
        dec_ref[u, 0:8, :] = cum[8 * u : 8 * u + 8]
        dec_ref[u, 8:16, :] = step[8 * u : 8 * u + 8]
    convolve(proj_ref, rows, cols, 0, [(inner_ref, 0, inner), (write_ref, inner, rows)])
    decay_rows, block_states = [], []
    for u in range(group):
        row = last[8 * u + heads - 1 : 8 * u + heads]
        for h in range(heads - 2, -1, -1):
            row = jnp.where(lane < (h + 1) * width, last[8 * u + h : 8 * u + h + 1], row)
        decay_rows.append(row)
        scaled = inner_ref[u].astype(f32) * spread(carry_weight, 8 * u, heads, width)
        scaled = jnp.concatenate([scaled.astype(bf16), jnp.zeros((LANES - inner, SCAN_BLOCK), bf16)], axis=0)
        block_states.append(contract(write_ref[u], scaled, 1))
    running = carry_ref[0:state, :]
    running_log = carry_ref[state:, :]
    for u in range(group):
        state_ref[u, 0:state, :] = running
        state_ref[u, state:, :] = running_log
        running = jnp.exp(decay_rows[u]) * running + block_states[u]
        running_log = running_log + decay_rows[u]
    carry_ref[0:state, :] = running
    carry_ref[state:, :] = running_log
    total_ref[0:state, :] = running
    total_ref[state:, :] = running_log


def local_kernel(
    layer, heads, hid_ref, tail_ref, matrix_ref, rows_ref, inner_ref, write_ref, dec_ref,
    local_ref, gate_ref, read_ref, proj_ref, score_ref, weights_ref,
):
    group = hid_ref.shape[0]
    model = matrix_ref.shape[1]
    inner = inner_ref.shape[1]
    width = inner // heads
    state = read_ref.shape[1]
    weight = jnp.transpose(matrix_ref[layer].astype(f32), (1, 0))
    weight = jnp.concatenate([weight[:inner], weight[2 * inner + state : 2 * (inner + state)]], axis=0).astype(bf16)
    cols = columns_of(layer, rows_ref)
    gain_col = cols[:model, 5:6]
    skip_cols = cols[:8, 8:9]

    @pl.when(pl.program_id(0) == 0)
    def _():
        proj_ref[:, span(0)] = rounded(project(weight[inner:], normalise(tail_tile(tail_ref, model), gain_col)))

    for q in range(0, group, wide):
        projected = rounded(project(weight, normalise(side_by_side(hid_ref, q, wide, model), gain_col)))
        proj_ref[:, span(q + 1, wide)] = projected[inner:]
        gate = half_silu(0.5 * projected[:inner])
        for u in range(wide):
            gate_ref[q + u] = gate[:, span(u)]
    convolve(proj_ref, state, cols, inner + state, [(read_ref, 0, state)])
    source = lax.broadcasted_iota(jnp.int32, (SCAN_BLOCK, SCAN_BLOCK), 0)
    target = lax.broadcasted_iota(jnp.int32, (SCAN_BLOCK, SCAN_BLOCK), 1)
    causal = source <= target
    log2e = 1.4426950408889634
    cum = jnp.concatenate([dec_ref[u, 0:8, :] for u in range(group)], axis=0)
    step = jnp.concatenate([dec_ref[u, 8:16, :] for u in range(group)], axis=0)
    source_cols = (cum - jnp.log(step)) * log2e
    if 8 * group < SCAN_BLOCK:
        unused = jnp.zeros((SCAN_BLOCK - 8 * group, SCAN_BLOCK), f32)
        source_cols = jnp.concatenate([source_cols, unused], axis=0)
    source_cols = jnp.transpose(source_cols, (1, 0))
    cum = cum * log2e
    for u in range(group):
        score_ref[u] = contract(write_ref[u], read_ref[u], 0)
    for u in range(group):
        scores = score_ref[u]
        for h in range(heads):
            at = 8 * u + h
            gap = jnp.where(causal, cum[at : at + 1] - source_cols[:, at : at + 1], -jnp.inf)
            weights_ref[u, h] = (scores * jnp.exp2(gap)).astype(bf16)
    for u in range(group):
        for h in range(heads):
            values = inner_ref[u, h * width : (h + 1) * width, :]
            local_ref[u, h * width : (h + 1) * width, :] = (
                project(values, weights_ref[u, h]) + skip_cols[h : h + 1, 0:1] * values.astype(f32)
            )


def finished(q, layer, heads, enter, refs, out_gain, out_proj):
    hid_ref, local_ref, gate_ref, read_ref, dec_ref, state_ref = refs
    inner = local_ref.shape[1]
    width = inner // heads
    state = read_ref.shape[1]
    inter = []
    for u in range(q, q + wide):
        entering = jnp.exp(state_ref[u, state : state + 1, :]) * enter + state_ref[u, 0:state, :]
        inter.append(contract(entering.astype(bf16), read_ref[u], 0)[:inner])
    decay = jnp.exp(jnp.concatenate([dec_ref[u, 0:8, :] for u in range(q, q + wide)], axis=1))
    scan_out = side_by_side(local_ref, q, wide) + spread(decay, 0, heads, width) * jnp.concatenate(inter, axis=1)
    gated = scan_out * side_by_side(gate_ref, q, wide)
    mean_sq = jnp.mean(gated * gated, axis=0, keepdims=True)
    gated = (gated * lax.rsqrt(mean_sq + eps) * out_gain).astype(bf16)
    hidden = side_by_side(hid_ref, q, wide, out_proj.shape[0]).astype(f32)
    return (hidden + project(out_proj, gated)).astype(bf16)


def entered(odd_ref, half_ref, other_half_ref, other_ref, state):
    odd = odd_ref[0] != 0
    mine, other = half_ref[...], other_half_ref[...]
    chip = jnp.concatenate([jnp.where(odd, other, mine), jnp.where(odd, mine, other)], axis=0)
    joined = jnp.exp(other_ref[state : state + 1, :]) * chip + other_ref[0:state, :]
    return jnp.where(odd, joined, chip)


def finish_kernel(
    layer, heads, cells_x, odd_ref, half_ref, other_half_ref, other_ref, hid_ref, local_ref, gate_ref, read_ref, dec_ref,
    state_ref, matrix_ref, rows_ref, out_ref, tile_ref, turn_ref, plane_ref,
):
    group = hid_ref.shape[0]
    model = matrix_ref.shape[1]
    inner = local_ref.shape[1]
    refs = (hid_ref, local_ref, gate_ref, read_ref, dec_ref, state_ref)
    enter = entered(odd_ref, half_ref, other_half_ref, other_ref, read_ref.shape[1])
    out_gain = columns_of(layer, rows_ref)[:inner, 9:10]
    out_proj = matrix_ref[layer][:, -LANES:][:, :inner]
    for q in range(0, group, wide):
        result = finished(q, layer, heads, enter, refs, out_gain, out_proj).astype(f32)
        for u in range(wide):
            at = pl.multiple_of((pl.program_id(0) * group + q + u) * model, 8)
            tile_ref[pl.ds(at, model), :] = result[:, span(u)]

    @pl.when(pl.program_id(0) == pl.num_programs(0) - 1)
    def _():
        to_planes(tile_ref, out_ref, turn_ref, plane_ref, model, cells_x)


def head_kernel(
    layer, heads, odd_ref, half_ref, other_half_ref, other_ref, hid_ref, local_ref, gate_ref, read_ref, dec_ref,
    state_ref, matrix_ref, rows_ref, head_ref, bias_ref, labels_ref, distance_ref, features_ref, grad_ref, loss_ref,
    feature_scr, logit_scr, sum_scr,
):
    group = hid_ref.shape[0]
    classes = distance_ref.shape[0]
    inner = local_ref.shape[1]
    refs = (hid_ref, local_ref, gate_ref, read_ref, dec_ref, state_ref)
    enter = entered(odd_ref, half_ref, other_half_ref, other_ref, read_ref.shape[1])
    out_gain = columns_of(layer, rows_ref)[:inner, 9:10]
    out_proj = matrix_ref[layer][:, -LANES:][:, :inner]
    bias = columns(bias_ref[...])[:classes, 0:1]

    @pl.when(pl.program_id(0) == 0)
    def _():
        sum_scr[...] = jnp.zeros_like(sum_scr)

    for q in range(0, group, wide):
        result = finished(q, layer, heads, enter, refs, out_gain, out_proj)
        logits = project(head_ref[...], result) + bias
        result = result.astype(f32)
        for u in range(wide):
            feature_scr[pl.ds(q + u, result.shape[0], stride=group), :] = result[:, span(u)]
            logit_scr[pl.ds(q + u, classes, stride=group), :] = logits[:, span(u)]
    features = feature_scr[...].reshape(-1, group, SCAN_BLOCK)
    features_ref[...] = features.astype(bf16)
    logits = logit_scr[...].reshape(-1, group, SCAN_BLOCK)
    labels = labels_ref[...]
    peak = jnp.max(logits, axis=0)
    shifted = jnp.exp(logits - peak[None])
    partition = jnp.sum(shifted, axis=0)
    probability = shifted / partition[None]
    distance_map = distance_ref[...].astype(f32) * (1.0 / dist_unit)
    weighted = probability * distance_map
    expect = jnp.sum(weighted, axis=0)
    hot = labels[None] == lax.broadcasted_iota(jnp.int32, logits.shape, 0)
    chosen = jnp.sum(jnp.where(hot, logits, 0.0), axis=0)
    loss = peak + jnp.log(partition) - chosen + expect
    grad_ref[...] = probability - jnp.where(hot, 1.0, 0.0) + weighted - probability * expect[None]
    sum_scr[...] += jnp.sum(loss, axis=0, keepdims=True)
    loss_ref[...] = jnp.broadcast_to(sum_scr[...], loss_ref.shape)


def whole(shape):
    return pl.BlockSpec(shape, lambda g: (0,) * len(shape))


def blocks(group, *rest):
    return pl.BlockSpec((group,) + rest, lambda g: (g,) + (0,) * len(rest))


def params(size=vmem_bytes):
    return pltpu.CompilerParams(vmem_limit_bytes=size)


def cost(us):
    return pl.CostEstimate(flops=0, bytes_accessed=int(us * 3.5e6), transcendentals=0)


def from_before(value):
    size = lax.axis_size(axes)
    value = jnp.where(lax.axis_index(axes) == size - 1, jnp.zeros_like(value), value)
    return lax.ppermute(value, axes, [(i, (i + 1) % size) for i in range(size)])


def prefix_state(total, state, beside):
    size = lax.axis_size(axes)
    me = lax.axis_index(axes)
    odd = (me & 1).astype(jnp.int32).reshape(1)
    swap = [(i, i ^ 1) for i in range(size)]
    other = lax.ppermute(total, axes, swap)
    chips = size // 2
    groups = [list(range(core, size, 2)) for core in range(2)]
    rows = state // 2 + 8
    smem, vmem = pl.BlockSpec(memory_space=pltpu.SMEM), pl.BlockSpec(memory_space=pltpu.VMEM)
    offer = pl.pallas_call(
        offer_kernel,
        in_specs=[smem, vmem, vmem],
        out_specs=vmem,
        out_shape=jax.ShapeDtypeStruct((chips, rows, LANES), f32),
        compiler_params=params(4 * 1024 * 1024),
        name="offer",
    )(odd, total, other)
    got = lax.all_to_all(offer, axes, 0, 0, tiled=True, axis_index_groups=groups)
    got, beside = lax.optimization_barrier((got, beside))
    ahead = pl.pallas_call(
        join_kernel,
        in_specs=[smem, vmem],
        out_specs=vmem,
        out_shape=jax.ShapeDtypeStruct((state // 2, LANES), f32),
        compiler_params=params(4 * 1024 * 1024),
        name="join",
    )((me // 2).astype(jnp.int32).reshape(1), got)
    return (odd, ahead, lax.ppermute(ahead, axes, swap), other), beside


def offer_kernel(odd_ref, mine_ref, other_ref, out_ref):
    odd = odd_ref[0] != 0
    half = out_ref.shape[1] - 8
    state = 2 * half
    first = jnp.where(odd, other_ref[...], mine_ref[...])
    second = jnp.where(odd, mine_ref[...], other_ref[...])
    pair = jnp.exp(second[state : state + 1]) * first[:state] + second[:state]
    part = jnp.where(odd, pair[half:], pair[:half])
    log = first[state:] + second[state:]
    for chip in range(out_ref.shape[0]):
        out_ref[chip, 0:half, :] = part
        out_ref[chip, half:, :] = log


def join_kernel(count_ref, parts_ref, out_ref):
    half = out_ref.shape[0]

    def step(j, running):
        return jnp.exp(parts_ref[j, half : half + 1, :]) * running + parts_ref[j, 0:half, :]

    out_ref[...] = lax.fori_loop(0, count_ref[0], step, jnp.zeros_like(out_ref))


def tile(count, rows, kind):
    return jax.ShapeDtypeStruct((count, rows, SCAN_BLOCK), kind)


def far_tile(count, rows, kind):
    return pltpu.HBM((count, rows, SCAN_BLOCK), kind)


def tail_spec(tail):
    if tail.ndim == 2:
        return whole(tail.shape)
    last = tail.shape[0] - 1
    return pl.BlockSpec((1,) + tail.shape[1:], lambda g: (last, 0, 0))


def call_states(layer, hidden, tail, weights, group):
    from_volume = tail.ndim == 2
    inner, heads, state = weights["inner"], weights["heads"], weights["state"]
    model = weights["model"]
    count = hidden.shape[1] * hidden.shape[2] // SCAN_BLOCK if from_volume else hidden.shape[0]
    first_rows = inner + state
    names = ("matrices", "rows")
    out_specs = [
        blocks(group, inner, SCAN_BLOCK),
        blocks(group, state, SCAN_BLOCK),
        blocks(group, 16, SCAN_BLOCK),
        blocks(group, state + 8, LANES),
        whole((state + 8, LANES)),
    ]
    out_shape = [
        tile(count, inner, bf16),
        far_tile(count, state, bf16),
        tile(count, 16, f32),
        far_tile(count, state + 8, f32),
        jax.ShapeDtypeStruct((state + 8, LANES), f32),
    ]
    scratch = [pltpu.VMEM((first_rows, (group + 1) * SCAN_BLOCK), f32), pltpu.VMEM((state + 8, LANES), f32)]
    if from_volume:
        out_specs.append(whole((count, model, SCAN_BLOCK)))
        out_shape.append(tile(count, model, bf16))
        per = LANES // hidden.shape[1]
        scratch.append(pltpu.VMEM((model // per, hidden.shape[2], LANES), f32))
        scratch.append(pltpu.VMEM((count * model, LANES), f32))
    return pl.pallas_call(
        functools.partial(state_kernel, layer, heads, from_volume),
        grid=(count // group,),
        in_specs=[whole(hidden.shape) if from_volume else blocks(group, *hidden.shape[1:]), tail_spec(tail)]
        + [whole(weights[name].shape) for name in names],
        out_specs=out_specs,
        out_shape=out_shape,
        scratch_shapes=scratch,
        compiler_params=params(),
        name="states",
    )(hidden, tail, *(weights[name] for name in names))


def call_local(layer, hidden, tail, inner_values, write, dec, weights, group):
    count = hidden.shape[0]
    inner, heads, state = weights["inner"], weights["heads"], weights["state"]
    names = ("matrices", "rows")
    return pl.pallas_call(
        functools.partial(local_kernel, layer, heads),
        grid=(count // group,),
        in_specs=[blocks(group, *hidden.shape[1:]), tail_spec(tail)]
        + [whole(weights[name].shape) for name in names]
        + [blocks(group, inner, SCAN_BLOCK), blocks(group, state, SCAN_BLOCK), blocks(group, 16, SCAN_BLOCK)],
        out_specs=[
            blocks(group, inner, SCAN_BLOCK),
            blocks(group, inner, SCAN_BLOCK),
            blocks(group, state, SCAN_BLOCK),
        ],
        out_shape=[far_tile(count, inner, f32), far_tile(count, inner, f32), far_tile(count, state, bf16)],
        scratch_shapes=[
            pltpu.VMEM((state, (group + 1) * SCAN_BLOCK), f32),
            pltpu.VMEM((group, SCAN_BLOCK, SCAN_BLOCK), f32),
            pltpu.VMEM((group, heads, SCAN_BLOCK, SCAN_BLOCK), bf16),
        ],
        compiler_params=params(),
        name="local",
    )(hidden, tail, *(weights[name] for name in names), inner_values, write, dec)


def finish_specs(group, hidden, weights):
    inner, state = weights["inner"], weights["state"]
    return [
        pl.BlockSpec(memory_space=pltpu.SMEM),
        whole((state // 2, LANES)),
        whole((state // 2, LANES)),
        whole((state + 8, LANES)),
        blocks(group, *hidden.shape[1:]),
        blocks(group, inner, SCAN_BLOCK),
        blocks(group, inner, SCAN_BLOCK),
        blocks(group, state, SCAN_BLOCK),
        blocks(group, 16, SCAN_BLOCK),
        blocks(group, state + 8, LANES),
        whole(weights["matrices"].shape),
        whole(weights["rows"].shape),
    ]


def call_finish(layer, cells, enter, hidden, local, gate, read, dec, states, weights, group):
    count, model, _ = hidden.shape
    cells_x, cells_y = cells
    rows = model + 8
    per = LANES // cells_x
    return pl.pallas_call(
        functools.partial(finish_kernel, layer, weights["heads"], cells_x),
        grid=(count // group,),
        in_specs=finish_specs(group, hidden, weights),
        out_specs=whole((cells_x, rows, cells_y)),
        out_shape=jax.ShapeDtypeStruct((cells_x, rows, cells_y), bf16),
        scratch_shapes=[
            pltpu.VMEM((count * model, LANES), f32),
            pltpu.VMEM((model // per, cells_y, LANES), f32),
            pltpu.VMEM(((cells_x + 1) * rows, LANES), f32),
        ],
        compiler_params=params(63 * 1024 * 1024),
        name="finish",
    )(*enter, hidden, local, gate, read, dec, states, weights["matrices"], weights["rows"])


def call_heads(
    layer, size, enter, hidden, local, gate, read, dec, states, weights, group, head_weight, head_bias, labels, distance
):
    classes, model = head_weight.shape
    count = hidden.shape[0]
    plane = lambda rows: pl.BlockSpec((rows, group, SCAN_BLOCK), lambda g: (0, g, 0))
    return pl.pallas_call(
        functools.partial(head_kernel, layer, weights["heads"]),
        grid=(count // group,),
        in_specs=finish_specs(group, hidden, weights)
        + [
            whole(head_weight.shape),
            whole(head_bias.shape),
            pl.BlockSpec((group, SCAN_BLOCK), lambda g: (g, 0)),
            plane(classes),
        ],
        out_specs=[plane(model), plane(classes), whole((size, SCAN_BLOCK))],
        out_shape=[
            jax.ShapeDtypeStruct((model, count, SCAN_BLOCK), bf16),
            jax.ShapeDtypeStruct((classes, count, SCAN_BLOCK), f32),
            jax.ShapeDtypeStruct((size, SCAN_BLOCK), f32),
        ],
        scratch_shapes=[
            pltpu.VMEM((model * group, SCAN_BLOCK), f32),
            pltpu.VMEM((classes * group, SCAN_BLOCK), f32),
            pltpu.VMEM((1, SCAN_BLOCK), f32),
        ],
        compiler_params=params(63 * 1024 * 1024),
        name="heads",
    )(
        *enter, hidden, local, gate, read, dec, states, weights["matrices"], weights["rows"],
        head_weight, head_bias, labels, distance,
    )


def packed(norm_gain, in_proj, dt_proj, dt_bias, decay_rate, conv_weight, conv_bias, skip_gain, out_gain, out_proj):
    lanes = lambda value, width: jnp.pad(value, ((0, 0),) * (value.ndim - 1) + ((0, width - value.shape[-1]),))
    first = jnp.concatenate([in_proj, dt_proj], axis=1)
    width = -(-(first.shape[1] + 8) // LANES) * LANES
    second = out_proj.shape[2]
    matrices = jnp.concatenate(
        [lanes(jnp.swapaxes(first, 1, 2), width), lanes(out_proj, -(-second // LANES) * LANES)], axis=2
    )
    width = -(-conv_bias.shape[1] // LANES) * LANES
    vectors = [conv_bias, norm_gain, dt_bias, -decay_rate, skip_gain, out_gain]
    rows = [lanes(jnp.swapaxes(conv_weight, 1, 2), width)] + [lanes(v, width)[:, None] for v in vectors]
    count = sum(r.shape[1] for r in rows)
    rows.append(jnp.zeros((rows[0].shape[0], -(-count // 8) * 8 - count, width), f32))
    return matrices, jnp.concatenate(rows, axis=1)


def per_device(
    volume, norm_gain, in_proj, dt_proj, dt_bias, decay_rate, conv_weight, conv_bias, skip_gain, out_gain,
    out_proj, head_weight, head_bias, labels, distance,
):
    size = lax.axis_size(axes)
    model, _, cells_y, cells_x = volume.shape
    classes = head_weight.shape[0]
    inner = out_proj.shape[2]
    heads = decay_rate.shape[1]
    weights = dict(heads=heads, inner=inner, state=(in_proj.shape[1] - 2 * inner) // 2, model=model)
    weights["matrices"], weights["rows"] = packed(
        norm_gain, in_proj, dt_proj, dt_bias, decay_rate, conv_weight, conv_bias, skip_gain, out_gain, out_proj
    )
    state = weights["state"]
    count = cells_y * cells_x // SCAN_BLOCK
    group = min(16, count)

    tail = from_before(jnp.pad(volume[:, 0, cells_y - 1, :], ((0, 0), (SCAN_BLOCK - cells_x, 0))))
    plane = jnp.swapaxes(volume[:, 0], 1, 2)
    inner_values, write, dec, states, total, hidden = call_states(0, plane, tail, weights, group)
    local, gate, read = call_local(0, hidden, tail, inner_values, write, dec, weights, group)
    enter, (local, gate, read) = prefix_state(total, state, (local, gate, read))
    planes = call_finish(0, (cells_x, cells_y), enter, hidden, local, gate, read, dec, states, weights, group)

    hidden = lax.all_to_all(planes, axes, split_axis=0, concat_axis=0, tiled=True)
    count = hidden.shape[0]
    group = min(16, count)
    inner_values, write, dec, states, total = call_states(1, hidden, hidden, weights, group)
    local, gate, read = call_local(1, hidden, hidden, inner_values, write, dec, weights, group)
    enter, (local, gate, read) = prefix_state(total, state, (local, gate, read))
    features, grad, loss = call_heads(
        1, size, enter, hidden, local, gate, read, dec, states, weights, group, head_weight, head_bias[None, :],
        labels.reshape(count, SCAN_BLOCK), distance.reshape(classes, count, SCAN_BLOCK),
    )
    shared = lax.all_to_all(loss, axes, 0, 0, tiled=True)
    voxel_weight = 1.0 + 3.0 * jnp.arange(size, dtype=f32) / (size - 1.0)
    total_loss = jnp.sum(voxel_weight[:, None] * shared) / (2.5 * count * SCAN_BLOCK * size)
    return (
        features.reshape(model, 1, count, SCAN_BLOCK),
        grad.reshape(classes, 1, count, SCAN_BLOCK),
        total_loss,
    )


def solution(mesh):
    plane = P(None, axes, None, None)
    return jax.shard_map(
        per_device,
        mesh=mesh,
        in_specs=(plane,) + (P(),) * 12 + (P(axes, None, None), plane),
        out_specs=(plane, plane, P()),
        check_vma=False,
    )
```

```python
import functools

import jax
import jax.numpy as jnp
from jax import lax
from jax.experimental import pallas as pl
from jax.experimental.pallas import tpu as pltpu
from jax.sharding import PartitionSpec as P

SCAN_BLOCK = 128
LANES = 128

eps = 1e-05
dist_unit = 4096.0
axes = ("row", "col")
f32, bf16 = jnp.float32, jnp.bfloat16
vmem_bytes = 24 * 1024 * 1024
wide = 4


def half_silu(v):
    return v + v * jnp.tanh(v)


def rounded(v):
    return v.astype(bf16).astype(f32)


def normalise(hidden, gain_col):
    values = hidden.astype(f32)
    mean_sq = jnp.mean(values * values, axis=0, keepdims=True)
    return (values * lax.rsqrt(mean_sq + eps) * gain_col).astype(bf16)


def project(weight, normed):
    return jnp.dot(weight, normed, preferred_element_type=f32)


def contract(a, b, dim):
    return lax.dot_general(a, b, (((dim,), (dim,)), ((), ())), preferred_element_type=f32)


def spread(rows, first, count, height):
    return jnp.concatenate(
        [jnp.broadcast_to(rows[first + h : first + h + 1], (height, rows.shape[1])) for h in range(count)], axis=0
    )


def side_by_side(ref, first, count, rows=None):
    rows = ref.shape[1] if rows is None else rows
    return jnp.concatenate([ref[u][:rows] for u in range(first, first + count)], axis=1)


def span(u, count=1):
    return slice(u * SCAN_BLOCK, (u + count) * SCAN_BLOCK)


def padded(values, rows, lanes):
    if values.shape[1] < lanes:
        values = jnp.concatenate([values, jnp.zeros((values.shape[0], lanes - values.shape[1]), f32)], axis=1)
    if values.shape[0] < rows:
        values = jnp.concatenate([values, jnp.zeros((rows - values.shape[0], lanes), f32)], axis=0)
    return values


def turned(values):
    lanes = -(-values.shape[1] // LANES) * LANES
    return jnp.transpose(padded(values, -(-values.shape[0] // 8) * 8, lanes), (1, 0))


def columns(*rows):
    return turned(jnp.concatenate(rows, axis=0))


def columns_of(layer, rows_ref):
    return jnp.transpose(rows_ref[layer], (1, 0))


def tail_tile(tail_ref, model):
    if tail_ref.ndim == 2:
        return tail_ref[...]
    block = tail_ref[tail_ref.shape[0] - 1].astype(f32)
    rows = block[model:]
    kept = lax.broadcasted_iota(jnp.int32, rows.shape, 0) >= rows.shape[0] - 3
    rows = jnp.where(kept, rows, 0.0)
    tile = jnp.concatenate([jnp.zeros((SCAN_BLOCK - rows.shape[0], LANES), f32), rows], axis=0)
    return jnp.transpose(tile, (1, 0))[:model].astype(bf16)


def pack(running, running_log, heads):
    rows, lanes = running.shape
    width = lanes // (heads + 1)
    inner = heads * width
    kept = rows * heads // (heads + 1)
    high = rows - kept
    logs, blocks = [], []
    for h in range(heads):
        moved = pltpu.roll(running[kept:], inner - h * width, 1)
        log = pltpu.roll(running_log, inner - h * width, 1)
        lane = lax.broadcasted_iota(jnp.int32, moved.shape, 1)
        blocks.append(jnp.where(lane < inner, running[h * high : (h + 1) * high], moved))
        logs.append(jnp.where(lane[:1] < inner, running_log[:1], log[:1]))
    logs.append(jnp.zeros((8 - heads, lanes), f32))
    return jnp.concatenate(blocks + logs, axis=0)


def unpack(packed_state, heads):
    lanes = packed_state.shape[1]
    width = lanes // (heads + 1)
    inner = heads * width
    kept = packed_state.shape[0] - 8
    high = kept // heads
    lane = lax.broadcasted_iota(jnp.int32, (high, lanes), 1)
    last = jnp.zeros((high, lanes), f32)
    for h in range(heads):
        moved = pltpu.roll(packed_state[h * high : (h + 1) * high], (h * width - inner) % lanes, 1)
        last = jnp.where(lane // width == h, moved, last)
    return jnp.concatenate([packed_state[:kept], last], axis=0)


def swap_lanes(parts):
    count = len(parts)
    if count == 1:
        return parts
    width = LANES // count
    place = lax.broadcasted_iota(jnp.int32, parts[0].shape, 1) // width
    result = []
    for b in range(count):
        total = None
        for a, part in enumerate(parts):
            shift = (a - b) * width % LANES
            moved = pltpu.roll(part, shift, 1) if shift else part
            total = moved if total is None else jnp.where(place == a, moved, total)
        result.append(total)
    return result


def to_sequence(volume_ref, hid_ref, turn_ref, tile_ref):
    model, cells_x, cells_y = volume_ref.shape
    count = hid_ref.shape[0]
    per = LANES // cells_x
    for c in range(0, model, per):
        turn_ref[c // per] = jnp.transpose(volume_ref[c : c + per].astype(f32).reshape(LANES, cells_y), (1, 0))
    for c in range(0, model, per):
        parts = [turn_ref[c // per, pl.ds(a, count, stride=per), :] for a in range(per)]
        for j, part in enumerate(swap_lanes(parts)):
            tile_ref[pl.ds(c + j, count, stride=model), :] = part
    for u in range(count):
        hid_ref[u] = tile_ref[u * model : (u + 1) * model, :].astype(bf16)


def to_planes(tile_ref, out_ref, turn_ref, plane_ref, model, cells_x):
    rows = out_ref.shape[1]
    cells_y = out_ref.shape[2]
    per = LANES // cells_x
    count = cells_y // per
    for c in range(0, model, per):
        parts = [tile_ref[pl.ds(c + j, count, stride=model), :] for j in range(per)]
        for a, part in enumerate(swap_lanes(parts)):
            turn_ref[c // per, pl.ds(a, count, stride=per), :] = part
    for c in range(0, model, per):
        turn = jnp.transpose(turn_ref[c // per], (1, 0))
        for j in range(per):
            plane_ref[pl.ds(c + j, cells_x, stride=rows), :] = turn[j * cells_x : (j + 1) * cells_x]
    for x in range(cells_x + 1):
        plane_ref[x * rows + model : (x + 1) * rows, :] = jnp.zeros((rows - model, LANES), f32)
    for y in range(cells_y - 3, cells_y):
        block, a = divmod(y, per)
        turn = jnp.transpose(padded(tile_ref[block * model : (block + 1) * model, :], LANES, LANES), (1, 0))
        at = 2 * rows - cells_y + y
        plane_ref[pl.ds(at, cells_x, stride=rows), :] = turn[a * cells_x : (a + 1) * cells_x]
    for x in range(cells_x):
        out_ref[x] = plane_ref[x * rows : (x + 1) * rows, :].astype(bf16)


def convolve(proj_ref, rows, cols, first, outs):
    group = proj_ref.shape[1] // SCAN_BLOCK - 1
    tap_count = 4
    for r in range(0, rows, 16):
        conv_in = proj_ref[r : r + 16, :]
        half = 0.5 * cols[first + r : first + r + 16, :]
        total = None
        for offset in range(tap_count):
            lag = tap_count - 1 - offset
            shifted = pltpu.roll(conv_in, lag, 1) if lag else conv_in
            term = half[:, offset : offset + 1] * shifted[:, SCAN_BLOCK:]
            total = half[:, tap_count : tap_count + 1] + term if total is None else total + term
        conv_out = half_silu(total).astype(bf16)
        ref, at = next((ref, r - low) for ref, low, high in outs if low <= r < high)
        for u in range(group):
            ref[u, at : at + 16, :] = conv_out[:, span(u)]
    proj_ref[:, span(0)] = proj_ref[:, span(group)]


def state_kernel(
    layer, heads, from_volume, group, hid_ref, tail_ref, matrix_ref, rows_ref, inner_ref, write_ref, dec_ref,
    state_ref, total_ref, *rest
):
    if from_volume:
        volume_ref, hid_ref, proj_ref, carry_ref, turn_ref, tile_ref = (hid_ref,) + rest
        to_sequence(volume_ref, hid_ref, turn_ref, tile_ref)
    else:
        proj_ref, carry_ref = rest
    model = matrix_ref.shape[1]
    inner = inner_ref.shape[1]
    width = inner // heads
    state = write_ref.shape[1]
    rows = inner + state
    weight = jnp.transpose(matrix_ref[layer].astype(f32), (1, 0))
    dt_first = 2 * (inner + state)
    weight = jnp.concatenate([weight[inner : inner + rows], weight[dt_first : dt_first + 8]], axis=0).astype(bf16)
    cols = columns_of(layer, rows_ref)
    gain_col = cols[:model, 5:6]
    head_cols = cols[:8, 6:8]

    carry_ref[...] = jnp.zeros_like(carry_ref)
    proj_ref[:, span(0)] = rounded(project(weight, normalise(tail_tile(tail_ref, model), gain_col))[:rows])
    lane = lax.broadcasted_iota(jnp.int32, (1, LANES), 1)
    alls = (hid_ref, inner_ref, write_ref, dec_ref, state_ref)

    @pl.loop(0, inner_ref.shape[0] // group)
    def _(g):
        hid_ref, inner_ref, write_ref, dec_ref, state_ref = (r.at[pl.ds(g * group, group)] for r in alls)
        dt_raw = []
        for q in range(0, group, wide):
            projected = project(weight, normalise(side_by_side(hid_ref, q, wide, model), gain_col))
            proj_ref[:, span(q + 1, wide)] = rounded(projected[:rows])
            dt_raw.append(projected[rows:])
        step = jnp.concatenate(dt_raw, axis=1) + head_cols[:, 0:1]
        step = jnp.maximum(step, 0.0) + jnp.log1p(jnp.exp(-jnp.abs(step)))
        log_decay = head_cols[:, 1:2] * step
        step = jnp.concatenate([step[:, span(u)] for u in range(group)], axis=0)
        log_decay = jnp.concatenate([log_decay[:, span(u)] for u in range(group)], axis=0)
        high = log_decay.astype(bf16)
        rest = log_decay - high.astype(f32)
        middle = rest.astype(bf16)
        low = (rest - middle.astype(f32)).astype(bf16)
        square = (SCAN_BLOCK, SCAN_BLOCK)
        earlier = lax.broadcasted_iota(jnp.int32, square, 0) <= lax.broadcasted_iota(jnp.int32, square, 1)
        tri = jnp.where(earlier, 1.0, 0.0).astype(bf16)
        cum = project(low, tri) + project(middle, tri) + project(high, tri)
        last = jnp.broadcast_to(cum[:, SCAN_BLOCK - 1 :], cum.shape)
        carry_weight = jnp.exp(last - cum) * step
        for u in range(group):
            dec_ref[u, 0:8, :] = cum[8 * u : 8 * u + 8]
            dec_ref[u, 8:16, :] = step[8 * u : 8 * u + 8]
        convolve(proj_ref, rows, cols, 0, [(inner_ref, 0, inner), (write_ref, inner, rows)])
        decay_rows, block_states = [], []
        for u in range(group):
            row = last[8 * u + heads - 1 : 8 * u + heads]
            for h in range(heads - 2, -1, -1):
                row = jnp.where(lane < (h + 1) * width, last[8 * u + h : 8 * u + h + 1], row)
            decay_rows.append(row)
            scaled = inner_ref[u].astype(f32) * spread(carry_weight, 8 * u, heads, width)
            scaled = jnp.concatenate([scaled.astype(bf16), jnp.zeros((LANES - inner, SCAN_BLOCK), bf16)], axis=0)
            block_states.append(contract(write_ref[u], scaled, 1))
        running = carry_ref[0:state, :]
        running_log = carry_ref[state:, :]
        for u in range(group):
            state_ref[u, 0:state, :] = running
            state_ref[u, state:, :] = running_log
            running = jnp.exp(decay_rows[u]) * running + block_states[u]
            running_log = running_log + decay_rows[u]
        carry_ref[0:state, :] = running
        carry_ref[state:, :] = running_log

    total_ref[...] = pack(carry_ref[0:state, :], carry_ref[state:, :], heads)


def local_kernel(
    layer, heads, first, count, group, hid_ref, tail_ref, matrix_ref, rows_ref, inner_ref, write_ref, dec_ref, *rest
):
    local_ref, gate_ref, read_ref, proj_ref, score_ref, weights_ref = rest[-6:]
    model = matrix_ref.shape[1]
    inner = inner_ref.shape[1]
    width = inner // heads
    state = read_ref.shape[1]
    weight = jnp.transpose(matrix_ref[layer].astype(f32), (1, 0))
    weight = jnp.concatenate([weight[:inner], weight[2 * inner + state : 2 * (inner + state)]], axis=0).astype(bf16)
    cols = columns_of(layer, rows_ref)
    gain_col = cols[:model, 5:6]
    skip_cols = cols[:8, 8:9]

    before = hid_ref[first - 1][:model] if first else tail_tile(tail_ref, model)
    proj_ref[:, span(0)] = rounded(project(weight[inner:], normalise(before, gain_col)))
    source = lax.broadcasted_iota(jnp.int32, (SCAN_BLOCK, SCAN_BLOCK), 0)
    target = lax.broadcasted_iota(jnp.int32, (SCAN_BLOCK, SCAN_BLOCK), 1)
    causal = source <= target
    log2e = 1.4426950408889634
    alls = (hid_ref, inner_ref, write_ref, dec_ref, local_ref, gate_ref, read_ref)

    @pl.loop(0, count // group)
    def _(g):
        hid_ref, inner_ref, write_ref, dec_ref, local_ref, gate_ref, read_ref = (
            r.at[pl.ds(first + g * group, group)] for r in alls
        )
        for q in range(0, group, wide):
            projected = rounded(project(weight, normalise(side_by_side(hid_ref, q, wide, model), gain_col)))
            proj_ref[:, span(q + 1, wide)] = projected[inner:]
            gate = half_silu(0.5 * projected[:inner])
            for u in range(wide):
                gate_ref[q + u] = gate[:, span(u)]
        convolve(proj_ref, state, cols, inner + state, [(read_ref, 0, state)])
        cum = jnp.concatenate([dec_ref[u, 0:8, :] for u in range(group)], axis=0)
        step = jnp.concatenate([dec_ref[u, 8:16, :] for u in range(group)], axis=0)
        source_cols = (cum - jnp.log(step)) * log2e
        if 8 * group < SCAN_BLOCK:
            unused = jnp.zeros((SCAN_BLOCK - 8 * group, SCAN_BLOCK), f32)
            source_cols = jnp.concatenate([source_cols, unused], axis=0)
        source_cols = jnp.transpose(source_cols, (1, 0))
        cum = cum * log2e
        for u in range(group):
            score_ref[u] = contract(write_ref[u], read_ref[u], 0)
        for u in range(group):
            scores = score_ref[u]
            for h in range(heads):
                at = 8 * u + h
                gap = jnp.where(causal, cum[at : at + 1] - source_cols[:, at : at + 1], -jnp.inf)
                weights_ref[u, h] = (scores * jnp.exp2(gap)).astype(bf16)
        for u in range(group):
            for h in range(heads):
                values = inner_ref[u, h * width : (h + 1) * width, :]
                local_ref[u, h * width : (h + 1) * width, :] = (
                    project(values, weights_ref[u, h]) + skip_cols[h : h + 1, 0:1] * values.astype(f32)
                )


def finished(q, layer, heads, enter, refs, out_gain, out_proj):
    hid_ref, local_ref, gate_ref, read_ref, dec_ref, state_ref = refs
    inner = local_ref.shape[1]
    width = inner // heads
    state = read_ref.shape[1]
    inter = []
    for u in range(q, q + wide):
        entering = jnp.exp(state_ref[u, state : state + 1, :]) * enter + state_ref[u, 0:state, :]
        inter.append(contract(entering.astype(bf16), read_ref[u], 0)[:inner])
    decay = jnp.exp(jnp.concatenate([dec_ref[u, 0:8, :] for u in range(q, q + wide)], axis=1))
    scan_out = side_by_side(local_ref, q, wide) + spread(decay, 0, heads, width) * jnp.concatenate(inter, axis=1)
    gated = scan_out * side_by_side(gate_ref, q, wide)
    mean_sq = jnp.mean(gated * gated, axis=0, keepdims=True)
    gated = (gated * lax.rsqrt(mean_sq + eps) * out_gain).astype(bf16)
    hidden = side_by_side(hid_ref, q, wide, out_proj.shape[0]).astype(f32)
    return (hidden + project(out_proj, gated)).astype(bf16)


def finish_kernel(
    layer, heads, cells_x, group, enter_ref, hid_ref, local_ref, gate_ref, read_ref, dec_ref, state_ref, matrix_ref,
    rows_ref, out_ref, tile_ref, turn_ref, plane_ref,
):
    model = matrix_ref.shape[1]
    inner = local_ref.shape[1]
    alls = (hid_ref, local_ref, gate_ref, read_ref, dec_ref, state_ref)
    enter = unpack(enter_ref[...], heads)
    out_gain = columns_of(layer, rows_ref)[:inner, 9:10]
    out_proj = matrix_ref[layer][:, -LANES:][:, :inner]

    @pl.loop(0, hid_ref.shape[0] // group)
    def _(g):
        refs = tuple(r.at[pl.ds(g * group, group)] for r in alls)
        for q in range(0, group, wide):
            result = finished(q, layer, heads, enter, refs, out_gain, out_proj).astype(f32)
            for u in range(wide):
                at = pl.multiple_of((g * group + q + u) * model, 8)
                tile_ref[pl.ds(at, model), :] = result[:, span(u)]

    to_planes(tile_ref, out_ref, turn_ref, plane_ref, model, cells_x)


def head_kernel(
    layer, heads, group, enter_ref, hid_ref, local_ref, gate_ref, read_ref, dec_ref, state_ref, matrix_ref, rows_ref,
    head_ref, bias_ref, labels_ref, distance_ref, features_ref, grad_ref, loss_ref, feature_scr, logit_scr, sum_scr,
):
    classes = distance_ref.shape[0]
    inner = local_ref.shape[1]
    alls = (hid_ref, local_ref, gate_ref, read_ref, dec_ref, state_ref)
    enter = unpack(enter_ref[...], heads)
    out_gain = columns_of(layer, rows_ref)[:inner, 9:10]
    out_proj = matrix_ref[layer][:, -LANES:][:, :inner]
    bias = columns(bias_ref[...])[:classes, 0:1]
    sum_scr[...] = jnp.zeros_like(sum_scr)

    @pl.loop(0, hid_ref.shape[0] // group)
    def _(g):
        refs = tuple(r.at[pl.ds(g * group, group)] for r in alls)
        here = pl.ds(pl.multiple_of(g * group, group), group)
        for q in range(0, group, wide):
            result = finished(q, layer, heads, enter, refs, out_gain, out_proj)
            logits = project(head_ref[...], result) + bias
            result = result.astype(f32)
            for u in range(wide):
                feature_scr[pl.ds(q + u, result.shape[0], stride=group), :] = result[:, span(u)]
                logit_scr[pl.ds(q + u, classes, stride=group), :] = logits[:, span(u)]
        features = feature_scr[...].reshape(-1, group, SCAN_BLOCK)
        features_ref[:, here, :] = features.astype(bf16)
        logits = logit_scr[...].reshape(-1, group, SCAN_BLOCK)
        labels = labels_ref[here, :]
        peak = jnp.max(logits, axis=0)
        shifted = jnp.exp(logits - peak[None])
        partition = jnp.sum(shifted, axis=0)
        probability = shifted / partition[None]
        distance_map = distance_ref[:, here, :].astype(f32) * (1.0 / dist_unit)
        weighted = probability * distance_map
        expect = jnp.sum(weighted, axis=0)
        hot = labels[None] == lax.broadcasted_iota(jnp.int32, logits.shape, 0)
        chosen = jnp.sum(jnp.where(hot, logits, 0.0), axis=0)
        loss = peak + jnp.log(partition) - chosen + expect
        grad_ref[:, here, :] = probability - jnp.where(hot, 1.0, 0.0) + weighted - probability * expect[None]
        sum_scr[...] += jnp.sum(loss, axis=0, keepdims=True)

    loss_ref[...] = jnp.broadcast_to(sum_scr[...], loss_ref.shape)


def params(size=vmem_bytes):
    return pltpu.CompilerParams(vmem_limit_bytes=size)


vmem = pl.BlockSpec(memory_space=pltpu.VMEM)


def from_before(value):
    size = lax.axis_size(axes)
    value = jnp.where(lax.axis_index(axes) == size - 1, jnp.zeros_like(value), value)
    return lax.ppermute(value, axes, [(i, (i + 1) % size) for i in range(size)])


def join_kernel(heads, reach, me_ref, before_ref, *refs):
    members, before_out, total_out = refs[:-2], refs[-2], refs[-1]
    radix = len(members)
    digit = (me_ref[0] & (radix * reach - 1)) // reach
    rows = before_ref.shape[0] - 8
    third = rows // heads

    def combine(earlier, latter):
        log = latter[rows:]
        grow = jnp.exp(log)
        blocks = [
            grow[h : h + 1] * earlier[h * third : (h + 1) * third] + latter[h * third : (h + 1) * third]
            for h in range(heads)
        ]
        return jnp.concatenate(blocks + [earlier[rows:] + log], axis=0)

    values = [ref[...] for ref in members]
    before = before_ref[...]
    ahead, total = None, None
    for place in range(radix):
        value = values[0]
        for k in range(1, radix):
            value = jnp.where(digit ^ k == place, values[k], value)
        total = value if total is None else combine(total, value)
        if place < radix - 1:
            ahead = jnp.where(place < digit, total, jnp.zeros_like(total) if ahead is None else ahead)
    before_out[...] = combine(ahead, before)
    total_out[...] = total


def prefix_state(me, total, held, pieces, heads):
    size = lax.axis_size(axes)
    rounds = [(1, 2)]
    while rounds[-1][0] * rounds[-1][1] < size:
        reach = rounds[-1][0] * rounds[-1][1]
        rounds.append((reach, 4 if 4 * reach <= size else 2))
    before = jnp.zeros_like(total)
    done = None
    for i, (reach, radix) in enumerate(rounds):
        piece = i - (len(rounds) - len(pieces))
        if piece >= 0:
            total, held = lax.optimization_barrier((total, held))
            done = pieces[piece](held, done)
        others = [
            lax.ppermute(total, axes, [(k, k ^ (step * reach | 1)) for k in range(size)]) for step in range(1, radix)
        ]
        if piece >= 0:
            others, done = lax.optimization_barrier((others, done))
        before, total = pl.pallas_call(
            functools.partial(join_kernel, heads, reach),
            in_specs=[pl.BlockSpec(memory_space=pltpu.SMEM)] + [vmem] * (1 + radix),
            out_specs=[vmem] * 2,
            out_shape=[jax.ShapeDtypeStruct(total.shape, f32)] * 2,
            compiler_params=params(2 * 1024 * 1024),
            name="join",
        )(me, before, total, *others)
    return before, done


def tile(count, rows, kind):
    return jax.ShapeDtypeStruct((count, rows, SCAN_BLOCK), kind)


def call_states(layer, hidden, tail, weights):
    from_volume = tail.ndim == 2
    inner, heads, state, model = (weights[k] for k in ("inner", "heads", "state", "model"))
    count = hidden.shape[1] * hidden.shape[2] // SCAN_BLOCK if from_volume else hidden.shape[0]
    group = min(16, count)
    out_shape = [
        tile(count, inner, bf16),
        tile(count, state, bf16),
        tile(count, 16, f32),
        tile(count, state + 8, f32),
        jax.ShapeDtypeStruct((state * inner // LANES + 8, LANES), f32),
    ]
    scratch = [
        pltpu.VMEM((inner + state, (group + 1) * SCAN_BLOCK), f32),
        pltpu.VMEM((state + 8, LANES), f32),
    ]
    if from_volume:
        out_shape.append(tile(count, model, bf16))
        per = LANES // hidden.shape[1]
        scratch.append(pltpu.VMEM((model // per, hidden.shape[2], LANES), f32))
        scratch.append(pltpu.VMEM((count * model, LANES), f32))
    return pl.pallas_call(
        functools.partial(state_kernel, layer, heads, from_volume, group),
        in_specs=[vmem] * 4,
        out_specs=[vmem] * len(out_shape),
        out_shape=out_shape,
        scratch_shapes=scratch,
        compiler_params=params(),
        name="states",
    )(hidden, tail, weights["matrices"], weights["rows"])


def call_local(layer, first, count, held, done, weights):
    hidden, tail, inner_values, write, dec = held
    total = hidden.shape[0]
    inner, heads, state = weights["inner"], weights["heads"], weights["state"]
    group = min(8, count)
    taken = [] if done is None else list(done)
    return pl.pallas_call(
        functools.partial(local_kernel, layer, heads, first, count, group),
        in_specs=[vmem] * (7 + len(taken)),
        out_specs=[vmem] * 3,
        out_shape=[tile(total, inner, f32), tile(total, inner, f32), tile(total, state, bf16)],
        input_output_aliases={7 + i: i for i in range(len(taken))},
        scratch_shapes=[
            pltpu.VMEM((state, (group + 1) * SCAN_BLOCK), f32),
            pltpu.VMEM((group, SCAN_BLOCK, SCAN_BLOCK), f32),
            pltpu.VMEM((group, heads, SCAN_BLOCK, SCAN_BLOCK), bf16),
        ],
        compiler_params=params(),
        name="local",
    )(hidden, tail, weights["matrices"], weights["rows"], inner_values, write, dec, *taken)


def layer_start(layer, me, hidden, tail, weights):
    inner_values, write, dec, states, total, *sequence = call_states(layer, hidden, tail, weights)
    if sequence:
        (hidden,) = sequence
    else:
        tail = hidden
    cut = hidden.shape[0] // 2
    pieces = [
        lambda held, done, first=first: call_local(layer, first, cut, held, done, weights)
        for first in range(0, hidden.shape[0], cut)
    ]
    enter, done = prefix_state(me, total, (hidden, tail, inner_values, write, dec), pieces, weights["heads"])
    return (enter, hidden, *done, dec, states, weights["matrices"], weights["rows"])


def call_finish(cells, parts, weights):
    count, model, _ = parts[1].shape
    model = weights["model"]
    cells_x, cells_y = cells
    rows = model + 8
    per = LANES // cells_x
    return pl.pallas_call(
        functools.partial(finish_kernel, 0, weights["heads"], cells_x, min(16, count)),
        in_specs=[vmem] * len(parts),
        out_specs=vmem,
        out_shape=jax.ShapeDtypeStruct((cells_x, rows, cells_y), bf16),
        scratch_shapes=[
            pltpu.VMEM((count * model, LANES), f32),
            pltpu.VMEM((model // per, cells_y, LANES), f32),
            pltpu.VMEM(((cells_x + 1) * rows, LANES), f32),
        ],
        compiler_params=params(),
        name="finish",
    )(*parts)


def call_heads(size, parts, weights, head_weight, head_bias, labels, distance):
    classes, model = head_weight.shape
    count = parts[1].shape[0]
    group = min(16, count)
    return pl.pallas_call(
        functools.partial(head_kernel, 1, weights["heads"], group),
        in_specs=[vmem] * (len(parts) + 4),
        out_specs=[vmem] * 3,
        out_shape=[
            jax.ShapeDtypeStruct((model, count, SCAN_BLOCK), bf16),
            jax.ShapeDtypeStruct((classes, count, SCAN_BLOCK), f32),
            jax.ShapeDtypeStruct((size, SCAN_BLOCK), f32),
        ],
        scratch_shapes=[
            pltpu.VMEM((model * group, SCAN_BLOCK), f32),
            pltpu.VMEM((classes * group, SCAN_BLOCK), f32),
            pltpu.VMEM((1, SCAN_BLOCK), f32),
        ],
        compiler_params=params(),
        name="heads",
    )(*parts, head_weight, head_bias, labels, distance)


def packed(norm_gain, in_proj, dt_proj, dt_bias, decay_rate, conv_weight, conv_bias, skip_gain, out_gain, out_proj):
    lanes = lambda value, width: jnp.pad(value, ((0, 0),) * (value.ndim - 1) + ((0, width - value.shape[-1]),))
    first = jnp.concatenate([in_proj, dt_proj], axis=1)
    width = -(-(first.shape[1] + 8) // LANES) * LANES
    second = out_proj.shape[2]
    matrices = jnp.concatenate(
        [lanes(jnp.swapaxes(first, 1, 2), width), lanes(out_proj, -(-second // LANES) * LANES)], axis=2
    )
    width = -(-conv_bias.shape[1] // LANES) * LANES
    vectors = [conv_bias, norm_gain, dt_bias, -decay_rate, skip_gain, out_gain]
    rows = [lanes(jnp.swapaxes(conv_weight, 1, 2), width)] + [lanes(v, width)[:, None] for v in vectors]
    count = sum(r.shape[1] for r in rows)
    rows.append(jnp.zeros((rows[0].shape[0], -(-count // 8) * 8 - count, width), f32))
    return matrices, jnp.concatenate(rows, axis=1)


def per_device(
    volume, norm_gain, in_proj, dt_proj, dt_bias, decay_rate, conv_weight, conv_bias, skip_gain, out_gain,
    out_proj, head_weight, head_bias, labels, distance,
):
    size = lax.axis_size(axes)
    model, _, cells_y, cells_x = volume.shape
    classes = head_weight.shape[0]
    inner = out_proj.shape[2]
    heads = decay_rate.shape[1]
    weights = dict(heads=heads, inner=inner, state=(in_proj.shape[1] - 2 * inner) // 2, model=model)
    weights["matrices"], weights["rows"] = packed(
        norm_gain, in_proj, dt_proj, dt_bias, decay_rate, conv_weight, conv_bias, skip_gain, out_gain, out_proj
    )
    tail = from_before(jnp.pad(volume[:, 0, cells_y - 1, :], ((0, 0), (SCAN_BLOCK - cells_x, 0))))
    tail, me = lax.optimization_barrier((tail, lax.axis_index(axes).astype(jnp.int32).reshape(1)))
    plane = jnp.swapaxes(volume[:, 0], 1, 2)
    parts = layer_start(0, me, plane, tail, weights)
    planes = call_finish((cells_x, cells_y), parts, weights)
    hidden = lax.all_to_all(planes, axes, split_axis=0, concat_axis=0, tiled=True)
    count = hidden.shape[0]
    parts = layer_start(1, me, hidden, hidden, weights)
    features, grad, loss = call_heads(
        size, parts, weights, head_weight, head_bias[None, :], labels.reshape(count, SCAN_BLOCK),
        distance.reshape(classes, count, SCAN_BLOCK),
    )
    shared = lax.all_to_all(loss, axes, 0, 0, tiled=True)
    voxel_weight = 1.0 + 3.0 * jnp.arange(size, dtype=f32) / (size - 1.0)
    total_loss = jnp.sum(voxel_weight[:, None] * shared) / (2.5 * count * SCAN_BLOCK * size)
    return (
        features.reshape(model, 1, count, SCAN_BLOCK),
        grad.reshape(classes, 1, count, SCAN_BLOCK),
        total_loss,
    )


def solution(mesh):
    plane = P(None, axes, None, None)
    return jax.shard_map(
        per_device,
        mesh=mesh,
        in_specs=(plane,) + (P(),) * 12 + (P(axes, None, None), plane),
        out_specs=(plane, plane, P()),
        check_vma=False,
    )
```

```python
import functools

import jax
import jax.numpy as jnp
from jax import lax
from jax.experimental import pallas as pl
from jax.experimental.pallas import tpu as pltpu
from jax.sharding import PartitionSpec as P

SCAN_BLOCK = 128
LANES = 128

eps = 1e-05
dist_unit = 4096.0
axes = ("row", "col")
f32, bf16 = jnp.float32, jnp.bfloat16
vmem_bytes = 24 * 1024 * 1024
wide = 4
tap_count = 4


def half_silu(v):
    return v + v * jnp.tanh(v)


def rounded(v):
    return v.astype(bf16).astype(f32)


def normalise(hidden, gain_col):
    values = hidden.astype(f32)
    mean_sq = jnp.mean(values * values, axis=0, keepdims=True)
    return (values * lax.rsqrt(mean_sq + eps) * gain_col).astype(bf16)


def project(weight, normed):
    return jnp.dot(weight, normed, preferred_element_type=f32)


def contract(a, b, dim):
    return lax.dot_general(a, b, (((dim,), (dim,)), ((), ())), preferred_element_type=f32)


def spread(rows, first, count, height):
    return jnp.concatenate(
        [jnp.broadcast_to(rows[first + h : first + h + 1], (height, rows.shape[1])) for h in range(count)], axis=0
    )


def side_by_side(ref, first, count, rows=None):
    rows = ref.shape[1] if rows is None else rows
    return jnp.concatenate([ref[u][:rows] for u in range(first, first + count)], axis=1)


def span(u, count=1):
    return slice(u * SCAN_BLOCK, (u + count) * SCAN_BLOCK)


def padded(values, rows, lanes):
    if values.shape[1] < lanes:
        values = jnp.concatenate([values, jnp.zeros((values.shape[0], lanes - values.shape[1]), f32)], axis=1)
    if values.shape[0] < rows:
        values = jnp.concatenate([values, jnp.zeros((rows - values.shape[0], lanes), f32)], axis=0)
    return values


def turned(values):
    lanes = -(-values.shape[1] // LANES) * LANES
    return jnp.transpose(padded(values, -(-values.shape[0] // 8) * 8, lanes), (1, 0))


def columns(*rows):
    return turned(jnp.concatenate(rows, axis=0))


def repeat(steps, body):
    if steps <= 2:
        for g in range(steps):
            body(g)
    else:
        pl.loop(0, steps)(body)


def tail_tile(tail_ref, model):
    if tail_ref.ndim == 2:
        return tail_ref[...]
    block = tail_ref[tail_ref.shape[0] - 1].astype(f32)
    rows = block[model:]
    kept = lax.broadcasted_iota(jnp.int32, rows.shape, 0) >= rows.shape[0] - 3
    rows = jnp.where(kept, rows, 0.0)
    tile = jnp.concatenate([jnp.zeros((SCAN_BLOCK - rows.shape[0], LANES), f32), rows], axis=0)
    return jnp.transpose(tile, (1, 0))[:model].astype(bf16)


def pack(running, running_log, heads):
    rows, lanes = running.shape
    width = lanes // (heads + 1)
    inner = heads * width
    kept = rows * heads // (heads + 1)
    high = rows - kept
    logs, blocks = [], []
    for h in range(heads):
        moved = pltpu.roll(running[kept:], inner - h * width, 1)
        log = pltpu.roll(running_log, inner - h * width, 1)
        lane = lax.broadcasted_iota(jnp.int32, moved.shape, 1)
        blocks.append(jnp.where(lane < inner, running[h * high : (h + 1) * high], moved))
        logs.append(jnp.where(lane[:1] < inner, running_log[:1], log[:1]))
    logs.append(jnp.zeros((8 - heads, lanes), f32))
    return jnp.concatenate(blocks + logs, axis=0)


def unpack(packed_state, heads):
    lanes = packed_state.shape[1]
    width = lanes // (heads + 1)
    inner = heads * width
    kept = packed_state.shape[0] - 8
    high = kept // heads
    lane = lax.broadcasted_iota(jnp.int32, (high, lanes), 1)
    last = jnp.zeros((high, lanes), f32)
    for h in range(heads):
        moved = pltpu.roll(packed_state[h * high : (h + 1) * high], (h * width - inner) % lanes, 1)
        last = jnp.where(lane // width == h, moved, last)
    return jnp.concatenate([packed_state[:kept], last], axis=0)


def swap_lanes(parts):
    parts = list(parts)
    width = LANES // len(parts)
    place = lax.broadcasted_iota(jnp.int32, parts[0].shape, 1) // width
    bit = 1
    while bit < len(parts):
        for a in range(len(parts)):
            if not a & bit:
                low, high = parts[a], parts[a | bit]
                upper = (place & bit) != 0
                parts[a] = jnp.where(upper, pltpu.roll(high, bit * width, 1), low)
                parts[a | bit] = jnp.where(upper, high, pltpu.roll(low, LANES - bit * width, 1))
        bit *= 2
    return parts


def to_sequence(volume_ref, hid_ref, turn_ref, tile_ref):
    model, cells_x, cells_y = volume_ref.shape
    count = hid_ref.shape[0]
    per = LANES // cells_x
    for c in range(0, model, per):
        turn_ref[c // per] = jnp.transpose(volume_ref[c : c + per].astype(f32).reshape(LANES, cells_y), (1, 0))
    for c in range(0, model, per):
        parts = [turn_ref[c // per, pl.ds(a, count, stride=per), :] for a in range(per)]
        for j, part in enumerate(swap_lanes(parts)):
            tile_ref[pl.ds(c + j, count, stride=model), :] = part
    for u in range(count):
        hid_ref[u] = tile_ref[u * model : (u + 1) * model, :].astype(bf16)


def to_planes(tile_ref, out_ref, turn_ref, plane_ref, model, cells_x):
    rows = out_ref.shape[1]
    cells_y = out_ref.shape[2]
    per = LANES // cells_x
    count = cells_y // per
    for c in range(0, model, per):
        parts = [tile_ref[pl.ds(c + j, count, stride=model), :] for j in range(per)]
        for a, part in enumerate(swap_lanes(parts)):
            turn_ref[c // per, pl.ds(a, count, stride=per), :] = part
    for c in range(0, model, per):
        turn = jnp.transpose(turn_ref[c // per], (1, 0))
        for j in range(per):
            plane_ref[pl.ds(c + j, cells_x, stride=rows), :] = turn[j * cells_x : (j + 1) * cells_x]
    for x in range(cells_x + 1):
        plane_ref[x * rows + model : (x + 1) * rows, :] = jnp.zeros((rows - model, LANES), f32)
    for y in range(cells_y - 3, cells_y):
        block, a = divmod(y, per)
        turn = jnp.transpose(padded(tile_ref[block * model : (block + 1) * model, :], LANES, LANES), (1, 0))
        at = 2 * rows - cells_y + y
        plane_ref[pl.ds(at, cells_x, stride=rows), :] = turn[a * cells_x : (a + 1) * cells_x]
    for x in range(cells_x):
        out_ref[x] = plane_ref[x * rows : (x + 1) * rows, :].astype(bf16)


def convolve(proj_ref, rows, cols, first, outs):
    group = proj_ref.shape[1] // SCAN_BLOCK - 1
    lags = range(1, tap_count)
    lane = lax.broadcasted_iota(jnp.int32, (16, SCAN_BLOCK), 1)
    for r in range(0, rows, 16):
        half = [
            jnp.broadcast_to(cols[first + r : first + r + 16, k : k + 1], (16, SCAN_BLOCK)) for k in range(tap_count + 1)
        ]
        ref, at = next((ref, r - low) for ref, low, high in outs if low <= r < high)
        before = proj_ref[r : r + 16, span(0)]
        before = [pltpu.roll(before, lag, 1) for lag in lags]
        for u in range(group):
            conv_in = proj_ref[r : r + 16, span(u + 1)]
            now = [pltpu.roll(conv_in, lag, 1) for lag in lags]
            total = half[tap_count]
            for lag in reversed(lags):
                shifted = jnp.where(lane < lag, before[lag - 1], now[lag - 1])
                total = total + half[tap_count - 1 - lag] * shifted
            total = total + half[tap_count - 1] * conv_in
            ref[u, at : at + 16, :] = half_silu(total).astype(bf16)
            before = now
    proj_ref[:, span(0)] = proj_ref[:, span(group)]


def sequence_kernel(size, me_ref, volume_ref, hid_ref, tail_ref, turn_ref, tile_ref):
    to_sequence(volume_ref, hid_ref, turn_ref, tile_ref)
    last = hid_ref[hid_ref.shape[0] - 1]
    tail_ref[...] = jnp.where(me_ref[0] == size - 1, jnp.zeros_like(last), last)


def weights_kernel(
    in_ref, dt_ref, taps_ref, conv_bias_ref, gain_ref, dt_bias_ref, rate_ref, skip_ref, out_gain_ref, weight_ref, cols_ref
):
    model = in_ref.shape[1]
    lanes = cols_ref.shape[1]
    for layer in range(in_ref.shape[0]):
        here = slice(layer, layer + 1)
        weight = turned(in_ref[layer].astype(f32))[: in_ref.shape[2]]
        steps = [dt_ref[h, here, :].astype(f32) for h in range(dt_ref.shape[0])]
        unused = jnp.zeros((weight_ref.shape[1] - weight.shape[0] - len(steps), model), f32)
        weight_ref[layer] = jnp.concatenate([weight] + steps + [unused], axis=0).astype(bf16)
        rows = [0.5 * taps_ref[layer], 0.5 * conv_bias_ref[here, :], gain_ref[here, :], dt_bias_ref[here, :]]
        rows += [-rate_ref[here, :], skip_ref[here, :], out_gain_ref[here, :]]
        rows = [padded(r, r.shape[0], lanes) for r in rows]
        count = sum(r.shape[0] for r in rows)
        rows.append(jnp.zeros((cols_ref.shape[2] - count, lanes), f32))
        cols_ref[layer] = jnp.transpose(jnp.concatenate(rows, axis=0), (1, 0))


def state_kernel(
    layer, heads, group, hid_ref, tail_ref, weight_ref, cols_ref, inner_ref, write_ref, dec_ref, state_ref, total_ref,
    proj_ref, carry_ref,
):
    model = weight_ref.shape[2]
    inner = inner_ref.shape[1]
    width = inner // heads
    state = write_ref.shape[1]
    rows = inner + state
    dt_first = 2 * rows
    weight = jnp.concatenate([weight_ref[layer, inner : inner + rows], weight_ref[layer, dt_first : dt_first + 16]], axis=0)
    cols = cols_ref[layer]
    gain_col = cols[:model, 5:6]
    head_cols = cols[:8, 6:8]
    carry_ref[...] = jnp.zeros_like(carry_ref)
    proj_ref[:, span(0)] = rounded(project(weight, normalise(tail_tile(tail_ref, model), gain_col))[:rows])
    lane = lax.broadcasted_iota(jnp.int32, (1, LANES), 1)
    alls = (hid_ref, inner_ref, write_ref, dec_ref, state_ref)

    def step_group(g):
        hid_ref, inner_ref, write_ref, dec_ref, state_ref = (r.at[pl.ds(g * group, group)] for r in alls)
        dt_raw = []
        for q in range(0, group, wide):
            projected = project(weight, normalise(side_by_side(hid_ref, q, wide, model), gain_col))
            proj_ref[:, span(q + 1, wide)] = rounded(projected[:rows])
            dt_raw.append(projected[rows : rows + 8])
        step = jnp.concatenate(dt_raw, axis=1) + head_cols[:, 0:1]
        step = jnp.maximum(step, 0.0) + jnp.log1p(jnp.exp(-jnp.abs(step)))
        log_decay = head_cols[:, 1:2] * step
        step = jnp.concatenate([step[:, span(u)] for u in range(group)], axis=0)
        log_decay = jnp.concatenate([log_decay[:, span(u)] for u in range(group)], axis=0)
        high = log_decay.astype(bf16)
        rest = log_decay - high.astype(f32)
        middle = rest.astype(bf16)
        low = (rest - middle.astype(f32)).astype(bf16)
        square = (SCAN_BLOCK, SCAN_BLOCK)
        earlier = lax.broadcasted_iota(jnp.int32, square, 0) <= lax.broadcasted_iota(jnp.int32, square, 1)
        tri = jnp.where(earlier, 1.0, 0.0).astype(bf16)
        cum = project(low, tri) + project(middle, tri) + project(high, tri)
        last = jnp.broadcast_to(cum[:, SCAN_BLOCK - 1 :], cum.shape)
        carry_weight = jnp.exp(last - cum) * step
        for u in range(group):
            dec_ref[u, 0:8, :] = cum[8 * u : 8 * u + 8]
            dec_ref[u, 8:16, :] = step[8 * u : 8 * u + 8]
        convolve(proj_ref, rows, cols, 0, [(inner_ref, 0, inner), (write_ref, inner, rows)])
        decay_rows, block_states = [], []
        for u in range(group):
            row = last[8 * u + heads - 1 : 8 * u + heads]
            for h in range(heads - 2, -1, -1):
                row = jnp.where(lane < (h + 1) * width, last[8 * u + h : 8 * u + h + 1], row)
            decay_rows.append(row)
            scaled = inner_ref[u].astype(f32) * spread(carry_weight, 8 * u, heads, width)
            scaled = jnp.concatenate([scaled.astype(bf16), jnp.zeros((LANES - inner, SCAN_BLOCK), bf16)], axis=0)
            block_states.append(contract(write_ref[u], scaled, 1))
        running = carry_ref[0:state, :]
        running_log = carry_ref[state:, :]
        for u in range(group):
            state_ref[u, 0:state, :] = running
            state_ref[u, state:, :] = running_log
            running = jnp.exp(decay_rows[u]) * running + block_states[u]
            running_log = running_log + decay_rows[u]
        carry_ref[0:state, :] = running
        carry_ref[state:, :] = running_log

    repeat(inner_ref.shape[0] // group, step_group)
    total_ref[...] = pack(carry_ref[0:state, :], carry_ref[state:, :], heads)


def local_kernel(
    layer, heads, first, count, group, hid_ref, tail_ref, weight_ref, cols_ref, inner_ref, write_ref, dec_ref, *rest
):
    local_ref, gate_ref, read_ref, proj_ref, score_ref, weights_ref = rest[-6:]
    model = weight_ref.shape[2]
    inner = inner_ref.shape[1]
    width = inner // heads
    state = read_ref.shape[1]
    read_first = 2 * inner + state
    weight = jnp.concatenate([weight_ref[layer, :inner], weight_ref[layer, read_first : read_first + state]], axis=0)
    cols = cols_ref[layer]
    gain_col = cols[:model, 5:6]
    skip_cols = cols[:8, 8:9]
    before = hid_ref[first - 1][:model] if first else tail_tile(tail_ref, model)
    proj_ref[:, span(0)] = rounded(project(weight[inner:], normalise(before, gain_col)))
    source = lax.broadcasted_iota(jnp.int32, (SCAN_BLOCK, SCAN_BLOCK), 0)
    target = lax.broadcasted_iota(jnp.int32, (SCAN_BLOCK, SCAN_BLOCK), 1)
    causal = source <= target
    log2e = 1.4426950408889634
    alls = (hid_ref, inner_ref, write_ref, dec_ref, local_ref, gate_ref, read_ref)

    def step_group(g):
        hid_ref, inner_ref, write_ref, dec_ref, local_ref, gate_ref, read_ref = (
            r.at[pl.ds(first + g * group, group)] for r in alls
        )
        for q in range(0, group, wide):
            projected = rounded(project(weight, normalise(side_by_side(hid_ref, q, wide, model), gain_col)))
            proj_ref[:, span(q + 1, wide)] = projected[inner:]
            gate = half_silu(0.5 * projected[:inner])
            for u in range(wide):
                gate_ref[q + u] = gate[:, span(u)]
        convolve(proj_ref, state, cols, inner + state, [(read_ref, 0, state)])
        cum = jnp.concatenate([dec_ref[u, 0:8, :] for u in range(group)], axis=0)
        step = jnp.concatenate([dec_ref[u, 8:16, :] for u in range(group)], axis=0)
        source_cols = (cum - jnp.log(step)) * log2e
        if 8 * group < SCAN_BLOCK:
            unused = jnp.zeros((SCAN_BLOCK - 8 * group, SCAN_BLOCK), f32)
            source_cols = jnp.concatenate([source_cols, unused], axis=0)
        source_cols = jnp.transpose(source_cols, (1, 0))
        cum = cum * log2e
        for u in range(group):
            score_ref[u] = contract(write_ref[u], read_ref[u], 0)
        for u in range(group):
            scores = score_ref[u]
            for h in range(heads):
                at = 8 * u + h
                gap = jnp.where(causal, cum[at : at + 1] - source_cols[:, at : at + 1], -jnp.inf)
                weights_ref[u, h] = (scores * jnp.exp2(gap)).astype(bf16)
        for u in range(group):
            for h in range(heads):
                values = inner_ref[u, h * width : (h + 1) * width, :]
                local_ref[u, h * width : (h + 1) * width, :] = (
                    project(values, weights_ref[u, h]) + skip_cols[h : h + 1, 0:1] * values.astype(f32)
                )

    repeat(count // group, step_group)


def finish_group(heads, enter, refs, out_gain, out_proj, gated_ref, square_ref, take):
    hid_ref, local_ref, gate_ref, read_ref, dec_ref, state_ref = refs
    group, inner, _ = local_ref.shape
    width = inner // heads
    state = read_ref.shape[1]
    for u in range(group):
        entering = jnp.exp(state_ref[u, state : state + 1, :]) * enter + state_ref[u, 0:state, :]
        inter = contract(entering.astype(bf16), read_ref[u], 0)[:inner]
        decay = jnp.exp(dec_ref[u, 0:8, :])
        gated = (local_ref[u] + spread(decay, 0, heads, width) * inter) * gate_ref[u]
        gated_ref[u] = gated
        square_ref[u] = jnp.sum((gated * gated).reshape(inner // 8, 8, SCAN_BLOCK), axis=0)
    for u in range(group):
        mean_sq = jnp.sum(square_ref[u], axis=0, keepdims=True) * (1.0 / inner)
        square_ref[u, 0:1, :] = lax.rsqrt(mean_sq + eps)
    for q in range(0, group, wide):
        scale = jnp.concatenate([square_ref[u, 0:1, :] for u in range(q, q + wide)], axis=1)
        gated = (side_by_side(gated_ref, q, wide) * scale * out_gain).astype(bf16)
        hidden = side_by_side(hid_ref, q, wide, out_proj.shape[0]).astype(f32)
        result = (hidden + project(out_proj, gated)).astype(bf16)
        for u in range(wide):
            take(q + u, result[:, span(u)])


def finish_kernel(
    layer, heads, cells_x, group, enter_ref, hid_ref, local_ref, gate_ref, read_ref, dec_ref, state_ref, cols_ref,
    out_proj_ref, out_ref, tile_ref, turn_ref, plane_ref, gated_ref, square_ref,
):
    model = out_proj_ref.shape[1]
    inner = local_ref.shape[1]
    alls = (hid_ref, local_ref, gate_ref, read_ref, dec_ref, state_ref)
    enter = unpack(enter_ref[...], heads)
    out_gain = cols_ref[layer, :inner, 9:10]

    def step_group(g):
        def take(u, result):
            at = (g * group + u) * model
            at = at if isinstance(at, int) else pl.multiple_of(at, 8)
            tile_ref[pl.ds(at, model), :] = result.astype(f32)

        refs = tuple(r.at[pl.ds(g * group, group)] for r in alls)
        finish_group(heads, enter, refs, out_gain, out_proj_ref[layer], gated_ref, square_ref, take)

    repeat(hid_ref.shape[0] // group, step_group)
    to_planes(tile_ref, out_ref, turn_ref, plane_ref, model, cells_x)


def softmax_parts(logits_ref, labels_ref, distance_ref, here):
    classes = logits_ref.shape[0]
    logits = logits_ref[:, here, :]
    peak = jnp.max(logits, axis=0)
    shifted = jnp.exp(logits - peak[None])
    partition = jnp.sum(shifted, axis=0)
    probability = shifted / partition[None]
    weighted = probability * (distance_ref[:, here, :].astype(f32) * (1.0 / dist_unit))
    expect = jnp.sum(weighted, axis=0)
    hot = labels_ref[here, :][None] == lax.broadcasted_iota(jnp.int32, logits.shape, 0)
    return logits, peak, partition, probability, weighted, expect, hot


def tiles_of(count, body):
    if count <= 32:
        for z in range(0, count, 8):
            body(pl.ds(z, 8))
    else:
        pl.loop(0, count // 8)(lambda z: body(pl.ds(pl.multiple_of(z * 8, 8), 8)))


def head_kernel(
    layer, heads, group, enter_ref, hid_ref, local_ref, gate_ref, read_ref, dec_ref, state_ref, cols_ref, out_proj_ref,
    head_ref, bias_ref, labels_ref, distance_ref, after_ref, logits_ref, loss_ref, gated_ref, square_ref, logit_scr,
    sum_scr,
):
    count = hid_ref.shape[0]
    classes = distance_ref.shape[0]
    inner = local_ref.shape[1]
    alls = (hid_ref, local_ref, gate_ref, read_ref, dec_ref, state_ref)
    enter = unpack(enter_ref[...], heads)
    out_gain = cols_ref[layer, :inner, 9:10]
    bias = columns(bias_ref[...])[:classes, 0:1]

    def step_group(g):
        def take(u, result):
            after_ref[g * group + u] = result
            logit_scr[pl.ds(u, classes, stride=group), :] = project(head_ref[...], result) + bias

        refs = tuple(r.at[pl.ds(g * group, group)] for r in alls)
        finish_group(heads, enter, refs, out_gain, out_proj_ref[layer], gated_ref, square_ref, take)
        at = g * group if isinstance(g, int) else pl.multiple_of(g * group, group)
        logits_ref[:, pl.ds(at, group), :] = logit_scr[...].reshape(classes, group, SCAN_BLOCK)

    repeat(count // group, step_group)
    sum_scr[...] = jnp.zeros_like(sum_scr)

    def losses(here):
        logits, peak, partition, _, _, expect, hot = softmax_parts(logits_ref, labels_ref, distance_ref, here)
        chosen = jnp.sum(jnp.where(hot, logits, 0.0), axis=0)
        sum_scr[...] += peak + jnp.log(partition) - chosen + expect

    tiles_of(count, losses)
    loss_ref[...] = jnp.broadcast_to(jnp.sum(sum_scr[...], axis=0, keepdims=True), loss_ref.shape)


def gradient_kernel(after_ref, logits_ref, labels_ref, distance_ref, features_ref, grad_ref, feature_scr):
    count, model, _ = after_ref.shape
    for u in range(count):
        feature_scr[pl.ds(u, model, stride=count), :] = after_ref[u].astype(f32)
    features_ref[...] = feature_scr[...].reshape(model, count, SCAN_BLOCK).astype(bf16)

    def gradients(here):
        _, _, _, probability, weighted, expect, hot = softmax_parts(logits_ref, labels_ref, distance_ref, here)
        grad_ref[:, here, :] = probability - jnp.where(hot, 1.0, 0.0) + weighted - probability * expect[None]

    tiles_of(count, gradients)


def params(size=vmem_bytes):
    return pltpu.CompilerParams(vmem_limit_bytes=size)


def cost(us):
    return pl.CostEstimate(flops=int(us * 1e9), bytes_accessed=int(us * 3.5e6), transcendentals=0)


vmem = pl.BlockSpec(memory_space=pltpu.VMEM)


def join_kernel(heads, reach, radix, me_ref, before_ref, *refs):
    members, outs = refs[:radix], refs[radix:]
    digit = (me_ref[0] & (radix * reach - 1)) // reach
    rows = before_ref.shape[0] - 8
    third = rows // heads

    def combine(earlier, latter):
        log = latter[rows:]
        grow = jnp.exp(log)
        blocks = [
            grow[h : h + 1] * earlier[h * third : (h + 1) * third] + latter[h * third : (h + 1) * third]
            for h in range(heads)
        ]
        return jnp.concatenate(blocks + [earlier[rows:] + log], axis=0)

    values = [ref[...] for ref in members]
    before = before_ref[...]
    ahead, total = None, None
    for place in range(radix if len(outs) > 1 else radix - 1):
        value = values[0]
        for k in range(1, radix):
            value = jnp.where(digit ^ k == place, values[k], value)
        total = value if total is None else combine(total, value)
        if place < radix - 1:
            ahead = jnp.where(place < digit, total, jnp.zeros_like(total) if ahead is None else ahead)
    outs[0][...] = combine(ahead, before)
    if len(outs) > 1:
        outs[1][...] = total


def prefix_state(me, total, held, pieces, heads):
    size = lax.axis_size(axes)
    rounds = [(1, 2)]
    while rounds[-1][0] * rounds[-1][1] < size:
        reach = rounds[-1][0] * rounds[-1][1]
        rounds.append((reach, 4 if 4 * reach <= size else 2))
    before = jnp.zeros_like(total)
    done = None
    for i, (reach, radix) in enumerate(rounds):
        piece = i - (len(rounds) - len(pieces))
        if piece >= 0:
            total, held = lax.optimization_barrier((total, held))
            done = pieces[piece](held, done)
        others = [
            lax.ppermute(total, axes, [(k, k ^ (step * reach | 1)) for k in range(size)]) for step in range(1, radix)
        ]
        if piece >= 0:
            others, done = lax.optimization_barrier((others, done))
        outs = 2 if reach * radix < size else 1
        before, *total = pl.pallas_call(
            functools.partial(join_kernel, heads, reach, radix),
            in_specs=[pl.BlockSpec(memory_space=pltpu.SMEM)] + [vmem] * (1 + radix),
            out_specs=[vmem] * outs,
            out_shape=[jax.ShapeDtypeStruct(before.shape, f32)] * outs,
            compiler_params=params(2 * 1024 * 1024),
            name="join",
        )(me, before, total, *others)
        total = total[0] if total else None
    return before, done


def tile(count, rows, kind):
    return jax.ShapeDtypeStruct((count, rows, SCAN_BLOCK), kind)


def call_sequence(me, size, volume):
    model, cells_x, cells_y = volume.shape
    count = cells_x * cells_y // SCAN_BLOCK
    return pl.pallas_call(
        functools.partial(sequence_kernel, size),
        in_specs=[pl.BlockSpec(memory_space=pltpu.SMEM), vmem],
        out_specs=[vmem] * 2,
        out_shape=[tile(count, model, bf16), jax.ShapeDtypeStruct((model, SCAN_BLOCK), bf16)],
        scratch_shapes=[
            pltpu.VMEM((model * cells_x // LANES, cells_y, LANES), f32),
            pltpu.VMEM((count * model, LANES), f32),
        ],
        compiler_params=params(),
        cost_estimate=cost(8),
        name="sequence",
    )(me, volume)


def call_weights(norm_gain, in_proj, dt_proj, dt_bias, decay_rate, conv_weight, conv_bias, skip_gain, out_gain):
    layers, projected, model = in_proj.shape
    return pl.pallas_call(
        weights_kernel,
        in_specs=[vmem] * 9,
        out_specs=[vmem] * 2,
        out_shape=[
            jax.ShapeDtypeStruct((layers, projected + 16, model), bf16),
            jax.ShapeDtypeStruct((layers, -(-conv_bias.shape[1] // LANES) * LANES, 16), f32),
        ],
        compiler_params=params(4 * 1024 * 1024),
        name="weights",
    )(
        jnp.swapaxes(in_proj, 1, 2), jnp.swapaxes(dt_proj, 0, 1), jnp.swapaxes(conv_weight, 1, 2), conv_bias, norm_gain,
        dt_bias, decay_rate, skip_gain, out_gain,
    )


def call_states(layer, hidden, tail, weights):
    inner, heads, state = (weights[k] for k in ("inner", "heads", "state"))
    count = hidden.shape[0]
    group = min(32, count)
    return pl.pallas_call(
        functools.partial(state_kernel, layer, heads, group),
        in_specs=[vmem] * 4,
        out_specs=[vmem] * 5,
        out_shape=[
            tile(count, inner, bf16),
            tile(count, state, bf16),
            tile(count, 16, f32),
            tile(count, state + 8, f32),
            jax.ShapeDtypeStruct((state * inner // LANES + 8, LANES), f32),
        ],
        scratch_shapes=[
            pltpu.VMEM((inner + state, (group + 1) * SCAN_BLOCK), f32),
            pltpu.VMEM((state + 8, LANES), f32),
        ],
        compiler_params=params(),
        name="states",
    )(hidden, tail, weights["rows"], weights["cols"])


def call_local(layer, first, count, held, done, weights):
    hidden, tail, inner_values, write, dec = held
    total = hidden.shape[0]
    inner, heads, state = weights["inner"], weights["heads"], weights["state"]
    group = min(16, count)
    taken = [] if done is None else list(done)
    return pl.pallas_call(
        functools.partial(local_kernel, layer, heads, first, count, group),
        in_specs=[vmem] * (7 + len(taken)),
        out_specs=[vmem] * 3,
        out_shape=[tile(total, inner, f32), tile(total, inner, f32), tile(total, state, bf16)],
        input_output_aliases={7 + i: i for i in range(len(taken))},
        scratch_shapes=[
            pltpu.VMEM((state, (group + 1) * SCAN_BLOCK), f32),
            pltpu.VMEM((group, SCAN_BLOCK, SCAN_BLOCK), f32),
            pltpu.VMEM((group, heads, SCAN_BLOCK, SCAN_BLOCK), bf16),
        ],
        compiler_params=params(),
        name="local",
    )(hidden, tail, weights["rows"], weights["cols"], inner_values, write, dec, *taken)


def layer_start(layer, me, hidden, tail, weights):
    inner_values, write, dec, states, total = call_states(layer, hidden, tail, weights)
    cut = hidden.shape[0] // 2
    pieces = [
        lambda held, done, first=first: call_local(layer, first, cut, held, done, weights)
        for first in range(0, hidden.shape[0], cut)
    ]
    enter, done = prefix_state(me, total, (hidden, tail, inner_values, write, dec), pieces, weights["heads"])
    return (enter, hidden, *done, dec, states, weights["cols"], weights["out_proj"])


def finish_scratch(group, weights):
    return [pltpu.VMEM((group, weights["inner"], SCAN_BLOCK), f32), pltpu.VMEM((group, 8, SCAN_BLOCK), f32)]


def call_finish(cells, parts, weights):
    count, model, _ = parts[1].shape
    model = weights["model"]
    cells_x, cells_y = cells
    rows = model + 8
    per = LANES // cells_x
    return pl.pallas_call(
        functools.partial(finish_kernel, 0, weights["heads"], cells_x, min(32, count)),
        in_specs=[vmem] * len(parts),
        out_specs=vmem,
        out_shape=jax.ShapeDtypeStruct((cells_x, rows, cells_y), bf16),
        scratch_shapes=[
            pltpu.VMEM((count * model, LANES), f32),
            pltpu.VMEM((model // per, cells_y, LANES), f32),
            pltpu.VMEM(((cells_x + 1) * rows, LANES), f32),
        ]
        + finish_scratch(min(32, count), weights),
        compiler_params=params(),
        name="finish",
    )(*parts)


def call_heads(size, parts, weights, head_weight, head_bias, labels, distance):
    classes, model = head_weight.shape
    count = parts[1].shape[0]
    group = min(32, count)
    return pl.pallas_call(
        functools.partial(head_kernel, 1, weights["heads"], group),
        in_specs=[vmem] * (len(parts) + 4),
        out_specs=[vmem] * 3,
        out_shape=[
            tile(count, model, bf16),
            jax.ShapeDtypeStruct((classes, count, SCAN_BLOCK), f32),
            jax.ShapeDtypeStruct((size, SCAN_BLOCK), f32),
        ],
        scratch_shapes=finish_scratch(group, weights)
        + [pltpu.VMEM((classes * group, SCAN_BLOCK), f32), pltpu.VMEM((8, SCAN_BLOCK), f32)],
        compiler_params=params(),
        name="heads",
    )(*parts, head_weight, head_bias, labels, distance)


def call_gradient(after, logits, labels, distance):
    count, model, _ = after.shape
    return pl.pallas_call(
        gradient_kernel,
        in_specs=[vmem] * 4,
        out_specs=[vmem] * 2,
        out_shape=[
            jax.ShapeDtypeStruct((model, count, SCAN_BLOCK), bf16),
            jax.ShapeDtypeStruct(logits.shape, f32),
        ],
        scratch_shapes=[pltpu.VMEM((model * count, SCAN_BLOCK), f32)],
        compiler_params=params(),
        cost_estimate=cost(4),
        name="gradient",
    )(after, logits, labels, distance)


def per_device(
    volume, norm_gain, in_proj, dt_proj, dt_bias, decay_rate, conv_weight, conv_bias, skip_gain, out_gain,
    out_proj, head_weight, head_bias, labels, distance,
):
    size = lax.axis_size(axes)
    model, _, cells_y, cells_x = volume.shape
    classes = head_weight.shape[0]
    inner = out_proj.shape[2]
    heads = decay_rate.shape[1]
    weights = dict(heads=heads, inner=inner, state=(in_proj.shape[1] - 2 * inner) // 2, model=model)
    me = lax.axis_index(axes).astype(jnp.int32).reshape(1)
    hidden, tail = call_sequence(me, size, jnp.swapaxes(volume[:, 0], 1, 2))
    weights["rows"], weights["cols"] = call_weights(
        norm_gain, in_proj, dt_proj, dt_bias, decay_rate, conv_weight, conv_bias, skip_gain, out_gain
    )
    weights["out_proj"] = out_proj
    tail = lax.ppermute(tail, axes, [(i, (i + 1) % size) for i in range(size)])
    parts = layer_start(0, me, hidden, tail, weights)
    planes = call_finish((cells_x, cells_y), parts, weights)
    hidden = lax.all_to_all(planes, axes, split_axis=0, concat_axis=0, tiled=True)
    count = hidden.shape[0]
    parts = layer_start(1, me, hidden, hidden, weights)
    labels, distance = labels.reshape(count, SCAN_BLOCK), distance.reshape(classes, count, SCAN_BLOCK)
    after, logits, loss = call_heads(size, parts, weights, head_weight, head_bias[None, :], labels, distance)
    shared = lax.all_to_all(loss, axes, 0, 0, tiled=True)
    features, grad = call_gradient(after, logits, labels, distance)
    shared, features, grad = lax.optimization_barrier((shared, features, grad))
    voxel_weight = 1.0 + 3.0 * jnp.arange(size, dtype=f32) / (size - 1.0)
    total_loss = jnp.sum(voxel_weight[:, None] * shared) / (2.5 * count * SCAN_BLOCK * size)
    return (
        features.reshape(model, 1, count, SCAN_BLOCK),
        grad.reshape(classes, 1, count, SCAN_BLOCK),
        total_loss,
    )


def solution(mesh):
    plane = P(None, axes, None, None)
    return jax.shard_map(
        per_device,
        mesh=mesh,
        in_specs=(plane,) + (P(),) * 12 + (P(axes, None, None), plane),
        out_specs=(plane, plane, P()),
        check_vma=False,
    )
```

```python
import functools

import jax
import jax.numpy as jnp
from jax import lax
from jax.experimental import pallas as pl
from jax.experimental.pallas import tpu as pltpu
from jax.sharding import PartitionSpec as P

SCAN_BLOCK = 128
LANES = 128

eps = 1e-05
dist_unit = 4096.0
axes = ("row", "col")
f32, bf16 = jnp.float32, jnp.bfloat16
vmem_bytes = 24 * 1024 * 1024
wide = 4
tap_count = 4


def half_silu(v):
    return v + v * jnp.tanh(v)


def rounded(v):
    return v.astype(bf16).astype(f32)


def normalise(hidden, gain_col):
    values = hidden.astype(f32)
    mean_sq = jnp.mean(values * values, axis=0, keepdims=True)
    return (values * lax.rsqrt(mean_sq + eps) * gain_col).astype(bf16)


def project(weight, normed):
    return jnp.dot(weight, normed, preferred_element_type=f32)


def contract(a, b, dim):
    return lax.dot_general(a, b, (((dim,), (dim,)), ((), ())), preferred_element_type=f32)


def spread(rows, first, count, height):
    return jnp.concatenate(
        [jnp.broadcast_to(rows[first + h : first + h + 1], (height, rows.shape[1])) for h in range(count)], axis=0
    )


def side_by_side(ref, first, count, rows=None):
    rows = ref.shape[1] if rows is None else rows
    return jnp.concatenate([ref[u][:rows] for u in range(first, first + count)], axis=1)


def span(u, count=1):
    return slice(u * SCAN_BLOCK, (u + count) * SCAN_BLOCK)


def padded(values, rows, lanes):
    if values.shape[1] < lanes:
        values = jnp.concatenate([values, jnp.zeros((values.shape[0], lanes - values.shape[1]), f32)], axis=1)
    if values.shape[0] < rows:
        values = jnp.concatenate([values, jnp.zeros((rows - values.shape[0], lanes), f32)], axis=0)
    return values


def turned(values):
    lanes = -(-values.shape[1] // LANES) * LANES
    return jnp.transpose(padded(values, -(-values.shape[0] // 8) * 8, lanes), (1, 0))


def columns(*rows):
    return turned(jnp.concatenate(rows, axis=0))


def repeat(steps, body):
    if steps <= 2:
        for g in range(steps):
            body(g)
    else:
        pl.loop(0, steps)(body)


def tail_tile(tail_ref, model):
    if tail_ref.ndim == 2:
        return tail_ref[...]
    block = tail_ref[tail_ref.shape[0] - 1].astype(f32)
    rows = block[model:]
    kept = lax.broadcasted_iota(jnp.int32, rows.shape, 0) >= rows.shape[0] - 3
    rows = jnp.where(kept, rows, 0.0)
    tile = jnp.concatenate([jnp.zeros((SCAN_BLOCK - rows.shape[0], LANES), f32), rows], axis=0)
    return jnp.transpose(tile, (1, 0))[:model].astype(bf16)


def pack(running, running_log, heads):
    rows, lanes = running.shape
    width = lanes // (heads + 1)
    inner = heads * width
    kept = rows * heads // (heads + 1)
    high = rows - kept
    logs, blocks = [], []
    for h in range(heads):
        moved = pltpu.roll(running[kept:], inner - h * width, 1)
        log = pltpu.roll(running_log, inner - h * width, 1)
        lane = lax.broadcasted_iota(jnp.int32, moved.shape, 1)
        blocks.append(jnp.where(lane < inner, running[h * high : (h + 1) * high], moved))
        logs.append(jnp.where(lane[:1] < inner, running_log[:1], log[:1]))
    logs.append(jnp.zeros((8 - heads, lanes), f32))
    return jnp.concatenate(blocks + logs, axis=0)


def unpack(packed_state, heads):
    lanes = packed_state.shape[1]
    width = lanes // (heads + 1)
    inner = heads * width
    kept = packed_state.shape[0] - 8
    high = kept // heads
    lane = lax.broadcasted_iota(jnp.int32, (high, lanes), 1)
    last = jnp.zeros((high, lanes), f32)
    for h in range(heads):
        moved = pltpu.roll(packed_state[h * high : (h + 1) * high], (h * width - inner) % lanes, 1)
        last = jnp.where(lane // width == h, moved, last)
    return jnp.concatenate([packed_state[:kept], last], axis=0)


def swap_lanes(parts):
    parts = list(parts)
    width = LANES // len(parts)
    place = lax.broadcasted_iota(jnp.int32, parts[0].shape, 1) // width
    bit = 1
    while bit < len(parts):
        for a in range(len(parts)):
            if not a & bit:
                low, high = parts[a], parts[a | bit]
                upper = (place & bit) != 0
                parts[a] = jnp.where(upper, pltpu.roll(high, bit * width, 1), low)
                parts[a | bit] = jnp.where(upper, high, pltpu.roll(low, LANES - bit * width, 1))
        bit *= 2
    return parts


def to_sequence(volume_ref, hid_ref, turn_ref, tile_ref):
    model, cells_x, cells_y = volume_ref.shape
    count = hid_ref.shape[0]
    per = LANES // cells_x
    for c in range(0, model, per):
        turn_ref[c // per] = jnp.transpose(volume_ref[c : c + per].astype(f32).reshape(LANES, cells_y), (1, 0))
    for c in range(0, model, per):
        parts = [turn_ref[c // per, pl.ds(a, count, stride=per), :] for a in range(per)]
        for j, part in enumerate(swap_lanes(parts)):
            tile_ref[pl.ds(c + j, count, stride=model), :] = part
    for u in range(count):
        hid_ref[u] = tile_ref[u * model : (u + 1) * model, :].astype(bf16)


def to_planes(tile_ref, out_ref, turn_ref, plane_ref, model, cells_x):
    rows = out_ref.shape[1]
    cells_y = out_ref.shape[2]
    per = LANES // cells_x
    count = cells_y // per
    for c in range(0, model, per):
        parts = [tile_ref[pl.ds(c + j, count, stride=model), :] for j in range(per)]
        for a, part in enumerate(swap_lanes(parts)):
            turn_ref[c // per, pl.ds(a, count, stride=per), :] = part
    for c in range(0, model, per):
        turn = jnp.transpose(turn_ref[c // per], (1, 0))
        for j in range(per):
            plane_ref[pl.ds(c + j, cells_x, stride=rows), :] = turn[j * cells_x : (j + 1) * cells_x]
    for x in range(cells_x + 1):
        plane_ref[x * rows + model : (x + 1) * rows, :] = jnp.zeros((rows - model, LANES), f32)
    for y in range(cells_y - 3, cells_y):
        block, a = divmod(y, per)
        turn = jnp.transpose(padded(tile_ref[block * model : (block + 1) * model, :], LANES, LANES), (1, 0))
        at = 2 * rows - cells_y + y
        plane_ref[pl.ds(at, cells_x, stride=rows), :] = turn[a * cells_x : (a + 1) * cells_x]
    for x in range(cells_x):
        out_ref[x] = plane_ref[x * rows : (x + 1) * rows, :].astype(bf16)


def convolve(proj_ref, shift_ref, rows, cols, first, outs, rotated=0):
    group = proj_ref.shape[1] // SCAN_BLOCK - 1
    batch = min(16, group)
    high = 32
    lags = range(1, tap_count)
    lane = lax.broadcasted_iota(jnp.int32, (high, SCAN_BLOCK), 1)
    for r in range(0, rows, high):
        half = [
            jnp.broadcast_to(cols[first + r : first + r + high, k : k + 1], (high, SCAN_BLOCK))
            for k in range(tap_count + 1)
        ]
        ref, at = next((ref, r - low) for ref, low, end in outs if low <= r < end)
        if r >= rows - rotated:
            before = proj_ref[r : r + high, span(0)].astype(f32)
            before = [pltpu.roll(before, lag, 1) for lag in lags]
            for u in range(group):
                conv_in = proj_ref[r : r + high, span(u + 1)].astype(f32)
                now = [pltpu.roll(conv_in, lag, 1) for lag in lags]
                total = half[tap_count]
                for lag in reversed(lags):
                    shifted = jnp.where(lane < lag, before[lag - 1], now[lag - 1])
                    total = total + half[tap_count - 1 - lag] * shifted
                total = total + half[tap_count - 1] * conv_in
                ref[u, at : at + high, :] = half_silu(total).astype(bf16)
                before = now
            continue
        for b in range(0, group, batch):
            pairs = [proj_ref[r : r + high, span(u, 2)] for u in range(b, b + batch)]
            moved = project(jnp.concatenate(pairs, axis=0), shift_ref[...])
            for i in range(batch):
                total = half[tap_count]
                for lag in reversed(range(tap_count)):
                    total = total + half[tap_count - 1 - lag] * moved[i * high : (i + 1) * high, span(lag)]
                ref[b + i, at : at + high, :] = half_silu(total).astype(bf16)
    proj_ref[:, span(0)] = proj_ref[:, span(group)]


def tail_kernel(size, me_ref, volume_ref, tail_ref, part_ref):
    model, cells_x, cells_y = volume_ref.shape
    per = LANES // cells_x
    last = jnp.where(lax.broadcasted_iota(jnp.int32, (16, cells_y), 1) == cells_y - 1, 1.0, 0.0).astype(bf16)
    row = contract(last, volume_ref[...].reshape(model * cells_x, cells_y), 1)[0:1]
    rows = jnp.concatenate([row[:, c * LANES : (c + 1) * LANES] for c in range(model // per)], axis=0)
    for j in range(per):
        shift = LANES - (j + 1) * cells_x
        part_ref[pl.ds(j, model // per, stride=per), :] = pltpu.roll(rows, shift, 1) if shift else rows
    tail = part_ref[...]
    tail_ref[...] = jnp.where(me_ref[0] == size - 1, jnp.zeros_like(tail), tail).astype(bf16)


def sequence_kernel(volume_ref, hid_ref, turn_ref, tile_ref):
    to_sequence(volume_ref, hid_ref, turn_ref, tile_ref)


def weights_kernel(
    in_ref, dt_ref, taps_ref, conv_bias_ref, gain_ref, dt_bias_ref, rate_ref, skip_ref, out_gain_ref, weight_ref, cols_ref,
    shift_ref,
):
    model = in_ref.shape[1]
    source = lax.broadcasted_iota(jnp.int32, shift_ref.shape, 0) - SCAN_BLOCK
    target = lax.broadcasted_iota(jnp.int32, shift_ref.shape, 1)
    shift_ref[...] = jnp.where(source == target % SCAN_BLOCK - target // SCAN_BLOCK, 1.0, 0.0).astype(bf16)
    lanes = cols_ref.shape[1]
    for layer in range(in_ref.shape[0]):
        here = slice(layer, layer + 1)
        weight = turned(in_ref[layer].astype(f32))[: in_ref.shape[2]]
        steps = [dt_ref[h, here, :].astype(f32) for h in range(dt_ref.shape[0])]
        unused = jnp.zeros((weight_ref.shape[1] - weight.shape[0] - len(steps), model), f32)
        weight_ref[layer] = jnp.concatenate([weight] + steps + [unused], axis=0).astype(bf16)
        rows = [0.5 * taps_ref[layer], 0.5 * conv_bias_ref[here, :], gain_ref[here, :], dt_bias_ref[here, :]]
        rows += [-rate_ref[here, :], skip_ref[here, :], out_gain_ref[here, :]]
        rows = [padded(r, r.shape[0], lanes) for r in rows]
        count = sum(r.shape[0] for r in rows)
        rows.append(jnp.zeros((cols_ref.shape[2] - count, lanes), f32))
        cols_ref[layer] = jnp.transpose(jnp.concatenate(rows, axis=0), (1, 0))


def state_kernel(
    layer, heads, group, hid_ref, tail_ref, weight_ref, cols_ref, shift_ref, inner_ref, write_ref, dec_ref, state_ref,
    total_ref, proj_ref, carry_ref,
):
    model = weight_ref.shape[2]
    inner = inner_ref.shape[1]
    width = inner // heads
    state = write_ref.shape[1]
    rows = inner + state
    dt_first = 2 * rows
    weight = jnp.concatenate([weight_ref[layer, inner : inner + rows], weight_ref[layer, dt_first : dt_first + 16]], axis=0)
    cols = cols_ref[layer]
    gain_col = cols[:model, 5:6]
    head_cols = cols[:8, 6:8]
    carry_ref[...] = jnp.zeros_like(carry_ref)
    proj_ref[:, span(0)] = project(weight, normalise(tail_tile(tail_ref, model), gain_col))[:rows].astype(bf16)
    lane = lax.broadcasted_iota(jnp.int32, (1, LANES), 1)
    alls = (hid_ref, inner_ref, write_ref, dec_ref, state_ref)

    def step_group(g):
        hid_ref, inner_ref, write_ref, dec_ref, state_ref = (r.at[pl.ds(g * group, group)] for r in alls)
        dt_raw = []
        for q in range(0, group, wide):
            projected = project(weight, normalise(side_by_side(hid_ref, q, wide, model), gain_col))
            proj_ref[:, span(q + 1, wide)] = projected[:rows].astype(bf16)
            dt_raw.append(projected[rows : rows + 8])
        step = jnp.concatenate(dt_raw, axis=1) + head_cols[:, 0:1]
        step = jnp.maximum(step, 0.0) + jnp.log1p(jnp.exp(-jnp.abs(step)))
        log_decay = head_cols[:, 1:2] * step
        step = jnp.concatenate([step[:, span(u)] for u in range(group)], axis=0)
        log_decay = jnp.concatenate([log_decay[:, span(u)] for u in range(group)], axis=0)
        high = log_decay.astype(bf16)
        rest = log_decay - high.astype(f32)
        middle = rest.astype(bf16)
        low = (rest - middle.astype(f32)).astype(bf16)
        square = (SCAN_BLOCK, SCAN_BLOCK)
        earlier = lax.broadcasted_iota(jnp.int32, square, 0) <= lax.broadcasted_iota(jnp.int32, square, 1)
        tri = jnp.where(earlier, 1.0, 0.0).astype(bf16)
        cum = project(low, tri) + project(middle, tri) + project(high, tri)
        last = jnp.broadcast_to(cum[:, SCAN_BLOCK - 1 :], cum.shape)
        carry_weight = jnp.exp(last - cum) * step
        for u in range(group):
            dec_ref[u, 0:8, :] = cum[8 * u : 8 * u + 8]
            dec_ref[u, 8:16, :] = step[8 * u : 8 * u + 8]
        convolve(proj_ref, shift_ref, rows, cols, 0, [(inner_ref, 0, inner), (write_ref, inner, rows)], 32)
        decay_rows, block_states = [], []
        for u in range(group):
            row = last[8 * u + heads - 1 : 8 * u + heads]
            for h in range(heads - 2, -1, -1):
                row = jnp.where(lane < (h + 1) * width, last[8 * u + h : 8 * u + h + 1], row)
            decay_rows.append(row)
            scaled = inner_ref[u].astype(f32) * spread(carry_weight, 8 * u, heads, width)
            scaled = jnp.concatenate([scaled.astype(bf16), jnp.zeros((LANES - inner, SCAN_BLOCK), bf16)], axis=0)
            block_states.append(contract(write_ref[u], scaled, 1))
        running = carry_ref[0:state, :]
        running_log = carry_ref[state:, :]
        for u in range(group):
            state_ref[u, 0:state, :] = running
            state_ref[u, state:, :] = running_log
            running = jnp.exp(decay_rows[u]) * running + block_states[u]
            running_log = running_log + decay_rows[u]
        carry_ref[0:state, :] = running
        carry_ref[state:, :] = running_log

    repeat(inner_ref.shape[0] // group, step_group)
    total_ref[...] = pack(carry_ref[0:state, :], carry_ref[state:, :], heads)


def local_kernel(
    layer, heads, first, count, group, hid_ref, tail_ref, weight_ref, cols_ref, shift_ref, inner_ref, write_ref, dec_ref,
    *rest
):
    local_ref, gate_ref, read_ref, proj_ref, score_ref, weights_ref = rest[-6:]
    model = weight_ref.shape[2]
    inner = inner_ref.shape[1]
    width = inner // heads
    state = read_ref.shape[1]
    read_first = 2 * inner + state
    weight = jnp.concatenate([weight_ref[layer, :inner], weight_ref[layer, read_first : read_first + state]], axis=0)
    cols = cols_ref[layer]
    gain_col = cols[:model, 5:6]
    skip_cols = cols[:8, 8:9]
    before = hid_ref[first - 1][:model] if first else tail_tile(tail_ref, model)
    proj_ref[:, span(0)] = project(weight[inner:], normalise(before, gain_col)).astype(bf16)
    source = lax.broadcasted_iota(jnp.int32, (SCAN_BLOCK, SCAN_BLOCK), 0)
    target = lax.broadcasted_iota(jnp.int32, (SCAN_BLOCK, SCAN_BLOCK), 1)
    causal = source <= target
    log2e = 1.4426950408889634
    alls = (hid_ref, inner_ref, write_ref, dec_ref, local_ref, gate_ref, read_ref)

    def step_group(g):
        hid_ref, inner_ref, write_ref, dec_ref, local_ref, gate_ref, read_ref = (
            r.at[pl.ds(first + g * group, group)] for r in alls
        )
        for q in range(0, group, wide):
            projected = project(weight, normalise(side_by_side(hid_ref, q, wide, model), gain_col)).astype(bf16)
            proj_ref[:, span(q + 1, wide)] = projected[inner:]
            gate = half_silu(0.5 * projected[:inner].astype(f32))
            for u in range(wide):
                gate_ref[q + u] = gate[:, span(u)]
        convolve(proj_ref, shift_ref, state, cols, inner + state, [(read_ref, 0, state)])
        cum = jnp.concatenate([dec_ref[u, 0:8, :] for u in range(group)], axis=0)
        step = jnp.concatenate([dec_ref[u, 8:16, :] for u in range(group)], axis=0)
        source_cols = (cum - jnp.log(step)) * log2e
        if 8 * group < SCAN_BLOCK:
            unused = jnp.zeros((SCAN_BLOCK - 8 * group, SCAN_BLOCK), f32)
            source_cols = jnp.concatenate([source_cols, unused], axis=0)
        source_cols = jnp.transpose(source_cols, (1, 0))
        cum = cum * log2e
        for u in range(group):
            score_ref[u] = contract(write_ref[u], read_ref[u], 0)
        for u in range(group):
            scores = score_ref[u]
            for h in range(heads):
                at = 8 * u + h
                gap = jnp.where(causal, cum[at : at + 1] - source_cols[:, at : at + 1], -jnp.inf)
                weights_ref[u, h] = (scores * jnp.exp2(gap)).astype(bf16)
        for u in range(group):
            for h in range(heads):
                values = inner_ref[u, h * width : (h + 1) * width, :]
                local_ref[u, h * width : (h + 1) * width, :] = (
                    project(values, weights_ref[u, h]) + skip_cols[h : h + 1, 0:1] * values.astype(f32)
                )

    repeat(count // group, step_group)


def finish_group(heads, enter, refs, out_gain, out_proj, gated_ref, square_ref, take):
    hid_ref, local_ref, gate_ref, read_ref, dec_ref, state_ref = refs
    group, inner, _ = local_ref.shape
    width = inner // heads
    state = read_ref.shape[1]
    for u in range(group):
        entering = jnp.exp(state_ref[u, state : state + 1, :]) * enter + state_ref[u, 0:state, :]
        inter = contract(entering.astype(bf16), read_ref[u], 0)[:inner]
        decay = jnp.exp(dec_ref[u, 0:8, :])
        gated = (local_ref[u] + spread(decay, 0, heads, width) * inter) * gate_ref[u]
        gated_ref[u] = gated
        square_ref[u] = jnp.sum((gated * gated).reshape(inner // 8, 8, SCAN_BLOCK), axis=0)
    for u in range(group):
        mean_sq = jnp.sum(square_ref[u], axis=0, keepdims=True) * (1.0 / inner)
        square_ref[u, 0:1, :] = lax.rsqrt(mean_sq + eps)
    for q in range(0, group, wide):
        scale = jnp.concatenate([square_ref[u, 0:1, :] for u in range(q, q + wide)], axis=1)
        gated = (side_by_side(gated_ref, q, wide) * scale * out_gain).astype(bf16)
        hidden = side_by_side(hid_ref, q, wide, out_proj.shape[0]).astype(f32)
        result = (hidden + project(out_proj, gated)).astype(bf16)
        for u in range(wide):
            take(q + u, result[:, span(u)])


def finish_kernel(
    layer, heads, cells_x, group, enter_ref, hid_ref, local_ref, gate_ref, read_ref, dec_ref, state_ref, cols_ref,
    out_proj_ref, out_ref, tile_ref, turn_ref, plane_ref, gated_ref, square_ref,
):
    model = out_proj_ref.shape[1]
    inner = local_ref.shape[1]
    alls = (hid_ref, local_ref, gate_ref, read_ref, dec_ref, state_ref)
    enter = unpack(enter_ref[...], heads)
    out_gain = cols_ref[layer, :inner, 9:10]

    def step_group(g):
        def take(u, result):
            at = (g * group + u) * model
            at = at if isinstance(at, int) else pl.multiple_of(at, 8)
            tile_ref[pl.ds(at, model), :] = result.astype(f32)

        refs = tuple(r.at[pl.ds(g * group, group)] for r in alls)
        finish_group(heads, enter, refs, out_gain, out_proj_ref[layer], gated_ref, square_ref, take)

    repeat(hid_ref.shape[0] // group, step_group)
    to_planes(tile_ref, out_ref, turn_ref, plane_ref, model, cells_x)


def head_kernel(
    layer, heads, group, size, me_ref, enter_ref, hid_ref, local_ref, gate_ref, read_ref, dec_ref, state_ref, cols_ref,
    out_proj_ref, head_ref, bias_ref, labels_ref, distance_ref, features_ref, grad_ref, loss_ref, gated_ref, square_ref,
    after_ref, feature_scr, logit_scr, sum_scr,
):
    count = hid_ref.shape[0]
    classes = distance_ref.shape[0]
    model = out_proj_ref.shape[1]
    inner = local_ref.shape[1]
    alls = (hid_ref, local_ref, gate_ref, read_ref, dec_ref, state_ref)
    enter = unpack(enter_ref[...], heads)
    out_gain = cols_ref[layer, :inner, 9:10]
    bias = columns(bias_ref[...])[:classes, 0:1]
    sum_scr[...] = jnp.zeros_like(sum_scr)

    def step_group(g):
        def take(u, result):
            after_ref[u] = result
            feature_scr[pl.ds(u, model, stride=group), :] = result.astype(f32)

        refs = tuple(r.at[pl.ds(g * group, group)] for r in alls)
        finish_group(heads, enter, refs, out_gain, out_proj_ref[layer], gated_ref, square_ref, take)
        for q in range(0, group, wide):
            logits = project(head_ref[...], side_by_side(after_ref, q, wide)) + bias
            for u in range(wide):
                logit_scr[pl.ds(q + u, classes, stride=group), :] = logits[:, span(u)]
        at = g * group if isinstance(g, int) else pl.multiple_of(g * group, group)
        features_ref[:, pl.ds(at, group), :] = feature_scr[...].reshape(model, group, SCAN_BLOCK).astype(bf16)
        for z in range(0, group, 8):
            here = pl.ds(at + z, 8)
            logits = jnp.stack([logit_scr[c * group + z : c * group + z + 8, :] for c in range(classes)], axis=0)
            peak = jnp.max(logits, axis=0)
            shifted = jnp.exp(logits - peak[None])
            partition = jnp.sum(shifted, axis=0)
            probability = shifted / partition[None]
            weighted = probability * (distance_ref[:, here, :].astype(f32) * (1.0 / dist_unit))
            expect = jnp.sum(weighted, axis=0)
            hot = labels_ref[here, :][None] == lax.broadcasted_iota(jnp.int32, logits.shape, 0)
            chosen = jnp.sum(jnp.where(hot, logits, 0.0), axis=0)
            grad_ref[:, here, :] = probability - jnp.where(hot, 1.0, 0.0) + weighted - probability * expect[None]
            sum_scr[...] += peak + jnp.log(partition) - chosen + expect

    repeat(count // group, step_group)
    weight = 1.0 + 3.0 * me_ref[0].astype(f32) / (size - 1.0)
    loss_ref[...] = jnp.broadcast_to(jnp.sum(sum_scr[...], axis=0, keepdims=True) * weight, loss_ref.shape)


def params(size=vmem_bytes):
    return pltpu.CompilerParams(vmem_limit_bytes=size)


def cost(us):
    return pl.CostEstimate(flops=int(us * 1e9), bytes_accessed=int(us * 3.5e6), transcendentals=0)


vmem = pl.BlockSpec(memory_space=pltpu.VMEM)


def join_kernel(heads, reach, radix, me_ref, before_ref, *refs):
    members, outs = refs[:radix], refs[radix:]
    digit = (me_ref[0] & (radix * reach - 1)) // reach
    rows = before_ref.shape[0] - 8
    third = rows // heads

    def combine(earlier, latter):
        log = latter[rows:]
        grow = jnp.exp(log)
        blocks = [
            grow[h : h + 1] * earlier[h * third : (h + 1) * third] + latter[h * third : (h + 1) * third]
            for h in range(heads)
        ]
        return jnp.concatenate(blocks + [earlier[rows:] + log], axis=0)

    values = [ref[...] for ref in members]
    before = before_ref[...]
    ahead, total = None, None
    for place in range(radix if len(outs) > 1 else radix - 1):
        value = values[0]
        for k in range(1, radix):
            value = jnp.where(digit ^ k == place, values[k], value)
        total = value if total is None else combine(total, value)
        if place < radix - 1:
            ahead = jnp.where(place < digit, total, jnp.zeros_like(total) if ahead is None else ahead)
    outs[0][...] = combine(ahead, before)
    if len(outs) > 1:
        outs[1][...] = total


def prefix_state(me, total, held, pieces, heads):
    size = lax.axis_size(axes)
    rounds = [(1, 2)]
    while rounds[-1][0] * rounds[-1][1] < size:
        reach = rounds[-1][0] * rounds[-1][1]
        rounds.append((reach, 4 if 4 * reach <= size else 2))
    before = jnp.zeros_like(total)
    done = None
    for i, (reach, radix) in enumerate(rounds):
        piece = i - (len(rounds) - len(pieces))
        if piece >= 0:
            total, held = lax.optimization_barrier((total, held))
            done = pieces[piece](held, done)
        others = [
            lax.ppermute(total, axes, [(k, k ^ (step * reach | 1)) for k in range(size)]) for step in range(1, radix)
        ]
        if piece >= 0:
            others, done = lax.optimization_barrier((others, done))
        outs = 2 if reach * radix < size else 1
        before, *total = pl.pallas_call(
            functools.partial(join_kernel, heads, reach, radix),
            in_specs=[pl.BlockSpec(memory_space=pltpu.SMEM)] + [vmem] * (1 + radix),
            out_specs=[vmem] * outs,
            out_shape=[jax.ShapeDtypeStruct(before.shape, f32)] * outs,
            compiler_params=params(2 * 1024 * 1024),
            name="join",
        )(me, before, total, *others)
        total = total[0] if total else None
    return before, done


def tile(count, rows, kind):
    return jax.ShapeDtypeStruct((count, rows, SCAN_BLOCK), kind)


def call_tail(me, size, volume):
    model = volume.shape[0]
    return pl.pallas_call(
        functools.partial(tail_kernel, size),
        in_specs=[pl.BlockSpec(memory_space=pltpu.SMEM), vmem],
        out_specs=vmem,
        out_shape=jax.ShapeDtypeStruct((model, SCAN_BLOCK), bf16),
        scratch_shapes=[pltpu.VMEM((model, LANES), f32)],
        compiler_params=params(4 * 1024 * 1024),
        cost_estimate=cost(2),
        name="tail",
    )(me, volume)


def call_sequence(volume):
    model, cells_x, cells_y = volume.shape
    count = cells_x * cells_y // SCAN_BLOCK
    return pl.pallas_call(
        sequence_kernel,
        in_specs=[vmem],
        out_specs=vmem,
        out_shape=tile(count, model, bf16),
        scratch_shapes=[
            pltpu.VMEM((model * cells_x // LANES, cells_y, LANES), f32),
            pltpu.VMEM((count * model, LANES), f32),
        ],
        compiler_params=params(),
        cost_estimate=cost(8),
        name="sequence",
    )(volume)


def call_weights(norm_gain, in_proj, dt_proj, dt_bias, decay_rate, conv_weight, conv_bias, skip_gain, out_gain):
    layers, projected, model = in_proj.shape
    return pl.pallas_call(
        weights_kernel,
        in_specs=[vmem] * 9,
        out_specs=[vmem] * 3,
        out_shape=[
            jax.ShapeDtypeStruct((layers, projected + 16, model), bf16),
            jax.ShapeDtypeStruct((layers, -(-conv_bias.shape[1] // LANES) * LANES, 16), f32),
            jax.ShapeDtypeStruct((2 * SCAN_BLOCK, tap_count * SCAN_BLOCK), bf16),
        ],
        compiler_params=params(4 * 1024 * 1024),
        name="weights",
    )(
        jnp.swapaxes(in_proj, 1, 2), jnp.swapaxes(dt_proj, 0, 1), jnp.swapaxes(conv_weight, 1, 2), conv_bias, norm_gain,
        dt_bias, decay_rate, skip_gain, out_gain,
    )


def call_states(layer, hidden, tail, weights):
    inner, heads, state = (weights[k] for k in ("inner", "heads", "state"))
    count = hidden.shape[0]
    group = min(32, count)
    return pl.pallas_call(
        functools.partial(state_kernel, layer, heads, group),
        in_specs=[vmem] * 5,
        out_specs=[vmem] * 5,
        out_shape=[
            tile(count, inner, bf16),
            tile(count, state, bf16),
            tile(count, 16, f32),
            tile(count, state + 8, f32),
            jax.ShapeDtypeStruct((state * inner // LANES + 8, LANES), f32),
        ],
        scratch_shapes=[
            pltpu.VMEM((inner + state, (group + 1) * SCAN_BLOCK), bf16),
            pltpu.VMEM((state + 8, LANES), f32),
        ],
        compiler_params=params(),
        name="states",
    )(hidden, tail, weights["rows"], weights["cols"], weights["shift"])


def call_local(layer, first, count, held, done, weights):
    hidden, tail, inner_values, write, dec = held
    total = hidden.shape[0]
    inner, heads, state = weights["inner"], weights["heads"], weights["state"]
    group = min(16, count)
    taken = [] if done is None else list(done)
    return pl.pallas_call(
        functools.partial(local_kernel, layer, heads, first, count, group),
        in_specs=[vmem] * (8 + len(taken)),
        out_specs=[vmem] * 3,
        out_shape=[tile(total, inner, f32), tile(total, inner, f32), tile(total, state, bf16)],
        input_output_aliases={8 + i: i for i in range(len(taken))},
        scratch_shapes=[
            pltpu.VMEM((state, (group + 1) * SCAN_BLOCK), bf16),
            pltpu.VMEM((group, SCAN_BLOCK, SCAN_BLOCK), f32),
            pltpu.VMEM((group, heads, SCAN_BLOCK, SCAN_BLOCK), bf16),
        ],
        compiler_params=params(),
        name="local",
    )(hidden, tail, weights["rows"], weights["cols"], weights["shift"], inner_values, write, dec, *taken)


def layer_start(layer, me, hidden, tail, weights):
    inner_values, write, dec, states, total = call_states(layer, hidden, tail, weights)
    cut = hidden.shape[0] // 2
    pieces = [
        lambda held, done, first=first: call_local(layer, first, cut, held, done, weights)
        for first in range(0, hidden.shape[0], cut)
    ]
    enter, done = prefix_state(me, total, (hidden, tail, inner_values, write, dec), pieces, weights["heads"])
    return (enter, hidden, *done, dec, states, weights["cols"], weights["out_proj"])


def finish_scratch(group, weights):
    return [pltpu.VMEM((group, weights["inner"], SCAN_BLOCK), f32), pltpu.VMEM((group, 8, SCAN_BLOCK), f32)]


def call_finish(cells, parts, weights):
    count, model, _ = parts[1].shape
    model = weights["model"]
    cells_x, cells_y = cells
    rows = model + 8
    per = LANES // cells_x
    return pl.pallas_call(
        functools.partial(finish_kernel, 0, weights["heads"], cells_x, min(32, count)),
        in_specs=[vmem] * len(parts),
        out_specs=vmem,
        out_shape=jax.ShapeDtypeStruct((cells_x, rows, cells_y), bf16),
        scratch_shapes=[
            pltpu.VMEM((count * model, LANES), f32),
            pltpu.VMEM((model // per, cells_y, LANES), f32),
            pltpu.VMEM(((cells_x + 1) * rows, LANES), f32),
        ]
        + finish_scratch(min(32, count), weights),
        compiler_params=params(),
        name="finish",
    )(*parts)


def call_heads(me, size, parts, weights, head_weight, head_bias, labels, distance):
    classes, model = head_weight.shape
    count = parts[1].shape[0]
    group = min(32, count)
    return pl.pallas_call(
        functools.partial(head_kernel, 1, weights["heads"], group, size),
        in_specs=[pl.BlockSpec(memory_space=pltpu.SMEM)] + [vmem] * (len(parts) + 4),
        out_specs=[vmem] * 3,
        out_shape=[
            jax.ShapeDtypeStruct((model, count, SCAN_BLOCK), bf16),
            jax.ShapeDtypeStruct((classes, count, SCAN_BLOCK), f32),
            jax.ShapeDtypeStruct((size, SCAN_BLOCK), f32),
        ],
        scratch_shapes=finish_scratch(group, weights)
        + [
            pltpu.VMEM((group, model, SCAN_BLOCK), bf16),
            pltpu.VMEM((model * group, SCAN_BLOCK), f32),
            pltpu.VMEM((classes * group, SCAN_BLOCK), f32),
            pltpu.VMEM((8, SCAN_BLOCK), f32),
        ],
        compiler_params=params(),
        name="heads",
    )(me, *parts, head_weight, head_bias, labels, distance)


def per_device(
    volume, norm_gain, in_proj, dt_proj, dt_bias, decay_rate, conv_weight, conv_bias, skip_gain, out_gain,
    out_proj, head_weight, head_bias, labels, distance,
):
    size = lax.axis_size(axes)
    model, _, cells_y, cells_x = volume.shape
    classes = head_weight.shape[0]
    inner = out_proj.shape[2]
    heads = decay_rate.shape[1]
    weights = dict(heads=heads, inner=inner, state=(in_proj.shape[1] - 2 * inner) // 2, model=model)
    me = lax.axis_index(axes).astype(jnp.int32).reshape(1)
    plane = jnp.swapaxes(volume[:, 0], 1, 2)
    tail = call_tail(me, size, plane)
    hidden = call_sequence(plane)
    weights["rows"], weights["cols"], weights["shift"] = call_weights(
        norm_gain, in_proj, dt_proj, dt_bias, decay_rate, conv_weight, conv_bias, skip_gain, out_gain
    )
    weights["out_proj"] = out_proj
    tail = lax.ppermute(tail, axes, [(i, (i + 1) % size) for i in range(size)])
    parts = layer_start(0, me, hidden, tail, weights)
    planes = call_finish((cells_x, cells_y), parts, weights)
    hidden = lax.all_to_all(planes, axes, split_axis=0, concat_axis=0, tiled=True)
    count = hidden.shape[0]
    parts = layer_start(1, me, hidden, hidden, weights)
    labels, distance = labels.reshape(count, SCAN_BLOCK), distance.reshape(classes, count, SCAN_BLOCK)
    features, grad, loss = call_heads(
        me, size, parts, weights, head_weight, head_bias[None, :], labels, distance
    )
    shared = lax.all_to_all(loss, axes, 0, 0, tiled=True)
    total_loss = jnp.sum(shared) / (2.5 * count * SCAN_BLOCK * size)
    return (
        features.reshape(model, 1, count, SCAN_BLOCK),
        grad.reshape(classes, 1, count, SCAN_BLOCK),
        total_loss,
    )


def solution(mesh):
    plane = P(None, axes, None, None)
    return jax.shard_map(
        per_device,
        mesh=mesh,
        in_specs=(plane,) + (P(),) * 12 + (P(axes, None, None), plane),
        out_specs=(plane, plane, P()),
        check_vma=False,
    )
```

```python
import functools

import jax
import jax.numpy as jnp
from jax import lax
from jax.experimental import pallas as pl
from jax.experimental.pallas import tpu as pltpu
from jax.sharding import PartitionSpec as P

SCAN_BLOCK = 128
LANES = 128

eps = 1e-05
dist_unit = 4096.0
axes = ("row", "col")
f32, bf16 = jnp.float32, jnp.bfloat16
vmem_bytes = 24 * 1024 * 1024
wide = 4
tap_count = 4


def half_silu(v):
    return v + v * jnp.tanh(v)


def rounded(v):
    return v.astype(bf16).astype(f32)


def normalise(hidden, gain_col):
    values = hidden.astype(f32)
    mean_sq = jnp.mean(values * values, axis=0, keepdims=True)
    return (values * lax.rsqrt(mean_sq + eps) * gain_col).astype(bf16)


def project(weight, normed):
    return jnp.dot(weight, normed, preferred_element_type=f32)


def contract(a, b, dim):
    return lax.dot_general(a, b, (((dim,), (dim,)), ((), ())), preferred_element_type=f32)


def spread(rows, first, count, height):
    return jnp.concatenate(
        [jnp.broadcast_to(rows[first + h : first + h + 1], (height, rows.shape[1])) for h in range(count)], axis=0
    )


def side_by_side(ref, first, count, rows=None):
    rows = ref.shape[1] if rows is None else rows
    return jnp.concatenate([ref[u][:rows] for u in range(first, first + count)], axis=1)


def span(u, count=1):
    return slice(u * SCAN_BLOCK, (u + count) * SCAN_BLOCK)


def padded(values, rows, lanes):
    if values.shape[1] < lanes:
        values = jnp.concatenate([values, jnp.zeros((values.shape[0], lanes - values.shape[1]), f32)], axis=1)
    if values.shape[0] < rows:
        values = jnp.concatenate([values, jnp.zeros((rows - values.shape[0], lanes), f32)], axis=0)
    return values


def turned(values):
    lanes = -(-values.shape[1] // LANES) * LANES
    return jnp.transpose(padded(values, -(-values.shape[0] // 8) * 8, lanes), (1, 0))


def columns(*rows):
    return turned(jnp.concatenate(rows, axis=0))


def repeat(steps, body):
    if steps <= 2:
        for g in range(steps):
            body(g)
    else:
        pl.loop(0, steps)(body)


def tail_tile(tail_ref, model):
    if tail_ref.ndim == 2:
        return tail_ref[...]
    block = tail_ref[tail_ref.shape[0] - 1].astype(f32)
    rows = block[model:]
    kept = lax.broadcasted_iota(jnp.int32, rows.shape, 0) >= rows.shape[0] - 3
    rows = jnp.where(kept, rows, 0.0)
    tile = jnp.concatenate([jnp.zeros((SCAN_BLOCK - rows.shape[0], LANES), f32), rows], axis=0)
    return jnp.transpose(tile, (1, 0))[:model].astype(bf16)


def pack(running, running_log, heads):
    rows, lanes = running.shape
    width = lanes // (heads + 1)
    inner = heads * width
    kept = rows * heads // (heads + 1)
    high = rows - kept
    logs, blocks = [], []
    for h in range(heads):
        moved = pltpu.roll(running[kept:], inner - h * width, 1)
        log = pltpu.roll(running_log, inner - h * width, 1)
        lane = lax.broadcasted_iota(jnp.int32, moved.shape, 1)
        blocks.append(jnp.where(lane < inner, running[h * high : (h + 1) * high], moved))
        logs.append(jnp.where(lane[:1] < inner, running_log[:1], log[:1]))
    logs.append(jnp.zeros((8 - heads, lanes), f32))
    return jnp.concatenate(blocks + logs, axis=0)


def unpack(packed_state, heads):
    lanes = packed_state.shape[1]
    width = lanes // (heads + 1)
    inner = heads * width
    kept = packed_state.shape[0] - 8
    high = kept // heads
    lane = lax.broadcasted_iota(jnp.int32, (high, lanes), 1)
    last = jnp.zeros((high, lanes), f32)
    for h in range(heads):
        moved = pltpu.roll(packed_state[h * high : (h + 1) * high], (h * width - inner) % lanes, 1)
        last = jnp.where(lane // width == h, moved, last)
    return jnp.concatenate([packed_state[:kept], last], axis=0)


def swap_lanes(parts):
    parts = list(parts)
    width = LANES // len(parts)
    place = lax.broadcasted_iota(jnp.int32, parts[0].shape, 1) // width
    bit = 1
    while bit < len(parts):
        for a in range(len(parts)):
            if not a & bit:
                low, high = parts[a], parts[a | bit]
                upper = (place & bit) != 0
                parts[a] = jnp.where(upper, pltpu.roll(high, bit * width, 1), low)
                parts[a | bit] = jnp.where(upper, high, pltpu.roll(low, LANES - bit * width, 1))
        bit *= 2
    return parts


def to_sequence(volume_ref, hid_ref, turn_ref, tile_ref):
    model, cells_x, cells_y = volume_ref.shape
    count = hid_ref.shape[0]
    per = LANES // cells_x
    for c in range(0, model, per):
        turn_ref[c // per] = jnp.transpose(volume_ref[c : c + per].astype(f32).reshape(LANES, cells_y), (1, 0))
    for c in range(0, model, per):
        parts = [turn_ref[c // per, pl.ds(a, count, stride=per), :] for a in range(per)]
        for j, part in enumerate(swap_lanes(parts)):
            tile_ref[pl.ds(c + j, count, stride=model), :] = part
    for u in range(count):
        hid_ref[u] = tile_ref[u * model : (u + 1) * model, :].astype(bf16)


def to_planes(tile_ref, out_ref, turn_ref, plane_ref, model, cells_x):
    rows = out_ref.shape[1]
    cells_y = out_ref.shape[2]
    per = LANES // cells_x
    count = cells_y // per
    for c in range(0, model, per):
        parts = [tile_ref[pl.ds(c + j, count, stride=model), :] for j in range(per)]
        for a, part in enumerate(swap_lanes(parts)):
            turn_ref[c // per, pl.ds(a, count, stride=per), :] = part
    for c in range(0, model, per):
        turn = jnp.transpose(turn_ref[c // per], (1, 0))
        for j in range(per):
            plane_ref[pl.ds(c + j, cells_x, stride=rows), :] = turn[j * cells_x : (j + 1) * cells_x]
    for x in range(cells_x + 1):
        plane_ref[x * rows + model : (x + 1) * rows, :] = jnp.zeros((rows - model, LANES), f32)
    for y in range(cells_y - 3, cells_y):
        block, a = divmod(y, per)
        turn = jnp.transpose(padded(tile_ref[block * model : (block + 1) * model, :], LANES, LANES), (1, 0))
        at = 2 * rows - cells_y + y
        plane_ref[pl.ds(at, cells_x, stride=rows), :] = turn[a * cells_x : (a + 1) * cells_x]
    for x in range(cells_x):
        out_ref[x] = plane_ref[x * rows : (x + 1) * rows, :].astype(bf16)


def convolve(proj_ref, shift_ref, rows, cols, first, outs, rotated=0):
    group = proj_ref.shape[1] // SCAN_BLOCK - 1
    batch = min(16, group)
    high = 32
    lags = range(1, tap_count)
    lane = lax.broadcasted_iota(jnp.int32, (high, SCAN_BLOCK), 1)
    for r in range(0, rows, high):
        half = [
            jnp.broadcast_to(cols[first + r : first + r + high, k : k + 1], (high, SCAN_BLOCK))
            for k in range(tap_count + 1)
        ]
        ref, at = next((ref, r - low) for ref, low, end in outs if low <= r < end)
        if r >= rows - rotated:
            before = proj_ref[r : r + high, span(0)].astype(f32)
            before = [pltpu.roll(before, lag, 1) for lag in lags]
            for u in range(group):
                conv_in = proj_ref[r : r + high, span(u + 1)].astype(f32)
                now = [pltpu.roll(conv_in, lag, 1) for lag in lags]
                total = half[tap_count]
                for lag in reversed(lags):
                    shifted = jnp.where(lane < lag, before[lag - 1], now[lag - 1])
                    total = total + half[tap_count - 1 - lag] * shifted
                total = total + half[tap_count - 1] * conv_in
                ref[u, at : at + high, :] = half_silu(total).astype(bf16)
                before = now
            continue
        for b in range(0, group, batch):
            pairs = [proj_ref[r : r + high, span(u, 2)] for u in range(b, b + batch)]
            moved = project(jnp.concatenate(pairs, axis=0), shift_ref[...])
            for i in range(batch):
                total = half[tap_count]
                for lag in reversed(range(tap_count)):
                    total = total + half[tap_count - 1 - lag] * moved[i * high : (i + 1) * high, span(lag)]
                ref[b + i, at : at + high, :] = half_silu(total).astype(bf16)
    proj_ref[:, span(0)] = proj_ref[:, span(group)]


def tail_kernel(size, me_ref, volume_ref, tail_ref, part_ref):
    model, cells_x, cells_y = volume_ref.shape
    per = LANES // cells_x
    last = jnp.where(lax.broadcasted_iota(jnp.int32, (16, cells_y), 1) == cells_y - 1, 1.0, 0.0).astype(bf16)
    row = contract(last, volume_ref[...].reshape(model * cells_x, cells_y), 1)[0:1]
    rows = jnp.concatenate([row[:, c * LANES : (c + 1) * LANES] for c in range(model // per)], axis=0)
    for j in range(per):
        shift = LANES - (j + 1) * cells_x
        part_ref[pl.ds(j, model // per, stride=per), :] = pltpu.roll(rows, shift, 1) if shift else rows
    tail = part_ref[0:model, :]
    tail_ref[...] = jnp.where(me_ref[0] == size - 1, jnp.zeros_like(tail), tail).astype(bf16)


def sequence_kernel(volume_ref, hid_ref, turn_ref, tile_ref):
    to_sequence(volume_ref, hid_ref, turn_ref, tile_ref)


def weights_kernel(
    in_ref, dt_ref, taps_ref, conv_bias_ref, gain_ref, dt_bias_ref, rate_ref, skip_ref, out_gain_ref, weight_ref, cols_ref,
    shift_ref,
):
    model = in_ref.shape[1]
    source = lax.broadcasted_iota(jnp.int32, shift_ref.shape, 0) - SCAN_BLOCK
    target = lax.broadcasted_iota(jnp.int32, shift_ref.shape, 1)
    shift_ref[...] = jnp.where(source == target % SCAN_BLOCK - target // SCAN_BLOCK, 1.0, 0.0).astype(bf16)
    lanes = cols_ref.shape[1]
    for layer in range(in_ref.shape[0]):
        here = slice(layer, layer + 1)
        weight = turned(in_ref[layer].astype(f32))[: in_ref.shape[2]]
        steps = [dt_ref[h, here, :].astype(f32) for h in range(dt_ref.shape[0])]
        unused = jnp.zeros((weight_ref.shape[1] - weight.shape[0] - len(steps), model), f32)
        weight_ref[layer] = jnp.concatenate([weight] + steps + [unused], axis=0).astype(bf16)
        rows = [0.5 * taps_ref[layer], 0.5 * conv_bias_ref[here, :], gain_ref[here, :], dt_bias_ref[here, :]]
        rows += [-rate_ref[here, :], skip_ref[here, :], out_gain_ref[here, :]]
        rows = [padded(r, r.shape[0], lanes) for r in rows]
        count = sum(r.shape[0] for r in rows)
        rows.append(jnp.zeros((cols_ref.shape[2] - count, lanes), f32))
        cols_ref[layer] = jnp.transpose(jnp.concatenate(rows, axis=0), (1, 0))


def state_kernel(
    layer, heads, group, hid_ref, tail_ref, weight_ref, cols_ref, shift_ref, inner_ref, write_ref, dec_ref, state_ref,
    total_ref, proj_ref, carry_ref,
):
    model = weight_ref.shape[2]
    inner = inner_ref.shape[1]
    width = inner // heads
    state = write_ref.shape[1]
    rows = inner + state
    dt_first = 2 * rows
    weight = jnp.concatenate([weight_ref[layer, inner : inner + rows], weight_ref[layer, dt_first : dt_first + 16]], axis=0)
    cols = cols_ref[layer]
    gain_col = cols[:model, 5:6]
    head_cols = cols[:8, 6:8]
    carry_ref[...] = jnp.zeros_like(carry_ref)
    proj_ref[:, span(0)] = project(weight, normalise(tail_tile(tail_ref, model), gain_col))[:rows].astype(bf16)
    lane = lax.broadcasted_iota(jnp.int32, (1, LANES), 1)
    alls = (hid_ref, inner_ref, write_ref, dec_ref, state_ref)

    def step_group(g):
        hid_ref, inner_ref, write_ref, dec_ref, state_ref = (r.at[pl.ds(g * group, group)] for r in alls)
        dt_raw = []
        for q in range(0, group, wide):
            projected = project(weight, normalise(side_by_side(hid_ref, q, wide, model), gain_col))
            proj_ref[:, span(q + 1, wide)] = projected[:rows].astype(bf16)
            dt_raw.append(projected[rows : rows + 8])
        step = jnp.concatenate(dt_raw, axis=1) + head_cols[:, 0:1]
        step = jnp.maximum(step, 0.0) + jnp.log1p(jnp.exp(-jnp.abs(step)))
        log_decay = head_cols[:, 1:2] * step
        step = jnp.concatenate([step[:, span(u)] for u in range(group)], axis=0)
        log_decay = jnp.concatenate([log_decay[:, span(u)] for u in range(group)], axis=0)
        high = log_decay.astype(bf16)
        rest = log_decay - high.astype(f32)
        middle = rest.astype(bf16)
        low = (rest - middle.astype(f32)).astype(bf16)
        square = (SCAN_BLOCK, SCAN_BLOCK)
        earlier = lax.broadcasted_iota(jnp.int32, square, 0) <= lax.broadcasted_iota(jnp.int32, square, 1)
        tri = jnp.where(earlier, 1.0, 0.0).astype(bf16)
        cum = project(low, tri) + project(middle, tri) + project(high, tri)
        last = jnp.broadcast_to(cum[:, SCAN_BLOCK - 1 :], cum.shape)
        carry_weight = jnp.exp(last - cum) * step
        for u in range(group):
            dec_ref[u, 0:8, :] = cum[8 * u : 8 * u + 8]
            dec_ref[u, 8:16, :] = step[8 * u : 8 * u + 8]
        convolve(proj_ref, shift_ref, rows, cols, 0, [(inner_ref, 0, inner), (write_ref, inner, rows)], 32)
        decay_rows, block_states = [], []
        for u in range(group):
            row = last[8 * u + heads - 1 : 8 * u + heads]
            for h in range(heads - 2, -1, -1):
                row = jnp.where(lane < (h + 1) * width, last[8 * u + h : 8 * u + h + 1], row)
            decay_rows.append(row)
            scaled = inner_ref[u].astype(f32) * spread(carry_weight, 8 * u, heads, width)
            scaled = jnp.concatenate([scaled.astype(bf16), jnp.zeros((LANES - inner, SCAN_BLOCK), bf16)], axis=0)
            block_states.append(contract(write_ref[u], scaled, 1))
        running = carry_ref[0:state, :]
        running_log = carry_ref[state:, :]
        for u in range(group):
            state_ref[u, 0:state, :] = running
            state_ref[u, state:, :] = running_log
            running = jnp.exp(decay_rows[u]) * running + block_states[u]
            running_log = running_log + decay_rows[u]
        carry_ref[0:state, :] = running
        carry_ref[state:, :] = running_log

    repeat(inner_ref.shape[0] // group, step_group)
    total_ref[...] = pack(carry_ref[0:state, :], carry_ref[state:, :], heads)


def local_kernel(
    layer, heads, first, count, group, hid_ref, tail_ref, weight_ref, cols_ref, shift_ref, inner_ref, write_ref, dec_ref,
    *rest
):
    local_ref, gate_ref, read_ref, proj_ref, score_ref, weights_ref = rest[-6:]
    model = weight_ref.shape[2]
    inner = inner_ref.shape[1]
    width = inner // heads
    state = read_ref.shape[1]
    read_first = 2 * inner + state
    weight = jnp.concatenate([weight_ref[layer, :inner], weight_ref[layer, read_first : read_first + state]], axis=0)
    cols = cols_ref[layer]
    gain_col = cols[:model, 5:6]
    skip_cols = cols[:8, 8:9]
    before = hid_ref[first - 1][:model] if first else tail_tile(tail_ref, model)
    proj_ref[:, span(0)] = project(weight[inner:], normalise(before, gain_col)).astype(bf16)
    source = lax.broadcasted_iota(jnp.int32, (SCAN_BLOCK, SCAN_BLOCK), 0)
    target = lax.broadcasted_iota(jnp.int32, (SCAN_BLOCK, SCAN_BLOCK), 1)
    causal = source <= target
    log2e = 1.4426950408889634
    alls = (hid_ref, inner_ref, write_ref, dec_ref, local_ref, gate_ref, read_ref)

    def step_group(g):
        hid_ref, inner_ref, write_ref, dec_ref, local_ref, gate_ref, read_ref = (
            r.at[pl.ds(first + g * group, group)] for r in alls
        )
        for q in range(0, group, wide):
            projected = project(weight, normalise(side_by_side(hid_ref, q, wide, model), gain_col)).astype(bf16)
            proj_ref[:, span(q + 1, wide)] = projected[inner:]
            gate = half_silu(0.5 * projected[:inner].astype(f32))
            for u in range(wide):
                gate_ref[q + u] = gate[:, span(u)]
        convolve(proj_ref, shift_ref, state, cols, inner + state, [(read_ref, 0, state)])
        cum = jnp.concatenate([dec_ref[u, 0:8, :] for u in range(group)], axis=0)
        step = jnp.concatenate([dec_ref[u, 8:16, :] for u in range(group)], axis=0)
        source_cols = (cum - jnp.log(step)) * log2e
        if 8 * group < SCAN_BLOCK:
            unused = jnp.zeros((SCAN_BLOCK - 8 * group, SCAN_BLOCK), f32)
            source_cols = jnp.concatenate([source_cols, unused], axis=0)
        source_cols = jnp.transpose(source_cols, (1, 0))
        cum = cum * log2e
        for u in range(group):
            score_ref[u] = contract(write_ref[u], read_ref[u], 0)
        for u in range(group):
            scores = score_ref[u]
            for h in range(heads):
                at = 8 * u + h
                gap = jnp.where(causal, cum[at : at + 1] - source_cols[:, at : at + 1], -jnp.inf)
                weights_ref[u, h] = (scores * jnp.exp2(gap)).astype(bf16)
        for u in range(group):
            for h in range(heads):
                values = inner_ref[u, h * width : (h + 1) * width, :]
                local_ref[u, h * width : (h + 1) * width, :] = (
                    project(values, weights_ref[u, h]) + skip_cols[h : h + 1, 0:1] * values.astype(f32)
                )

    repeat(count // group, step_group)


def finish_group(heads, enter, refs, out_gain, out_proj, gated_ref, square_ref, take):
    hid_ref, local_ref, gate_ref, read_ref, dec_ref, state_ref = refs
    group, inner, _ = local_ref.shape
    width = inner // heads
    state = read_ref.shape[1]
    for u in range(group):
        entering = jnp.exp(state_ref[u, state : state + 1, :]) * enter + state_ref[u, 0:state, :]
        inter = contract(entering.astype(bf16), read_ref[u], 0)[:inner]
        decay = jnp.exp(dec_ref[u, 0:8, :])
        gated = (local_ref[u] + spread(decay, 0, heads, width) * inter) * gate_ref[u]
        gated_ref[u] = gated
        square_ref[u] = jnp.sum((gated * gated).reshape(inner // 8, 8, SCAN_BLOCK), axis=0)
    for u in range(group):
        mean_sq = jnp.sum(square_ref[u], axis=0, keepdims=True) * (1.0 / inner)
        square_ref[u, 0:1, :] = lax.rsqrt(mean_sq + eps)
    for q in range(0, group, wide):
        scale = jnp.concatenate([square_ref[u, 0:1, :] for u in range(q, q + wide)], axis=1)
        gated = (side_by_side(gated_ref, q, wide) * scale * out_gain).astype(bf16)
        hidden = side_by_side(hid_ref, q, wide, out_proj.shape[0]).astype(f32)
        result = (hidden + project(out_proj, gated)).astype(bf16)
        for u in range(wide):
            take(q + u, result[:, span(u)])


def finish_kernel(
    layer, heads, cells_x, group, enter_ref, hid_ref, local_ref, gate_ref, read_ref, dec_ref, state_ref, cols_ref,
    out_proj_ref, out_ref, tile_ref, turn_ref, plane_ref, gated_ref, square_ref,
):
    model = out_proj_ref.shape[1]
    inner = local_ref.shape[1]
    alls = (hid_ref, local_ref, gate_ref, read_ref, dec_ref, state_ref)
    enter = unpack(enter_ref[...], heads)
    out_gain = cols_ref[layer, :inner, 9:10]

    def step_group(g):
        def take(u, result):
            at = (g * group + u) * model
            at = at if isinstance(at, int) else pl.multiple_of(at, 8)
            tile_ref[pl.ds(at, model), :] = result.astype(f32)

        refs = tuple(r.at[pl.ds(g * group, group)] for r in alls)
        finish_group(heads, enter, refs, out_gain, out_proj_ref[layer], gated_ref, square_ref, take)

    repeat(hid_ref.shape[0] // group, step_group)
    to_planes(tile_ref, out_ref, turn_ref, plane_ref, model, cells_x)


def head_kernel(
    layer, heads, group, size, me_ref, enter_ref, hid_ref, local_ref, gate_ref, read_ref, dec_ref, state_ref, cols_ref,
    out_proj_ref, head_ref, bias_ref, labels_ref, distance_ref, features_ref, grad_ref, loss_ref, gated_ref, square_ref,
    after_ref, feature_scr, logit_scr, sum_scr,
):
    count = hid_ref.shape[0]
    classes = distance_ref.shape[0]
    model = out_proj_ref.shape[1]
    inner = local_ref.shape[1]
    alls = (hid_ref, local_ref, gate_ref, read_ref, dec_ref, state_ref)
    enter = unpack(enter_ref[...], heads)
    out_gain = cols_ref[layer, :inner, 9:10]
    bias = columns(bias_ref[...])[:classes, 0:1]
    sum_scr[...] = jnp.zeros_like(sum_scr)

    def step_group(g):
        def take(u, result):
            after_ref[u] = result
            feature_scr[pl.ds(u, model, stride=group), :] = result.astype(f32)

        refs = tuple(r.at[pl.ds(g * group, group)] for r in alls)
        finish_group(heads, enter, refs, out_gain, out_proj_ref[layer], gated_ref, square_ref, take)
        for q in range(0, group, wide):
            logits = project(head_ref[...], side_by_side(after_ref, q, wide)) + bias
            for u in range(wide):
                logit_scr[pl.ds(q + u, classes, stride=group), :] = logits[:, span(u)]
        at = g * group if isinstance(g, int) else pl.multiple_of(g * group, group)
        features_ref[:, pl.ds(at, group), :] = feature_scr[...].reshape(model, group, SCAN_BLOCK).astype(bf16)
        for z in range(0, group, 8):
            here = pl.ds(at + z, 8)
            logits = jnp.stack([logit_scr[c * group + z : c * group + z + 8, :] for c in range(classes)], axis=0)
            peak = jnp.max(logits, axis=0)
            shifted = jnp.exp(logits - peak[None])
            partition = jnp.sum(shifted, axis=0)
            probability = shifted / partition[None]
            weighted = probability * (distance_ref[:, here, :].astype(f32) * (1.0 / dist_unit))
            expect = jnp.sum(weighted, axis=0)
            hot = labels_ref[here, :][None] == lax.broadcasted_iota(jnp.int32, logits.shape, 0)
            chosen = jnp.sum(jnp.where(hot, logits, 0.0), axis=0)
            grad_ref[:, here, :] = probability - jnp.where(hot, 1.0, 0.0) + weighted - probability * expect[None]
            sum_scr[...] += peak + jnp.log(partition) - chosen + expect

    repeat(count // group, step_group)
    weight = 1.0 + 3.0 * me_ref[0].astype(f32) / (size - 1.0)
    loss_ref[...] = jnp.broadcast_to(jnp.sum(sum_scr[...], axis=0, keepdims=True) * weight, loss_ref.shape)


def params(size=vmem_bytes):
    return pltpu.CompilerParams(vmem_limit_bytes=size)


def cost(us):
    return pl.CostEstimate(flops=int(us * 1e9), bytes_accessed=int(us * 3.5e6), transcendentals=0)


vmem = pl.BlockSpec(memory_space=pltpu.VMEM)


def join_kernel(heads, reach, radix, me_ref, before_ref, *refs):
    members, outs = refs[:radix], refs[radix:]
    digit = (me_ref[0] & (radix * reach - 1)) // reach
    rows = before_ref.shape[0] - 8
    third = rows // heads

    def combine(earlier, latter):
        log = latter[rows:]
        grow = jnp.exp(log)
        blocks = [
            grow[h : h + 1] * earlier[h * third : (h + 1) * third] + latter[h * third : (h + 1) * third]
            for h in range(heads)
        ]
        return jnp.concatenate(blocks + [earlier[rows:] + log], axis=0)

    values = [ref[...] for ref in members]
    before = before_ref[...]
    ahead, total = None, None
    for place in range(radix if len(outs) > 1 else radix - 1):
        value = values[0]
        for k in range(1, radix):
            value = jnp.where(digit ^ k == place, values[k], value)
        total = value if total is None else combine(total, value)
        if place < radix - 1:
            ahead = jnp.where(place < digit, total, jnp.zeros_like(total) if ahead is None else ahead)
    outs[0][...] = combine(ahead, before)
    if len(outs) > 1:
        outs[1][...] = total


def prefix_state(me, total, held, pieces, heads):
    size = lax.axis_size(axes)
    rounds = [(1, 2)]
    while rounds[-1][0] * rounds[-1][1] < size:
        reach = rounds[-1][0] * rounds[-1][1]
        rounds.append((reach, 4 if 4 * reach <= size else 2))
    before = jnp.zeros_like(total)
    done = None
    for i, (reach, radix) in enumerate(rounds):
        piece = i - (len(rounds) - len(pieces))
        if piece >= 0:
            total, held = lax.optimization_barrier((total, held))
            done = pieces[piece](held, done)
        others = [
            lax.ppermute(total, axes, [(k, k ^ (step * reach | 1)) for k in range(size)]) for step in range(1, radix)
        ]
        if piece >= 0:
            others, done = lax.optimization_barrier((others, done))
        outs = 2 if reach * radix < size else 1
        before, *total = pl.pallas_call(
            functools.partial(join_kernel, heads, reach, radix),
            in_specs=[pl.BlockSpec(memory_space=pltpu.SMEM)] + [vmem] * (1 + radix),
            out_specs=[vmem] * outs,
            out_shape=[jax.ShapeDtypeStruct(before.shape, f32)] * outs,
            compiler_params=params(2 * 1024 * 1024),
            name="join",
        )(me, before, total, *others)
        total = total[0] if total else None
    return before, done


def tile(count, rows, kind):
    return jax.ShapeDtypeStruct((count, rows, SCAN_BLOCK), kind)


def call_tail(me, size, volume):
    model = volume.shape[0]
    per = LANES // volume.shape[1]
    return pl.pallas_call(
        functools.partial(tail_kernel, size),
        in_specs=[pl.BlockSpec(memory_space=pltpu.SMEM), vmem],
        out_specs=vmem,
        out_shape=jax.ShapeDtypeStruct((model, SCAN_BLOCK), bf16),
        scratch_shapes=[pltpu.VMEM((-(-model // (8 * per)) * 8 * per, LANES), f32)],
        compiler_params=params(4 * 1024 * 1024),
        cost_estimate=cost(2),
        name="tail",
    )(me, volume)


def call_sequence(volume):
    model, cells_x, cells_y = volume.shape
    count = cells_x * cells_y // SCAN_BLOCK
    return pl.pallas_call(
        sequence_kernel,
        in_specs=[vmem],
        out_specs=vmem,
        out_shape=tile(count, model, bf16),
        scratch_shapes=[
            pltpu.VMEM((model * cells_x // LANES, cells_y, LANES), f32),
            pltpu.VMEM((count * model, LANES), f32),
        ],
        compiler_params=params(),
        cost_estimate=cost(8),
        name="sequence",
    )(volume)


def call_weights(norm_gain, in_proj, dt_proj, dt_bias, decay_rate, conv_weight, conv_bias, skip_gain, out_gain):
    layers, projected, model = in_proj.shape
    return pl.pallas_call(
        weights_kernel,
        in_specs=[vmem] * 9,
        out_specs=[vmem] * 3,
        out_shape=[
            jax.ShapeDtypeStruct((layers, projected + 16, model), bf16),
            jax.ShapeDtypeStruct((layers, -(-conv_bias.shape[1] // LANES) * LANES, 16), f32),
            jax.ShapeDtypeStruct((2 * SCAN_BLOCK, tap_count * SCAN_BLOCK), bf16),
        ],
        compiler_params=params(4 * 1024 * 1024),
        name="weights",
    )(
        jnp.swapaxes(in_proj, 1, 2), jnp.swapaxes(dt_proj, 0, 1), jnp.swapaxes(conv_weight, 1, 2), conv_bias, norm_gain,
        dt_bias, decay_rate, skip_gain, out_gain,
    )


def call_states(layer, hidden, tail, weights):
    inner, heads, state = (weights[k] for k in ("inner", "heads", "state"))
    count = hidden.shape[0]
    group = min(32, count)
    return pl.pallas_call(
        functools.partial(state_kernel, layer, heads, group),
        in_specs=[vmem] * 5,
        out_specs=[vmem] * 5,
        out_shape=[
            tile(count, inner, bf16),
            tile(count, state, bf16),
            tile(count, 16, f32),
            tile(count, state + 8, f32),
            jax.ShapeDtypeStruct((state * inner // LANES + 8, LANES), f32),
        ],
        scratch_shapes=[
            pltpu.VMEM((inner + state, (group + 1) * SCAN_BLOCK), bf16),
            pltpu.VMEM((state + 8, LANES), f32),
        ],
        compiler_params=params(),
        name="states",
    )(hidden, tail, weights["rows"], weights["cols"], weights["shift"])


def call_local(layer, first, count, held, done, weights):
    hidden, tail, inner_values, write, dec = held
    total = hidden.shape[0]
    inner, heads, state = weights["inner"], weights["heads"], weights["state"]
    group = min(16, count)
    taken = [] if done is None else list(done)
    return pl.pallas_call(
        functools.partial(local_kernel, layer, heads, first, count, group),
        in_specs=[vmem] * (8 + len(taken)),
        out_specs=[vmem] * 3,
        out_shape=[tile(total, inner, f32), tile(total, inner, f32), tile(total, state, bf16)],
        input_output_aliases={8 + i: i for i in range(len(taken))},
        scratch_shapes=[
            pltpu.VMEM((state, (group + 1) * SCAN_BLOCK), bf16),
            pltpu.VMEM((group, SCAN_BLOCK, SCAN_BLOCK), f32),
            pltpu.VMEM((group, heads, SCAN_BLOCK, SCAN_BLOCK), bf16),
        ],
        compiler_params=params(),
        name="local",
    )(hidden, tail, weights["rows"], weights["cols"], weights["shift"], inner_values, write, dec, *taken)


def layer_start(layer, me, hidden, tail, weights):
    inner_values, write, dec, states, total = call_states(layer, hidden, tail, weights)
    cut = hidden.shape[0] // 2
    pieces = [
        lambda held, done, first=first: call_local(layer, first, cut, held, done, weights)
        for first in range(0, hidden.shape[0], cut)
    ]
    enter, done = prefix_state(me, total, (hidden, tail, inner_values, write, dec), pieces, weights["heads"])
    return (enter, hidden, *done, dec, states, weights["cols"], weights["out_proj"])


def finish_scratch(group, weights):
    return [pltpu.VMEM((group, weights["inner"], SCAN_BLOCK), f32), pltpu.VMEM((group, 8, SCAN_BLOCK), f32)]


def call_finish(cells, parts, weights):
    count, model, _ = parts[1].shape
    model = weights["model"]
    cells_x, cells_y = cells
    rows = model + 8
    per = LANES // cells_x
    return pl.pallas_call(
        functools.partial(finish_kernel, 0, weights["heads"], cells_x, min(32, count)),
        in_specs=[vmem] * len(parts),
        out_specs=vmem,
        out_shape=jax.ShapeDtypeStruct((cells_x, rows, cells_y), bf16),
        scratch_shapes=[
            pltpu.VMEM((count * model, LANES), f32),
            pltpu.VMEM((model // per, cells_y, LANES), f32),
            pltpu.VMEM(((cells_x + 1) * rows, LANES), f32),
        ]
        + finish_scratch(min(32, count), weights),
        compiler_params=params(),
        name="finish",
    )(*parts)


def call_heads(me, size, parts, weights, head_weight, head_bias, labels, distance):
    classes, model = head_weight.shape
    count = parts[1].shape[0]
    group = min(32, count)
    return pl.pallas_call(
        functools.partial(head_kernel, 1, weights["heads"], group, size),
        in_specs=[pl.BlockSpec(memory_space=pltpu.SMEM)] + [vmem] * (len(parts) + 4),
        out_specs=[vmem] * 3,
        out_shape=[
            jax.ShapeDtypeStruct((model, count, SCAN_BLOCK), bf16),
            jax.ShapeDtypeStruct((classes, count, SCAN_BLOCK), f32),
            jax.ShapeDtypeStruct((size, SCAN_BLOCK), f32),
        ],
        scratch_shapes=finish_scratch(group, weights)
        + [
            pltpu.VMEM((group, model, SCAN_BLOCK), bf16),
            pltpu.VMEM((model * group, SCAN_BLOCK), f32),
            pltpu.VMEM((-(-classes // 8) * 8 * group, SCAN_BLOCK), f32),
            pltpu.VMEM((8, SCAN_BLOCK), f32),
        ],
        compiler_params=params(),
        name="heads",
    )(me, *parts, head_weight, head_bias, labels, distance)


def per_device(
    volume, norm_gain, in_proj, dt_proj, dt_bias, decay_rate, conv_weight, conv_bias, skip_gain, out_gain,
    out_proj, head_weight, head_bias, labels, distance,
):
    size = lax.axis_size(axes)
    model, _, cells_y, cells_x = volume.shape
    classes = head_weight.shape[0]
    inner = out_proj.shape[2]
    heads = decay_rate.shape[1]
    weights = dict(heads=heads, inner=inner, state=(in_proj.shape[1] - 2 * inner) // 2, model=model)
    me = lax.axis_index(axes).astype(jnp.int32).reshape(1)
    plane = jnp.swapaxes(volume[:, 0], 1, 2)
    tail = call_tail(me, size, plane)
    hidden = call_sequence(plane)
    weights["rows"], weights["cols"], weights["shift"] = call_weights(
        norm_gain, in_proj, dt_proj, dt_bias, decay_rate, conv_weight, conv_bias, skip_gain, out_gain
    )
    weights["out_proj"] = out_proj
    tail = lax.ppermute(tail, axes, [(i, (i + 1) % size) for i in range(size)])
    parts = layer_start(0, me, hidden, tail, weights)
    planes = call_finish((cells_x, cells_y), parts, weights)
    hidden = lax.all_to_all(planes, axes, split_axis=0, concat_axis=0, tiled=True)
    count = hidden.shape[0]
    parts = layer_start(1, me, hidden, hidden, weights)
    labels, distance = labels.reshape(count, SCAN_BLOCK), distance.reshape(classes, count, SCAN_BLOCK)
    features, grad, loss = call_heads(
        me, size, parts, weights, head_weight, head_bias[None, :], labels, distance
    )
    shared = lax.all_to_all(loss, axes, 0, 0, tiled=True)
    total_loss = jnp.sum(shared) / (2.5 * count * SCAN_BLOCK * size)
    return (
        features.reshape(model, 1, count, SCAN_BLOCK),
        grad.reshape(classes, 1, count, SCAN_BLOCK),
        total_loss,
    )


def solution(mesh):
    plane = P(None, axes, None, None)
    return jax.shard_map(
        per_device,
        mesh=mesh,
        in_specs=(plane,) + (P(),) * 12 + (P(axes, None, None), plane),
        out_specs=(plane, plane, P()),
        check_vma=False,
    )
```
